32 devices in a mesh: grp: 2 (over y), mesh: 16 (over z, x, core).
Axes of the slice: x: 2, y: 2, z: 4, core: 2. Of those that a mesh axis runs over, the one named last changes fastest.
Arguments:
- basis: bfloat16 [65536, 512], P(('grp', 'mesh')), parts along dimension 0, may hold values from -6 to 6
- blocks: bfloat16 [2, 512, 3, 128, 128], P(None, ('grp', 'mesh')), parts along dimension 1, may hold values from -0.0017089844 to 0.0017089844
- columns: int32 [2, 512, 2], P(None, ('grp', 'mesh')), parts along dimension 1, may hold values from 0 to 31
- sends: int32 [32, 16], P(('grp', 'mesh')), parts along dimension 0, may hold values from 0 to 15
Outputs:
- projected: float32 [1024, 1024], P(('grp', 'mesh')), parts along dimension 0
The draws below stay inside these ranges and needn't reach their ends.
There are 2 independent parts, one for each index of `grp`. The reference program is written for one: setup_inputs(seed, part) draws one part's arguments, and reference() takes and returns one part's arrays. A program takes and returns all parts, laid end to end along the dimension named above; each array names one. Nothing has to cross between parts.
All inputs are finite; a program needn't handle non-finite values.
Results may differ from the reference program's by a relative error of at most 0.0029.
Values may be sent and summed in bfloat16 or wider, within the bound.
No kernel may reach another device: no remote copies, remote signals or barrier semaphores. Data moves between devices by JAX's collectives and lax.ppermute only.
A program may use at most 64 MiB of HBM per device.

```python
import jax
import jax.numpy as jnp
from jax import lax

BLOCK = 128
BASIS = 512
PARAMS = 2
ROWBLK = 16
SLOTS = 3
HALO = 8
NROWB = 256
NROWS = 32768
N_MESH = 16


def plant(values, own_key, smallest, largest):
    place = [jax.random.randint(jax.random.fold_in(own_key, axis), (), 0, length) for axis, length in enumerate(values.shape)]
    main_axis = values.shape.index(max(values.shape))
    beside = place[:main_axis] + [(place[main_axis] + 1) % values.shape[main_axis]] + place[main_axis + 1:]
    return values.at[tuple(place)].set(smallest).at[tuple(beside)].set(largest)


def with_spikes(drawn, key, source, target, blocks, factor):
    owner, partner = [(jnp.arange(drawn.shape[position]) // (drawn.shape[position] // blocks)).reshape([-1 if axis == position else 1 for axis in range(drawn.ndim)]) for position in (source, target)]
    chosen = jax.random.permutation(key, blocks)[partner]
    strong = (owner == chosen) | (owner == (partner + blocks // 2) % blocks)
    return jnp.where(strong, factor * drawn, drawn)


def block_scale(key, shape, shards, least, high):
    factor_of, own = 1.0, jax.random.fold_in(key, 6)
    for dim, shards_of in shards:
        heights = jnp.exp(jax.random.uniform(jax.random.fold_in(own, dim), (shards_of,), jnp.float32, least / len(shards), high / len(shards)))
        factor_of = factor_of * jnp.repeat(heights, shape[dim] // shards_of).reshape([-1 if axis == dim else 1 for axis in range(len(shape))])
    return factor_of


def bell_draw(rng, shape, deviation, reach, pieces=(), kind=jnp.bfloat16):
    drawn = deviation * jax.random.normal(rng, shape, jnp.float32)
    if pieces:
        drawn = drawn * block_scale(rng, shape, pieces, -0.22, 0.18)
    return jnp.clip(drawn, -reach, reach).astype(kind)


def heavy_noise(own_key, extent, scale, bound, cuts, heavy, held_as=jnp.bfloat16):
    drawn = scale * jax.random.normal(own_key, extent, jnp.float32)
    if cuts:
        drawn = drawn * block_scale(own_key, extent, cuts, -0.22, 0.18)
    return jnp.clip(with_spikes(drawn, jax.random.fold_in(own_key, 3), *heavy), -bound, bound).astype(held_as)


def setup_inputs(seed: int = 0, part: int = 0) -> dict:
    seeds = jax.random.split(jax.random.key(seed), 5)
    own_keys = jax.random.split(jax.random.fold_in(seeds[4], part), 5)
    return {
        "basis": heavy_noise(own_keys[0], (NROWS, BASIS), 1.0, 6.0, ((0, 16),), (0, 1, 16, 2.0)),
        "blocks": bell_draw(own_keys[1], (PARAMS, NROWB, SLOTS, BLOCK, BLOCK), (SLOTS * BLOCK * NROWS) ** -0.5, 0.0017089844, ((1, 16),)),
        "columns": plant(jax.random.randint(own_keys[2], (PARAMS, NROWB, SLOTS - 1), 0, ROWBLK + 2 * HALO), jax.random.fold_in(own_keys[2], 1), 0, (ROWBLK + 2 * HALO) - 1).astype(jnp.int32),
        "sends": plant(jax.random.randint(own_keys[3], (N_MESH, 2 * HALO), 0, ROWBLK), jax.random.fold_in(own_keys[3], 1), 0, ROWBLK - 1).astype(jnp.int32),
    }


def take_rows(source, positions):
    return jnp.take(source, positions, axis=0)


def reference(basis, blocks, columns, sends):
    own_blocks = basis.reshape(N_MESH, ROWBLK, BLOCK, BASIS)
    picker = jax.vmap(take_rows)
    upward = picker(own_blocks, sends[:, HALO:].astype(jnp.int32))
    downward = picker(own_blocks, sends[:, :HALO].astype(jnp.int32))
    empty_rim = jnp.zeros((1, HALO, BLOCK, BASIS), basis.dtype)
    from_below = jnp.concatenate([empty_rim, upward[:-1]], axis=0)
    from_above = jnp.concatenate([downward[1:], empty_rim], axis=0)
    extended = jnp.concatenate([own_blocks, from_below, from_above], axis=1)
    diag_index = jnp.broadcast_to(jnp.arange(ROWBLK, dtype=jnp.int32)[None, :, None], (N_MESH, ROWBLK, 1))

    def project_param(param):
        slot_index = jnp.concatenate([diag_index, columns[param].reshape(N_MESH, ROWBLK, SLOTS - 1).astype(jnp.int32)], axis=2)
        param_blocks = blocks[param].reshape(N_MESH, ROWBLK, SLOTS, BLOCK, BLOCK)
        accumulated = jnp.zeros((N_MESH, ROWBLK, BLOCK, BASIS), jnp.float32)
        for slot in range(SLOTS):
            gathered = picker(extended, slot_index[:, :, slot])
            accumulated = accumulated + jnp.einsum("dbik,dbkj->dbij", param_blocks[:, :, slot].astype(jnp.float32), gathered.astype(jnp.float32))
        image_rows = accumulated.astype(jnp.bfloat16).reshape(NROWS, BASIS)
        return lax.dot_general(basis, image_rows, (((0,), (0,)), ((), ())), preferred_element_type=jnp.float32)

    return jnp.concatenate([project_param(param) for param in range(PARAMS)], axis=1)
```

```python
import jax
import jax.numpy as jnp
from jax import lax
from jax.sharding import PartitionSpec as P

AXIS = "mesh"


def pairs(count, first):
    both = []
    for low in range(first, count - 1, 2):
        both += [(low, low + 1), (low + 1, low)]
    return both


def shards(basis, blocks, columns, sends):
    count_params, count_blocks, count_slots, block_size, _ = blocks.shape
    width = basis.shape[1]
    halo = sends.shape[1] // 2
    count = lax.axis_size(AXIS)
    odd = lax.rem(lax.axis_index(AXIS), 2)
    own = basis.reshape(count_blocks, block_size, width)

    lists = sends.reshape(2, halo)
    far = jnp.take(own, lists[odd], axis=0, mode="clip")
    near = jnp.take(own, lists[1 - odd], axis=0, mode="clip")
    from_far = lax.ppermute(far, AXIS, pairs(count, 1))
    from_near = lax.ppermute(near, AXIS, pairs(count, 0))
    lower = jnp.where(odd == 0, from_far, from_near)
    upper = jnp.where(odd == 0, from_near, from_far)
    extended = jnp.concatenate([own, lower, upper], axis=0)

    diagonal = jnp.arange(count_blocks, dtype=jnp.int32)[:, None]
    images = []
    for param in range(count_params):
        index = jnp.concatenate([diagonal, columns[param]], axis=1)
        gathered = jnp.take(extended, index, axis=0, mode="clip")
        image = jnp.einsum(
            "bsik,bskj->bij", blocks[param], gathered, preferred_element_type=jnp.float32
        )
        images.append(image.astype(jnp.bfloat16).reshape(count_blocks * block_size, width))
    stacked = jnp.concatenate(images, axis=1)
    partial = lax.dot_general(
        basis, stacked, (((0,), (0,)), ((), ())), preferred_element_type=jnp.float32
    )
    chips = count // 2
    rows = partial.shape[0] // count
    partial = partial.reshape(chips, 2, rows, partial.shape[1])
    keep = lax.dynamic_index_in_dim(partial, odd, axis=1, keepdims=False)
    give = lax.dynamic_index_in_dim(partial, 1 - odd, axis=1, keepdims=False)
    taken = lax.ppermute(give.astype(jnp.bfloat16), AXIS, pairs(count, 0))
    chip_sum = (keep + taken.astype(jnp.float32)).astype(jnp.bfloat16)
    groups = [list(range(core, count, 2)) for core in range(2)]
    parts = lax.all_to_all(
        chip_sum, AXIS, split_axis=0, concat_axis=0, axis_index_groups=groups, tiled=True
    )
    return jnp.sum(parts.astype(jnp.float32), axis=0)


def solution(mesh):
    placed = (
        P(("grp", "mesh"), None),
        P(None, ("grp", "mesh"), None, None, None),
        P(None, ("grp", "mesh"), None),
        P(("grp", "mesh"), None),
    )
    return jax.shard_map(
        shards, mesh=mesh, in_specs=placed, out_specs=P(("grp", "mesh"), None), check_vma=False
    )
```

```python
import jax
import jax.numpy as jnp
from jax import lax
from jax.experimental import pallas as pl
from jax.experimental.pallas import tpu as pltpu
from jax.sharding import PartitionSpec as P

AXIS = "mesh"
VMEM_BYTES = 40 * 1024 * 1024


def pairs(count, first):
    both = []
    for low in range(first, count - 1, 2):
        both += [(low, low + 1), (low + 1, low)]
    return both


def pick_blocks(own, sends, far):
    halo = sends.shape[1] // 2

    def kernel(sends_ref, own_ref, out_ref, sems):
        odd = lax.rem(lax.axis_index(AXIS), 2)
        first = (odd if far else 1 - odd) * halo
        copies = []
        for place in range(halo):
            block = sends_ref[0, first + place]
            copies.append(
                pltpu.make_async_copy(own_ref.at[block], out_ref.at[place], sems.at[place])
            )
        for copy in copies:
            copy.start()
        for copy in copies:
            copy.wait()

    size = halo * own.shape[1] * own.shape[2] * own.dtype.itemsize
    return pl.pallas_call(
        kernel,
        out_shape=jax.ShapeDtypeStruct((halo,) + own.shape[1:], own.dtype),
        in_specs=[pl.BlockSpec(memory_space=pltpu.SMEM), pl.BlockSpec(memory_space=pl.ANY)],
        out_specs=pl.BlockSpec(memory_space=pl.ANY),
        scratch_shapes=[pltpu.SemaphoreType.DMA((halo,))],
        cost_estimate=pl.CostEstimate(flops=0, bytes_accessed=2 * size, transcendentals=0),
    )(sends, own)


def project(turned, own, far, near, blocks, columns):
    params, count, slots, size, _ = blocks.shape
    width = own.shape[2]
    halo = far.shape[0]
    half = width // 2

    def kernel(
        columns_ref, turned_hbm, own_hbm, far_hbm, near_hbm, blocks_hbm,
        keep_ref, give_ref, turned_ref, list_ref, blocks_ref, image_ref, sems,
    ):
        odd = lax.rem(lax.axis_index(AXIS), 2)
        far_at = count + odd * halo
        near_at = count + (1 - odd) * halo
        loads = [
            pltpu.make_async_copy(own_hbm, list_ref.at[pl.ds(0, count)], sems.at[0]),
            pltpu.make_async_copy(far_hbm, list_ref.at[pl.ds(far_at, halo)], sems.at[1]),
            pltpu.make_async_copy(near_hbm, list_ref.at[pl.ds(near_at, halo)], sems.at[2]),
            pltpu.make_async_copy(blocks_hbm, blocks_ref, sems.at[3]),
            pltpu.make_async_copy(turned_hbm, turned_ref, sems.at[4]),
        ]
        for load in loads:
            load.start()
        for load in loads[:-1]:
            load.wait()

        @pl.loop(0, count)
        def _(row):
            for param in range(params):
                left = [blocks_ref[param, row, slot] for slot in range(slots)]
                right = [list_ref[row]]
                for slot in range(1, slots):
                    right.append(list_ref[columns_ref[param, row, slot - 1]])
                image = jnp.dot(
                    jnp.concatenate(left, axis=1),
                    jnp.concatenate(right, axis=0),
                    preferred_element_type=jnp.float32,
                )
                image_ref[pl.ds(pl.multiple_of(row * size, size), size), pl.ds(param * width, width)] = (
                    image.astype(image_ref.dtype)
                )

        loads[-1].wait()
        mine = pl.ds(pl.multiple_of(odd * half, half), half)
        other = pl.ds(pl.multiple_of((1 - odd) * half, half), half)
        step = 256 if width % 256 == 0 else width
        for at in range(0, params * width, step):
            cols = pl.ds(at, step)
            give_ref[:, cols] = jnp.dot(
                turned_ref[other], image_ref[:, cols], preferred_element_type=jnp.float32
            ).astype(give_ref.dtype)
            keep_ref[:, cols] = jnp.dot(
                turned_ref[mine], image_ref[:, cols], preferred_element_type=jnp.float32
            )

    any_space = pl.BlockSpec(memory_space=pl.ANY)
    flops = 2 * params * count * size * width * (slots * size + width)
    moved = 2 * (2 * own.size + 2 * far.size + blocks.size) + 6 * half * params * width
    return pl.pallas_call(
        kernel,
        out_shape=(
            jax.ShapeDtypeStruct((half, params * width), jnp.float32),
            jax.ShapeDtypeStruct((half, params * width), jnp.bfloat16),
        ),
        in_specs=[pl.BlockSpec(memory_space=pltpu.SMEM)] + [any_space] * 5,
        out_specs=(pl.BlockSpec(memory_space=pltpu.VMEM),) * 2,
        scratch_shapes=[
            pltpu.VMEM(turned.shape, turned.dtype),
            pltpu.VMEM((count + 2 * halo, size, width), own.dtype),
            pltpu.VMEM(blocks.shape, blocks.dtype),
            pltpu.VMEM((count * size, params * width), jnp.bfloat16),
            pltpu.SemaphoreType.DMA((5,)),
        ],
        compiler_params=pltpu.CompilerParams(vmem_limit_bytes=VMEM_BYTES),
        cost_estimate=pl.CostEstimate(flops=flops, bytes_accessed=moved, transcendentals=0),
    )(columns, turned, own, far, near, blocks)


def shards(basis, blocks, columns, sends):
    params, count, _, size, _ = blocks.shape
    width = basis.shape[1]
    devices = lax.axis_size(AXIS)
    chips = devices // 2
    rows = width // devices
    own = basis.reshape(count, size, width)

    far = pick_blocks(own, sends, True)
    from_far = lax.ppermute(far, AXIS, pairs(devices, 1))
    near = pick_blocks(own, sends, False)
    from_near = lax.ppermute(near, AXIS, pairs(devices, 0))
    turned = basis.T.reshape(chips, 2, rows, count * size)
    turned = turned.transpose(1, 0, 2, 3).reshape(width, count * size)

    keep, give = project(turned, own, from_far, from_near, blocks, columns)
    taken = lax.ppermute(give, AXIS, pairs(devices, 0))
    chip_sum = (keep + taken.astype(jnp.float32)).astype(jnp.bfloat16)
    groups = [list(range(core, devices, 2)) for core in range(2)]
    parts = lax.all_to_all(
        chip_sum.reshape(chips, rows, params * width), AXIS,
        split_axis=0, concat_axis=0, axis_index_groups=groups, tiled=True,
    )
    return jnp.sum(parts.astype(jnp.float32), axis=0)


def solution(mesh):
    placed = (
        P(("grp", "mesh"), None),
        P(None, ("grp", "mesh"), None, None, None),
        P(None, ("grp", "mesh"), None),
        P(("grp", "mesh"), None),
    )
    return jax.shard_map(
        shards, mesh=mesh, in_specs=placed, out_specs=P(("grp", "mesh"), None), check_vma=False
    )
```

```python
import jax
import jax.numpy as jnp
from jax import lax
from jax.experimental import pallas as pl
from jax.experimental.pallas import tpu as pltpu
from jax.sharding import PartitionSpec as P

AXIS = "mesh"
VMEM_BYTES = 28 * 1024 * 1024


def pairs(count, first):
    both = []
    for low in range(first, count - 1, 2):
        both += [(low, low + 1), (low + 1, low)]
    return both


def pick_blocks(own, sends, far):
    halo = sends.shape[1] // 2

    def kernel(sends_ref, own_ref, out_ref, sems):
        odd = lax.rem(lax.axis_index(AXIS), 2)
        first = (odd if far else 1 - odd) * halo
        copies = []
        for place in range(halo):
            block = sends_ref[0, first + place]
            copies.append(
                pltpu.make_async_copy(own_ref.at[block], out_ref.at[place], sems.at[place])
            )
        for copy in copies:
            copy.start()
        for copy in copies:
            copy.wait()

    size = halo * own.shape[1] * own.shape[2] * own.dtype.itemsize
    return pl.pallas_call(
        kernel,
        out_shape=jax.ShapeDtypeStruct((halo,) + own.shape[1:], own.dtype),
        in_specs=[pl.BlockSpec(memory_space=pltpu.SMEM), pl.BlockSpec(memory_space=pl.ANY)],
        out_specs=pl.BlockSpec(memory_space=pltpu.VMEM),
        scratch_shapes=[pltpu.SemaphoreType.DMA((halo,))],
        compiler_params=pltpu.CompilerParams(vmem_limit_bytes=VMEM_BYTES),
        cost_estimate=pl.CostEstimate(flops=0, bytes_accessed=2 * size, transcendentals=0),
    )(sends, own)


def own_terms(own, blocks, columns):
    params, count, slots, size, _ = blocks.shape
    width = own.shape[2]

    def kernel(columns_ref, own_ref, blocks_ref, out_ref):
        @pl.loop(0, count, unroll=2)
        def _(row):
            at = pl.ds(pl.multiple_of(row * size, size), size)
            for param in range(params):
                left, right = [blocks_ref[param, row, 0]], [own_ref[row]]
                for slot in range(1, slots):
                    block = blocks_ref[param, row, slot]
                    column = columns_ref[param, row, slot - 1]
                    left.append(jnp.where(column < count, block, jnp.zeros_like(block)))
                    right.append(own_ref[jnp.minimum(column, count - 1)])
                out_ref[param, at] = jnp.dot(
                    jnp.concatenate(left, axis=1),
                    jnp.concatenate(right, axis=0),
                    preferred_element_type=jnp.float32,
                )

    vmem = pl.BlockSpec(memory_space=pltpu.VMEM)
    terms = jax.ShapeDtypeStruct((params, count * size, width), jnp.float32)
    return pl.pallas_call(
        kernel,
        out_shape=terms,
        in_specs=[pl.BlockSpec(memory_space=pltpu.SMEM), vmem, vmem],
        out_specs=vmem,
        compiler_params=pltpu.CompilerParams(vmem_limit_bytes=VMEM_BYTES),
        cost_estimate=pl.CostEstimate(
            flops=2 * slots * size * terms.size,
            bytes_accessed=4 * terms.size + 2 * (own.size + blocks.size),
            transcendentals=0,
        ),
    )(columns, own, blocks)


def project(turned, terms, far, near, blocks, columns):
    params, count, slots, size, _ = blocks.shape
    halo, _, width = far.shape
    half = turned.shape[0] // 2

    def kernel(
        columns_ref, turned_ref, terms_ref, far_ref, near_ref, blocks_ref,
        keep_ref, give_ref, list_ref, image_ref,
    ):
        odd = lax.rem(lax.axis_index(AXIS), 2)
        list_ref[pl.ds(odd * halo, halo)] = far_ref[...]
        list_ref[pl.ds((1 - odd) * halo, halo)] = near_ref[...]

        @pl.loop(0, count, unroll=2)
        def _(row):
            at = pl.ds(pl.multiple_of(row * size, size), size)
            for param in range(params):
                left, right = [], []
                for slot in range(1, slots):
                    block = blocks_ref[param, row, slot]
                    column = columns_ref[param, row, slot - 1]
                    left.append(jnp.where(column < count, jnp.zeros_like(block), block))
                    right.append(list_ref[jnp.maximum(column - count, 0)])
                image = terms_ref[param, at] + jnp.dot(
                    jnp.concatenate(left, axis=1),
                    jnp.concatenate(right, axis=0),
                    preferred_element_type=jnp.float32,
                )
                image_ref[at, pl.ds(param * width, width)] = image.astype(image_ref.dtype)

        mine = pl.ds(pl.multiple_of(odd * half, half), half)
        other = pl.ds(pl.multiple_of((1 - odd) * half, half), half)
        step = 256 if width % 256 == 0 else width
        for at in range(0, params * width, step):
            cols = pl.ds(at, step)
            give_ref[:, cols] = jnp.dot(
                turned_ref[other], image_ref[:, cols], preferred_element_type=jnp.float32
            ).astype(give_ref.dtype)
            keep_ref[:, cols] = jnp.dot(
                turned_ref[mine], image_ref[:, cols], preferred_element_type=jnp.float32
            )

    vmem = pl.BlockSpec(memory_space=pltpu.VMEM)
    flops = 2 * params * count * size * width * ((slots - 1) * size + 2 * half)
    moved = 4 * terms.size + 2 * (turned.size + 2 * far.size + blocks.size)
    return pl.pallas_call(
        kernel,
        out_shape=(
            jax.ShapeDtypeStruct((half, params * width), jnp.float32),
            jax.ShapeDtypeStruct((half, params * width), jnp.bfloat16),
        ),
        in_specs=[pl.BlockSpec(memory_space=pltpu.SMEM)] + [vmem] * 5,
        out_specs=(vmem,) * 2,
        scratch_shapes=[
            pltpu.VMEM((2 * halo, size, width), far.dtype),
            pltpu.VMEM((count * size, params * width), jnp.bfloat16),
        ],
        compiler_params=pltpu.CompilerParams(vmem_limit_bytes=VMEM_BYTES),
        cost_estimate=pl.CostEstimate(flops=flops, bytes_accessed=moved, transcendentals=0),
    )(columns, turned, terms, far, near, blocks)


def shards(basis, blocks, columns, sends):
    params, count, _, size, _ = blocks.shape
    width = basis.shape[1]
    devices = lax.axis_size(AXIS)
    chips = devices // 2
    rows = width // devices
    own = basis.reshape(count, size, width)

    far = pick_blocks(own, sends, True)
    from_far = lax.ppermute(far, AXIS, pairs(devices, 1))
    near = pick_blocks(own, sends, False)
    from_near = lax.ppermute(near, AXIS, pairs(devices, 0))
    turned = basis.T.reshape(chips, 2, rows, count * size)
    turned = turned.transpose(1, 0, 2, 3).reshape(width, count * size)

    terms = own_terms(own, blocks, columns)

    keep, give = project(turned, terms, from_far, from_near, blocks, columns)
    taken = lax.ppermute(give, AXIS, pairs(devices, 0))
    chip_sum = (keep + taken.astype(jnp.float32)).astype(jnp.bfloat16)
    groups = [list(range(core, devices, 2)) for core in range(2)]
    parts = lax.all_to_all(
        chip_sum.reshape(chips, rows, params * width), AXIS,
        split_axis=0, concat_axis=0, axis_index_groups=groups, tiled=True,
    )
    return jnp.sum(parts.astype(jnp.float32), axis=0)


def solution(mesh):
    placed = (
        P(("grp", "mesh"), None),
        P(None, ("grp", "mesh"), None, None, None),
        P(None, ("grp", "mesh"), None),
        P(("grp", "mesh"), None),
    )
    return jax.shard_map(
        shards, mesh=mesh, in_specs=placed, out_specs=P(("grp", "mesh"), None), check_vma=False
    )
```

```python
import jax
import jax.numpy as jnp
from jax import lax
from jax.experimental import pallas as pl
from jax.experimental.pallas import tpu as pltpu
from jax.sharding import PartitionSpec as P

AXIS = "mesh"
VMEM_BYTES = 28 * 1024 * 1024


def pairs(count, first):
    both = []
    for low in range(first, count - 1, 2):
        both += [(low, low + 1), (low + 1, low)]
    return both


def pick_blocks(own, sends, far):
    halo = sends.shape[1] // 2

    def kernel(sends_hbm, own_ref, out_ref, sends_ref, sems):
        pltpu.sync_copy(sends_hbm, sends_ref)
        odd = lax.rem(lax.axis_index(AXIS), 2)
        first = (odd if far else 1 - odd) * halo
        copies = []
        for place in range(halo):
            block = sends_ref[0, first + place]
            copies.append(
                pltpu.make_async_copy(own_ref.at[block], out_ref.at[place], sems.at[place])
            )
        for copy in copies:
            copy.start()
        for copy in copies:
            copy.wait()

    size = halo * own.shape[1] * own.shape[2] * own.dtype.itemsize
    return pl.pallas_call(
        kernel,
        out_shape=jax.ShapeDtypeStruct((halo,) + own.shape[1:], own.dtype),
        in_specs=[pl.BlockSpec(memory_space=pltpu.HBM)] * 2,
        out_specs=pl.BlockSpec(memory_space=pltpu.VMEM),
        scratch_shapes=[pltpu.SMEM(sends.shape, sends.dtype), pltpu.SemaphoreType.DMA((halo,))],
        compiler_params=pltpu.CompilerParams(vmem_limit_bytes=VMEM_BYTES),
        cost_estimate=pl.CostEstimate(flops=0, bytes_accessed=2 * size, transcendentals=0),
    )(
        pltpu.with_memory_space_constraint(sends, pltpu.HBM),
        pltpu.with_memory_space_constraint(own, pltpu.HBM),
    )


def own_terms(own, blocks, columns):
    params, count, slots, size, _ = blocks.shape
    width = own.shape[2]

    def kernel(columns_ref, own_ref, blocks_ref, out_ref):
        @pl.loop(0, count, unroll=4)
        def _(row):
            at = pl.ds(pl.multiple_of(row * size, size), size)
            for param in range(params):
                left, right = [blocks_ref[param, row, 0]], [own_ref[row]]
                for slot in range(1, slots):
                    block = blocks_ref[param, row, slot]
                    column = columns_ref[param, row, slot - 1]
                    left.append(jnp.where(column < count, block, jnp.zeros_like(block)))
                    right.append(own_ref[jnp.minimum(column, count - 1)])
                out_ref[param, at] = jnp.dot(
                    jnp.concatenate(left, axis=1),
                    jnp.concatenate(right, axis=0),
                    preferred_element_type=jnp.float32,
                )

    vmem = pl.BlockSpec(memory_space=pltpu.VMEM)
    terms = jax.ShapeDtypeStruct((params, count * size, width), jnp.float32)
    return pl.pallas_call(
        kernel,
        out_shape=terms,
        in_specs=[pl.BlockSpec(memory_space=pltpu.SMEM), vmem, vmem],
        out_specs=vmem,
        compiler_params=pltpu.CompilerParams(vmem_limit_bytes=VMEM_BYTES),
        cost_estimate=pl.CostEstimate(
            flops=2 * slots * size * terms.size,
            bytes_accessed=4 * terms.size + 2 * (own.size + blocks.size),
            transcendentals=0,
        ),
    )(columns, own, blocks)


def project(turned, terms, far, near, blocks, columns):
    params, count, slots, size, _ = blocks.shape
    halo, _, width = far.shape
    half = turned.shape[0] // 2

    def kernel(
        columns_ref, turned_ref, terms_ref, far_ref, near_ref, blocks_ref,
        keep_ref, give_ref, list_ref, image_ref,
    ):
        odd = lax.rem(lax.axis_index(AXIS), 2)
        list_ref[pl.ds(odd * halo, halo)] = far_ref[...]
        list_ref[pl.ds((1 - odd) * halo, halo)] = near_ref[...]

        @pl.loop(0, count, unroll=4)
        def _(row):
            at = pl.ds(pl.multiple_of(row * size, size), size)
            for param in range(params):
                left, right = [], []
                for slot in range(1, slots):
                    block = blocks_ref[param, row, slot]
                    column = columns_ref[param, row, slot - 1]
                    left.append(jnp.where(column < count, jnp.zeros_like(block), block))
                    right.append(list_ref[jnp.maximum(column - count, 0)])
                image = terms_ref[param, at] + jnp.dot(
                    jnp.concatenate(left, axis=1),
                    jnp.concatenate(right, axis=0),
                    preferred_element_type=jnp.float32,
                )
                image_ref[at, pl.ds(param * width, width)] = image.astype(image_ref.dtype)

        step = 256 if width % 256 == 0 else width
        for at in range(0, params * width, step):
            cols = pl.ds(at, step)
            both = jnp.dot(
                turned_ref[...], image_ref[:, cols], preferred_element_type=jnp.float32
            )
            give_ref[:, cols] = both[:half].astype(give_ref.dtype)
            keep_ref[:, cols] = both[half:]

    vmem = pl.BlockSpec(memory_space=pltpu.VMEM)
    flops = 2 * params * count * size * width * ((slots - 1) * size + 2 * half)
    moved = 4 * terms.size + 2 * (turned.size + 2 * far.size + blocks.size)
    return pl.pallas_call(
        kernel,
        out_shape=(
            jax.ShapeDtypeStruct((half, params * width), jnp.float32),
            jax.ShapeDtypeStruct((half, params * width), jnp.bfloat16),
        ),
        in_specs=[pl.BlockSpec(memory_space=pltpu.SMEM)] + [vmem] * 5,
        out_specs=(vmem,) * 2,
        scratch_shapes=[
            pltpu.VMEM((2 * halo, size, width), far.dtype),
            pltpu.VMEM((count * size, params * width), jnp.bfloat16),
        ],
        compiler_params=pltpu.CompilerParams(vmem_limit_bytes=VMEM_BYTES),
        cost_estimate=pl.CostEstimate(flops=flops, bytes_accessed=moved, transcendentals=0),
    )(columns, turned, terms, far, near, blocks)


def shards(basis, blocks, columns, sends):
    params, count, _, size, _ = blocks.shape
    width = basis.shape[1]
    devices = lax.axis_size(AXIS)
    chips = devices // 2
    rows = width // devices
    own = basis.reshape(count, size, width)

    far = pick_blocks(own, sends, True)
    from_far = lax.ppermute(far, AXIS, pairs(devices, 1))
    near = pick_blocks(own, sends, False)
    from_near = lax.ppermute(near, AXIS, pairs(devices, 0))
    odd = lax.rem(lax.axis_index(AXIS), 2)
    turned = basis.T.reshape(chips, 2, rows, count * size).transpose(1, 0, 2, 3)
    turned = jnp.where(odd == 0, turned[::-1], turned).reshape(width, count * size)

    terms = own_terms(own, blocks, columns)

    keep, give = project(turned, terms, from_far, from_near, blocks, columns)
    taken = lax.ppermute(give, AXIS, pairs(devices, 0))
    chip_sum = (keep + taken.astype(jnp.float32)).astype(jnp.bfloat16)
    groups = [list(range(core, devices, 2)) for core in range(2)]
    parts = lax.all_to_all(
        chip_sum.reshape(chips, rows, params * width), AXIS,
        split_axis=0, concat_axis=0, axis_index_groups=groups, tiled=True,
    )
    return jnp.sum(parts.astype(jnp.float32), axis=0)


def solution(mesh):
    placed = (
        P(("grp", "mesh"), None),
        P(None, ("grp", "mesh"), None, None, None),
        P(None, ("grp", "mesh"), None),
        P(("grp", "mesh"), None),
    )
    return jax.shard_map(
        shards, mesh=mesh, in_specs=placed, out_specs=P(("grp", "mesh"), None), check_vma=False
    )
```

```python
import jax
import jax.numpy as jnp
from jax import lax
from jax.experimental import pallas as pl
from jax.experimental.pallas import tpu as pltpu
from jax.sharding import PartitionSpec as P

AXIS = "mesh"
LANES = 128
VMEM_BYTES = 28 * 1024 * 1024
VMEM = pl.BlockSpec(memory_space=pltpu.VMEM)
SMEM = pl.BlockSpec(memory_space=pltpu.SMEM)
PARAMETERS = pltpu.CompilerParams(vmem_limit_bytes=VMEM_BYTES)


def cost(flops, moved):
    return pl.CostEstimate(flops=flops, bytes_accessed=moved, transcendentals=0)


def pairs(count, first):
    both = []
    for low in range(first, count - 1, 2):
        both += [(low, low + 1), (low + 1, low)]
    return both


def chunks(width):
    first = width // 4
    if first % LANES:
        return [(0, width)]
    return [(0, first), (first, width - first)]


def copy_listed(own_ref, sends_ref, part, far_ref, near_ref):
    halo = far_ref.shape[0]
    odd = lax.rem(lax.axis_index(AXIS), 2)
    for place in range(halo):
        far_ref[place] = own_ref[sends_ref[0, odd * halo + place], :, pl.ds(*part)]
    for place in range(halo):
        near_ref[place] = own_ref[sends_ref[0, (1 - odd) * halo + place], :, pl.ds(*part)]


def pick_first(own, sends, part):
    count, size, _ = own.shape
    listed = jax.ShapeDtypeStruct((sends.shape[1] // 2, size, part[1]), own.dtype)

    def kernel(sends_hbm, own_hbm, own_ref, far_ref, near_ref, sends_ref, sems):
        lists = pltpu.make_async_copy(sends_hbm, sends_ref, sems.at[0])
        load = pltpu.make_async_copy(own_hbm, own_ref, sems.at[1])
        lists.start()
        load.start()
        lists.wait()
        load.wait()
        copy_listed(own_ref, sends_ref, part, far_ref, near_ref)

    return pl.pallas_call(
        kernel,
        out_shape=(jax.ShapeDtypeStruct(own.shape, own.dtype), listed, listed),
        in_specs=[pl.BlockSpec(memory_space=pltpu.HBM)] * 2,
        out_specs=(VMEM,) * 3,
        scratch_shapes=[pltpu.SMEM(sends.shape, sends.dtype), pltpu.SemaphoreType.DMA((2,))],
        compiler_params=PARAMETERS,
        cost_estimate=cost(0, 4 * own.size),
    )(
        pltpu.with_memory_space_constraint(sends, pltpu.HBM),
        pltpu.with_memory_space_constraint(own, pltpu.HBM),
    )


def pick_next(own, sends, part):
    listed = jax.ShapeDtypeStruct((sends.shape[1] // 2, own.shape[1], part[1]), own.dtype)

    def kernel(sends_hbm, own_ref, far_ref, near_ref, sends_ref):
        pltpu.sync_copy(sends_hbm, sends_ref)
        copy_listed(own_ref, sends_ref, part, far_ref, near_ref)

    return pl.pallas_call(
        kernel,
        out_shape=(listed, listed),
        in_specs=[pl.BlockSpec(memory_space=pltpu.HBM), VMEM],
        out_specs=(VMEM,) * 2,
        scratch_shapes=[pltpu.SMEM(sends.shape, sends.dtype)],
        compiler_params=PARAMETERS,
        cost_estimate=cost(0, 0),
    )(pltpu.with_memory_space_constraint(sends, pltpu.HBM), own)


def own_terms(own, blocks, columns, start, span):
    params, count, slots, size, _ = blocks.shape

    def kernel(columns_ref, own_ref, blocks_ref, out_ref):
        cols = pl.ds(start, span)

        @pl.loop(0, count, unroll=4)
        def _(row):
            at = pl.ds(pl.multiple_of(row * size, size), size)
            for param in range(params):
                left, right = [blocks_ref[param, row, 0]], [own_ref[row, :, cols]]
                for slot in range(1, slots):
                    block = blocks_ref[param, row, slot]
                    column = columns_ref[param, row, slot - 1]
                    left.append(jnp.where(column < count, block, jnp.zeros_like(block)))
                    right.append(own_ref[jnp.minimum(column, count - 1), :, cols])
                out_ref[param, at] = jnp.dot(
                    jnp.concatenate(left, axis=1),
                    jnp.concatenate(right, axis=0),
                    preferred_element_type=jnp.float32,
                )

    terms = jax.ShapeDtypeStruct((params, count * size, span), jnp.float32)
    return pl.pallas_call(
        kernel,
        out_shape=terms,
        in_specs=[SMEM, VMEM, VMEM],
        out_specs=VMEM,
        compiler_params=PARAMETERS,
        cost_estimate=cost(0, 0),
    )(columns, own, blocks)


def transposed(own, devices):
    count, size, width = own.shape
    chips, rows = devices // 2, width // devices
    if rows % 16:
        turned = own.reshape(count * size, width).T.reshape(chips, 2, rows, count * size)
        return turned.transpose(1, 0, 2, 3).reshape(width, count * size)

    def kernel(own_ref, out_ref):
        @pl.loop(0, count)
        def _(block):
            cols = pl.ds(pl.multiple_of(block * size, size), size)
            turned = own_ref[block].T
            for device in range(devices):
                chip, core = divmod(device, 2)
                out_ref[pl.ds((core * chips + chip) * rows, rows), cols] = (
                    turned[device * rows : (device + 1) * rows]
                )

    return pl.pallas_call(
        kernel,
        out_shape=jax.ShapeDtypeStruct((width, count * size), own.dtype),
        in_specs=[VMEM],
        out_specs=VMEM,
        compiler_params=PARAMETERS,
        cost_estimate=cost(0, 0),
    )(own)


def image_and_give(turned, terms, far, near, blocks, columns):
    params, count, slots, size, _ = blocks.shape
    halo, _, span = far.shape
    half = turned.shape[0] // 2

    def kernel(
        columns_ref, turned_ref, terms_ref, far_ref, near_ref, blocks_ref,
        image_ref, give_ref, list_ref,
    ):
        odd = lax.rem(lax.axis_index(AXIS), 2)
        list_ref[pl.ds(odd * halo, halo)] = far_ref[...]
        list_ref[pl.ds((1 - odd) * halo, halo)] = near_ref[...]

        @pl.loop(0, count, unroll=4)
        def _(row):
            at = pl.ds(pl.multiple_of(row * size, size), size)
            for param in range(params):
                left, right = [], []
                for slot in range(1, slots):
                    block = blocks_ref[param, row, slot]
                    column = columns_ref[param, row, slot - 1]
                    left.append(jnp.where(column < count, jnp.zeros_like(block), block))
                    right.append(list_ref[jnp.maximum(column - count, 0)])
                image = terms_ref[param, at] + jnp.dot(
                    jnp.concatenate(left, axis=1),
                    jnp.concatenate(right, axis=0),
                    preferred_element_type=jnp.float32,
                )
                image_ref[at, pl.ds(param * span, span)] = image.astype(image_ref.dtype)

        other = pl.ds(pl.multiple_of((1 - odd) * half, half), half)
        for cols in steps(params * span):
            give_ref[:, cols] = jnp.dot(
                turned_ref[other], image_ref[:, cols], preferred_element_type=jnp.float32
            ).astype(give_ref.dtype)

    rows = count * size
    flops = 2 * params * rows * span * ((slots - 1) * size + half)
    moved = 4 * terms.size + 2 * (half * rows + 2 * far.size + blocks.size + params * span * (rows + half))
    return pl.pallas_call(
        kernel,
        out_shape=(
            jax.ShapeDtypeStruct((rows, params * span), jnp.bfloat16),
            jax.ShapeDtypeStruct((half, params * span), jnp.bfloat16),
        ),
        in_specs=[SMEM] + [VMEM] * 5,
        out_specs=(VMEM,) * 2,
        scratch_shapes=[pltpu.VMEM((2 * halo, size, span), far.dtype)],
        compiler_params=PARAMETERS,
        cost_estimate=cost(flops, moved),
    )(columns, turned, terms, far, near, blocks)


def steps(columns):
    step = 2 * LANES if columns % (2 * LANES) == 0 else columns
    return [pl.ds(at, step) for at in range(0, columns, step)]


def keep_rows(turned, image):
    half, rows = turned.shape[0] // 2, turned.shape[1]
    columns = image.shape[1]

    def kernel(turned_ref, image_ref, keep_ref):
        odd = lax.rem(lax.axis_index(AXIS), 2)
        mine = pl.ds(pl.multiple_of(odd * half, half), half)
        for cols in steps(columns):
            keep_ref[:, cols] = jnp.dot(
                turned_ref[mine], image_ref[:, cols], preferred_element_type=jnp.float32
            )

    return pl.pallas_call(
        kernel,
        out_shape=jax.ShapeDtypeStruct((half, columns), jnp.float32),
        in_specs=[VMEM] * 2,
        out_specs=VMEM,
        compiler_params=PARAMETERS,
        cost_estimate=cost(
            2 * half * rows * columns, 2 * rows * (half + columns) + 4 * half * columns
        ),
    )(turned, image)


def add_chips(received, params, width):
    rows = received[0].shape[1]
    ranges = chunks(width)

    def kernel(*refs):
        out_ref = refs[-1]
        for (start, span), ref in zip(ranges, refs):
            total = jnp.sum(ref[...].astype(jnp.float32), axis=0)
            for param in range(params):
                out_ref[:, pl.ds(param * width + start, span)] = total[:, param * span : (param + 1) * span]

    return pl.pallas_call(
        kernel,
        out_shape=jax.ShapeDtypeStruct((rows, params * width), jnp.float32),
        in_specs=[VMEM] * len(received),
        out_specs=VMEM,
        compiler_params=PARAMETERS,
        cost_estimate=cost(0, sum(2 * part.size for part in received)),
    )(*received)


def shards(basis, blocks, columns, sends):
    params, count, _, size, _ = blocks.shape
    width = basis.shape[1]
    devices = lax.axis_size(AXIS)
    chips = devices // 2
    rows = width // devices
    ranges = chunks(width)
    near_pairs = pairs(devices, 0)

    own, far, near = pick_first(basis.reshape(count, size, width), sends, ranges[0])
    listed = [(far, near)]
    terms = [own_terms(own, blocks, columns, *ranges[0])]
    own, terms[0] = lax.optimization_barrier((own, terms[0]))
    listed += [pick_next(own, sends, part) for part in ranges[1:]]
    halos = [
        (lax.ppermute(far, AXIS, pairs(devices, 1)), lax.ppermute(near, AXIS, near_pairs))
        for far, near in listed
    ]
    terms += [own_terms(own, blocks, columns, *part) for part in ranges[1:]]
    turned = transposed(own, devices)
    groups = [list(range(core, devices, 2)) for core in range(2)]
    received = []
    for (_, span), (far, near), term in zip(ranges, halos, terms):
        if received:
            received[-1], term = lax.optimization_barrier((received[-1], term))
        image, give = image_and_give(turned, term, far, near, blocks, columns)
        taken = lax.ppermute(give, AXIS, near_pairs)
        keep = keep_rows(turned, image)
        chip_sum = (keep + taken.astype(jnp.float32)).astype(jnp.bfloat16)
        parts = lax.all_to_all(
            chip_sum.reshape(chips, rows, params * span), AXIS,
            split_axis=0, concat_axis=0, axis_index_groups=groups, tiled=True,
        )
        received.append(parts)
    return add_chips(received, params, width)


def solution(mesh):
    placed = (
        P(("grp", "mesh"), None),
        P(None, ("grp", "mesh"), None, None, None),
        P(None, ("grp", "mesh"), None),
        P(("grp", "mesh"), None),
    )
    return jax.shard_map(
        shards, mesh=mesh, in_specs=placed, out_specs=P(("grp", "mesh"), None), check_vma=False
    )
```

```python
import jax
import jax.numpy as jnp
from jax import lax
from jax.experimental import pallas as pl
from jax.experimental.pallas import tpu as pltpu
from jax.sharding import PartitionSpec as P

AXIS = "mesh"
LANES = 128
EASE = 8
VMEM_BYTES = 24 * 1024 * 1024
VMEM = pl.BlockSpec(memory_space=pltpu.VMEM)
SMEM = pl.BlockSpec(memory_space=pltpu.SMEM)
PARAMETERS = pltpu.CompilerParams(vmem_limit_bytes=VMEM_BYTES)


def cost(flops, moved):
    return pl.CostEstimate(flops=flops // EASE, bytes_accessed=moved // EASE, transcendentals=0)


def pairs(count, first):
    both = []
    for low in range(first, count - 1, 2):
        both += [(low, low + 1), (low + 1, low)]
    return both


def chunks(width):
    first = width // 4 * 3
    if first % LANES:
        return [(0, width)]
    return [(0, first), (first, width - first)]


def halves(width):
    half = width // 2
    return [(0, width)] if half % LANES else [(0, half), (half, half)]


def copy_listed(own_ref, sends_ref, far, part, out_ref):
    halo = out_ref.shape[0]
    odd = lax.rem(lax.axis_index(AXIS), 2)
    first = (odd if far else 1 - odd) * halo
    for place in range(halo):
        out_ref[place] = own_ref[sends_ref[0, first + place], :, pl.ds(*part)]


def pick_first(own, sends, part):
    count, size, width = own.shape
    halo = sends.shape[1] // 2
    ranges = halves(width)

    def kernel(sends_hbm, own_hbm, own_ref, far_ref, *refs):
        near_refs, (sends_ref, sems) = refs[: len(ranges)], refs[len(ranges) :]
        lists = pltpu.make_async_copy(sends_hbm, sends_ref, sems.at[0])
        load = pltpu.make_async_copy(own_hbm, own_ref, sems.at[1])
        lists.start()
        load.start()
        lists.wait()
        load.wait()
        copy_listed(own_ref, sends_ref, True, part, far_ref)
        for near_part, near_ref in zip(ranges, near_refs):
            copy_listed(own_ref, sends_ref, False, near_part, near_ref)

    return pl.pallas_call(
        kernel,
        out_shape=[
            jax.ShapeDtypeStruct(own.shape, own.dtype),
            jax.ShapeDtypeStruct((halo, size, part[1]), own.dtype),
        ]
        + [jax.ShapeDtypeStruct((halo, size, span), own.dtype) for _, span in ranges],
        in_specs=[pl.BlockSpec(memory_space=pltpu.HBM)] * 2,
        out_specs=[VMEM] * (2 + len(ranges)),
        scratch_shapes=[pltpu.SMEM(sends.shape, sends.dtype), pltpu.SemaphoreType.DMA((2,))],
        compiler_params=PARAMETERS,
        cost_estimate=cost(0, 6 * own.size),
    )(
        pltpu.with_memory_space_constraint(sends, pltpu.HBM),
        pltpu.with_memory_space_constraint(own, pltpu.HBM),
    )


def pick_next(own, sends, part):
    _, size, _ = own.shape
    halo = sends.shape[1] // 2

    def kernel(sends_hbm, own_ref, far_ref, sends_ref):
        pltpu.sync_copy(sends_hbm, sends_ref)
        copy_listed(own_ref, sends_ref, True, part, far_ref)

    return pl.pallas_call(
        kernel,
        out_shape=jax.ShapeDtypeStruct((halo, size, part[1]), own.dtype),
        in_specs=[pl.BlockSpec(memory_space=pltpu.HBM), VMEM],
        out_specs=VMEM,
        scratch_shapes=[pltpu.SMEM(sends.shape, sends.dtype)],
        compiler_params=PARAMETERS,
        cost_estimate=cost(0, 4 * halo * size * part[1]),
    )(pltpu.with_memory_space_constraint(sends, pltpu.HBM), own)


def transposed(own, devices):
    count, size, width = own.shape
    chips, rows = devices // 2, width // devices
    if rows % 16:
        turned = own.reshape(count * size, width).T.reshape(chips, 2, rows, count * size)
        return turned.transpose(1, 0, 2, 3).reshape(width, count * size)

    def kernel(own_ref, out_ref):
        @pl.loop(0, count)
        def _(block):
            cols = pl.ds(pl.multiple_of(block * size, size), size)
            turned = own_ref[block].T
            for device in range(devices):
                chip, core = divmod(device, 2)
                out_ref[pl.ds((core * chips + chip) * rows, rows), cols] = (
                    turned[device * rows : (device + 1) * rows]
                )

    return pl.pallas_call(
        kernel,
        out_shape=jax.ShapeDtypeStruct((width, count * size), own.dtype),
        in_specs=[VMEM],
        out_specs=VMEM,
        compiler_params=PARAMETERS,
        cost_estimate=cost(0, 4 * own.size),
    )(own)


def steps(columns):
    step = 2 * LANES if columns % (2 * LANES) == 0 else columns
    return [pl.ds(at, step) for at in range(0, columns, step)]


def halo_place(column, count, halo):
    place = column - count
    upper = place >= halo
    odd = lax.rem(lax.axis_index(AXIS), 2)
    return upper == (odd == 1), jnp.where(upper, place - halo, place)


def fold_far(turned, blocks, columns, halo):
    params, count, slots, size, _ = blocks.shape
    width = turned.shape[0]

    def kernel(columns_ref, turned_ref, blocks_ref, out_ref, sum_ref):
        sum_ref[...] = jnp.zeros_like(sum_ref)

        @pl.loop(0, count)
        def _(row):
            rows = pl.ds(pl.multiple_of(row * size, size), size)
            for param in range(params):
                for slot in range(1, slots):
                    column = columns_ref[param, row, slot - 1]
                    far, place = halo_place(column, count, halo)

                    @pl.when((column >= count) & far)
                    def _():
                        at = pl.ds(pl.multiple_of(place * size, size), size)
                        sum_ref[param, :, at] += jnp.dot(
                            turned_ref[:, rows],
                            blocks_ref[param, row, slot],
                            preferred_element_type=jnp.float32,
                        )

        out_ref[...] = sum_ref[...].astype(out_ref.dtype)

    shape = (params, width, halo * size)
    return pl.pallas_call(
        kernel,
        out_shape=jax.ShapeDtypeStruct(shape, turned.dtype),
        in_specs=[SMEM, VMEM, VMEM],
        out_specs=VMEM,
        scratch_shapes=[pltpu.VMEM(shape, jnp.float32)],
        compiler_params=PARAMETERS,
        cost_estimate=cost(
            params * count * (slots - 1) * size * size * width, 2 * (turned.size + blocks.size)
        ),
    )(columns, turned, blocks)


def local_parts(turned, own, nears, blocks, columns):
    params, count, slots, size, _ = blocks.shape
    halo, width = nears[0].shape[0], own.shape[2]
    ranges = halves(width)

    def kernel(columns_ref, turned_ref, own_ref, blocks_ref, *refs):
        near_refs, (out_ref, list_ref, image_ref) = refs[: len(ranges)], refs[len(ranges) :]
        list_ref[pl.ds(0, count)] = own_ref[...]
        for part, near_ref in zip(ranges, near_refs):
            list_ref[pl.ds(count, halo), :, pl.ds(*part)] = near_ref[...]

        @pl.loop(0, count, unroll=4)
        def _(row):
            at = pl.ds(pl.multiple_of(row * size, size), size)
            for param in range(params):
                left, right = [blocks_ref[param, row, 0]], [list_ref[row]]
                for slot in range(1, slots):
                    block = blocks_ref[param, row, slot]
                    column = columns_ref[param, row, slot - 1]
                    far, place = halo_place(column, count, halo)
                    here = (column < count) | jnp.logical_not(far)
                    left.append(jnp.where(here, block, jnp.zeros_like(block)))
                    right.append(list_ref[jnp.where(column < count, column, count + place)])
                image = jnp.dot(
                    jnp.concatenate(left, axis=1),
                    jnp.concatenate(right, axis=0),
                    preferred_element_type=jnp.float32,
                )
                image_ref[at, pl.ds(param * width, width)] = image.astype(image_ref.dtype)

        for param in range(params):
            for cols in steps(width):
                out_ref[param, :, cols] = jnp.dot(
                    turned_ref[...],
                    image_ref[:, pl.ds(param * width + cols.start, cols.size)],
                    preferred_element_type=jnp.float32,
                )

    rows = count * size
    return pl.pallas_call(
        kernel,
        out_shape=jax.ShapeDtypeStruct((params, width, width), jnp.float32),
        in_specs=[SMEM] + [VMEM] * (3 + len(ranges)),
        out_specs=VMEM,
        scratch_shapes=[
            pltpu.VMEM((count + halo, size, width), own.dtype),
            pltpu.VMEM((rows, params * width), jnp.bfloat16),
        ],
        compiler_params=PARAMETERS,
        cost_estimate=cost(
            2 * params * rows * width * (slots * size + width),
            2 * (turned.size + 2 * own.size + blocks.size) + 4 * params * width * width,
        ),
    )(columns, turned, own, blocks, *nears)


def with_far(local, folds, far, part, mine):
    params, width, depth = folds.shape
    half = width // 2
    start, span = part

    def kernel(local_ref, folds_ref, far_ref, out_ref):
        odd = lax.rem(lax.axis_index(AXIS), 2)
        rows = pl.ds(pl.multiple_of((odd if mine else 1 - odd) * half, half), half)
        right = far_ref[...].reshape(depth, span)
        for param in range(params):
            total = local_ref[param, rows, pl.ds(start, span)] + jnp.dot(
                folds_ref[param, rows], right, preferred_element_type=jnp.float32
            )
            out_ref[:, pl.ds(param * span, span)] = total.astype(out_ref.dtype)

    return pl.pallas_call(
        kernel,
        out_shape=jax.ShapeDtypeStruct(
            (half, params * span), jnp.float32 if mine else jnp.bfloat16
        ),
        in_specs=[VMEM] * 3,
        out_specs=VMEM,
        compiler_params=PARAMETERS,
        cost_estimate=cost(
            2 * params * half * depth * span,
            4 * params * half * span + params * half * depth * 2 + 2 * depth * span,
        ),
    )(local, folds, far)


def add_chips(received, params, width):
    rows = received[0].shape[1]
    ranges = chunks(width)

    def kernel(*refs):
        out_ref = refs[-1]
        for (start, span), ref in zip(ranges, refs):
            total = jnp.sum(ref[...].astype(jnp.float32), axis=0)
            for param in range(params):
                out_ref[:, pl.ds(param * width + start, span)] = total[:, param * span : (param + 1) * span]

    return pl.pallas_call(
        kernel,
        out_shape=jax.ShapeDtypeStruct((rows, params * width), jnp.float32),
        in_specs=[VMEM] * len(received),
        out_specs=VMEM,
        compiler_params=PARAMETERS,
        cost_estimate=cost(0, sum(2 * part.size for part in received)),
    )(*received)


def shards(basis, blocks, columns, sends):
    params, count, _, size, _ = blocks.shape
    width = basis.shape[1]
    halo = sends.shape[1] // 2
    devices = lax.axis_size(AXIS)
    chips = devices // 2
    rows = width // devices
    ranges = chunks(width)
    near_pairs, far_pairs = pairs(devices, 0), pairs(devices, 1)

    own, first, *nears = pick_first(basis.reshape(count, size, width), sends, ranges[0])
    fars = [lax.ppermute(first, AXIS, far_pairs)]
    nears = [lax.ppermute(near, AXIS, near_pairs) for near in nears]
    for part in ranges[1:]:
        fars.append(lax.ppermute(pick_next(own, sends, part), AXIS, far_pairs))

    turned = transposed(own, devices)
    folds = fold_far(turned, blocks, columns, halo)
    local = local_parts(turned, own, nears, blocks, columns)

    groups = [list(range(core, devices, 2)) for core in range(2)]
    received, ready = [], None
    for part, far in zip(ranges, fars):
        if ready is not None:
            ready, far = lax.optimization_barrier((ready, far))
            received.append(exchange(ready, groups))
        give = with_far(local, folds, far, part, False)
        taken = lax.ppermute(give, AXIS, near_pairs)
        keep = with_far(local, folds, far, part, True)
        chip_sum = (keep + taken.astype(jnp.float32)).astype(jnp.bfloat16)
        ready = chip_sum.reshape(chips, rows, params * part[1])
    received.append(exchange(ready, groups))
    return add_chips(received, params, width)


def exchange(parts, groups):
    return lax.all_to_all(
        parts, AXIS, split_axis=0, concat_axis=0, axis_index_groups=groups, tiled=True
    )


def solution(mesh):
    placed = (
        P(("grp", "mesh"), None),
        P(None, ("grp", "mesh"), None, None, None),
        P(None, ("grp", "mesh"), None),
        P(("grp", "mesh"), None),
    )
    return jax.shard_map(
        shards, mesh=mesh, in_specs=placed, out_specs=P(("grp", "mesh"), None), check_vma=False
    )
```

```python
import jax
import jax.numpy as jnp
from jax import lax
from jax.experimental import pallas as pl
from jax.experimental.pallas import tpu as pltpu
from jax.sharding import PartitionSpec as P

AXIS = "mesh"
LANES = 128
EASE = 8
VMEM_BYTES = 24 * 1024 * 1024
VMEM = pl.BlockSpec(memory_space=pltpu.VMEM)
SMEM = pl.BlockSpec(memory_space=pltpu.SMEM)
PARAMETERS = pltpu.CompilerParams(vmem_limit_bytes=VMEM_BYTES)


def cost(flops, moved):
    return pl.CostEstimate(flops=flops // EASE, bytes_accessed=moved // EASE, transcendentals=0)


def pairs(count, first):
    both = []
    for low in range(first, count - 1, 2):
        both += [(low, low + 1), (low + 1, low)]
    return both


def chunks(width):
    first = width
    if first == width or first % LANES:
        return [(0, width)]
    return [(0, first), (first, width - first)]


def halves(width):
    half = width // 2
    return [(0, width)] if half % LANES else [(0, half), (half, half)]


def copy_listed(own_ref, sends_ref, far, part, out_ref):
    halo = out_ref.shape[0]
    odd = lax.rem(lax.axis_index(AXIS), 2)
    first = (odd if far else 1 - odd) * halo
    for place in range(halo):
        out_ref[place] = own_ref[sends_ref[0, first + place], :, pl.ds(*part)]


def pick_first(own, sends, part):
    count, size, width = own.shape
    halo = sends.shape[1] // 2
    ranges = halves(width)

    def kernel(sends_hbm, own_hbm, own_ref, far_ref, *refs):
        near_refs, (sends_ref, sems) = refs[: len(ranges)], refs[len(ranges) :]
        lists = pltpu.make_async_copy(sends_hbm, sends_ref, sems.at[0])
        load = pltpu.make_async_copy(own_hbm, own_ref, sems.at[1])
        lists.start()
        load.start()
        lists.wait()
        load.wait()
        copy_listed(own_ref, sends_ref, True, part, far_ref)
        for near_part, near_ref in zip(ranges, near_refs):
            copy_listed(own_ref, sends_ref, False, near_part, near_ref)

    return pl.pallas_call(
        kernel,
        out_shape=[
            jax.ShapeDtypeStruct(own.shape, own.dtype),
            jax.ShapeDtypeStruct((halo, size, part[1]), own.dtype),
        ]
        + [jax.ShapeDtypeStruct((halo, size, span), own.dtype) for _, span in ranges],
        in_specs=[pl.BlockSpec(memory_space=pltpu.HBM)] * 2,
        out_specs=[VMEM] * (2 + len(ranges)),
        scratch_shapes=[pltpu.SMEM(sends.shape, sends.dtype), pltpu.SemaphoreType.DMA((2,))],
        compiler_params=PARAMETERS,
        cost_estimate=cost(0, 6 * own.size),
    )(
        pltpu.with_memory_space_constraint(sends, pltpu.HBM),
        pltpu.with_memory_space_constraint(own, pltpu.HBM),
    )


def pick_next(own, sends, part):
    _, size, _ = own.shape
    halo = sends.shape[1] // 2

    def kernel(sends_hbm, own_ref, far_ref, sends_ref):
        pltpu.sync_copy(sends_hbm, sends_ref)
        copy_listed(own_ref, sends_ref, True, part, far_ref)

    return pl.pallas_call(
        kernel,
        out_shape=jax.ShapeDtypeStruct((halo, size, part[1]), own.dtype),
        in_specs=[pl.BlockSpec(memory_space=pltpu.HBM), VMEM],
        out_specs=VMEM,
        scratch_shapes=[pltpu.SMEM(sends.shape, sends.dtype)],
        compiler_params=PARAMETERS,
        cost_estimate=cost(0, 4 * halo * size * part[1]),
    )(pltpu.with_memory_space_constraint(sends, pltpu.HBM), own)


def transposed(own, devices):
    count, size, width = own.shape
    chips, rows = devices // 2, width // devices
    if rows % 16:
        turned = own.reshape(count * size, width).T.reshape(chips, 2, rows, count * size)
        return turned.transpose(1, 0, 2, 3).reshape(width, count * size)

    def kernel(own_ref, out_ref):
        @pl.loop(0, count)
        def _(block):
            cols = pl.ds(pl.multiple_of(block * size, size), size)
            turned = own_ref[block].T
            for device in range(devices):
                chip, core = divmod(device, 2)
                out_ref[pl.ds((core * chips + chip) * rows, rows), cols] = (
                    turned[device * rows : (device + 1) * rows]
                )

    return pl.pallas_call(
        kernel,
        out_shape=jax.ShapeDtypeStruct((width, count * size), own.dtype),
        in_specs=[VMEM],
        out_specs=VMEM,
        compiler_params=PARAMETERS,
        cost_estimate=cost(0, 4 * own.size),
    )(own)


def steps(columns):
    step = 2 * LANES if columns % (2 * LANES) == 0 else columns
    return [pl.ds(at, step) for at in range(0, columns, step)]


def halo_place(column, count, halo):
    place = column - count
    upper = place >= halo
    odd = lax.rem(lax.axis_index(AXIS), 2)
    return upper == (odd == 1), jnp.where(upper, place - halo, place)


def fold_far(turned, blocks, columns, halo):
    params, count, slots, size, _ = blocks.shape
    width = turned.shape[0]

    def kernel(columns_ref, turned_ref, blocks_ref, out_ref, sum_ref):
        sum_ref[...] = jnp.zeros_like(sum_ref)

        @pl.loop(0, count)
        def _(row):
            rows = pl.ds(pl.multiple_of(row * size, size), size)
            for param in range(params):
                for slot in range(1, slots):
                    column = columns_ref[param, row, slot - 1]
                    far, place = halo_place(column, count, halo)

                    @pl.when((column >= count) & far)
                    def _():
                        at = pl.ds(pl.multiple_of(place * size, size), size)
                        sum_ref[param, :, at] += jnp.dot(
                            turned_ref[:, rows],
                            blocks_ref[param, row, slot],
                            preferred_element_type=jnp.float32,
                        )

        out_ref[...] = sum_ref[...].astype(out_ref.dtype)

    shape = (params, width, halo * size)
    return pl.pallas_call(
        kernel,
        out_shape=jax.ShapeDtypeStruct(shape, turned.dtype),
        in_specs=[SMEM, VMEM, VMEM],
        out_specs=VMEM,
        scratch_shapes=[pltpu.VMEM(shape, jnp.float32)],
        compiler_params=PARAMETERS,
        cost_estimate=cost(
            params * count * (slots - 1) * size * size * width, 2 * (turned.size + blocks.size)
        ),
    )(columns, turned, blocks)


def local_parts(turned, own, nears, blocks, columns):
    params, count, slots, size, _ = blocks.shape
    halo, width = nears[0].shape[0], own.shape[2]
    ranges = halves(width)

    def kernel(columns_ref, turned_ref, own_ref, blocks_ref, *refs):
        near_refs, (out_ref, list_ref, image_ref) = refs[: len(ranges)], refs[len(ranges) :]
        list_ref[pl.ds(0, count)] = own_ref[...]
        for part, near_ref in zip(ranges, near_refs):
            list_ref[pl.ds(count, halo), :, pl.ds(*part)] = near_ref[...]

        @pl.loop(0, count, unroll=4)
        def _(row):
            at = pl.ds(pl.multiple_of(row * size, size), size)
            for param in range(params):
                left, right = [blocks_ref[param, row, 0]], [list_ref[row]]
                for slot in range(1, slots):
                    block = blocks_ref[param, row, slot]
                    column = columns_ref[param, row, slot - 1]
                    far, place = halo_place(column, count, halo)
                    here = (column < count) | jnp.logical_not(far)
                    left.append(jnp.where(here, block, jnp.zeros_like(block)))
                    right.append(list_ref[jnp.where(column < count, column, count + place)])
                image = jnp.dot(
                    jnp.concatenate(left, axis=1),
                    jnp.concatenate(right, axis=0),
                    preferred_element_type=jnp.float32,
                )
                image_ref[at, pl.ds(param * width, width)] = image.astype(image_ref.dtype)

        for param in range(params):
            for cols in steps(width):
                out_ref[param, :, cols] = jnp.dot(
                    turned_ref[...],
                    image_ref[:, pl.ds(param * width + cols.start, cols.size)],
                    preferred_element_type=jnp.float32,
                )

    rows = count * size
    return pl.pallas_call(
        kernel,
        out_shape=jax.ShapeDtypeStruct((params, width, width), jnp.float32),
        in_specs=[SMEM] + [VMEM] * (3 + len(ranges)),
        out_specs=VMEM,
        scratch_shapes=[
            pltpu.VMEM((count + halo, size, width), own.dtype),
            pltpu.VMEM((rows, params * width), jnp.bfloat16),
        ],
        compiler_params=PARAMETERS,
        cost_estimate=cost(
            2 * params * rows * width * (slots * size + width),
            2 * (turned.size + 2 * own.size + blocks.size) + 4 * params * width * width,
        ),
    )(columns, turned, own, blocks, *nears)


def with_far(local, folds, far, part, mine):
    params, width, depth = folds.shape
    half = width // 2
    start, span = part

    def kernel(local_ref, folds_ref, far_ref, out_ref):
        odd = lax.rem(lax.axis_index(AXIS), 2)
        rows = pl.ds(pl.multiple_of((odd if mine else 1 - odd) * half, half), half)
        right = far_ref[...].reshape(depth, span)
        for param in range(params):
            total = local_ref[param, rows, pl.ds(start, span)] + jnp.dot(
                folds_ref[param, rows], right, preferred_element_type=jnp.float32
            )
            out_ref[:, pl.ds(param * span, span)] = total.astype(out_ref.dtype)

    return pl.pallas_call(
        kernel,
        out_shape=jax.ShapeDtypeStruct(
            (half, params * span), jnp.float32 if mine else jnp.bfloat16
        ),
        in_specs=[VMEM] * 3,
        out_specs=VMEM,
        compiler_params=PARAMETERS,
        cost_estimate=cost(
            2 * params * half * depth * span,
            4 * params * half * span + params * half * depth * 2 + 2 * depth * span,
        ),
    )(local, folds, far)


def add_chips(received, params, width):
    rows = received[0].shape[1]
    ranges = chunks(width)

    def kernel(*refs):
        out_ref = refs[-1]
        for (start, span), ref in zip(ranges, refs):
            total = jnp.sum(ref[...].astype(jnp.float32), axis=0)
            for param in range(params):
                out_ref[:, pl.ds(param * width + start, span)] = total[:, param * span : (param + 1) * span]

    return pl.pallas_call(
        kernel,
        out_shape=jax.ShapeDtypeStruct((rows, params * width), jnp.float32),
        in_specs=[VMEM] * len(received),
        out_specs=VMEM,
        compiler_params=PARAMETERS,
        cost_estimate=cost(0, sum(2 * part.size for part in received)),
    )(*received)


def shards(basis, blocks, columns, sends):
    params, count, _, size, _ = blocks.shape
    width = basis.shape[1]
    halo = sends.shape[1] // 2
    devices = lax.axis_size(AXIS)
    chips = devices // 2
    rows = width // devices
    ranges = chunks(width)
    near_pairs, far_pairs = pairs(devices, 0), pairs(devices, 1)

    own, first, *nears = pick_first(basis.reshape(count, size, width), sends, ranges[0])
    fars = [lax.ppermute(first, AXIS, far_pairs)]
    nears = [lax.ppermute(near, AXIS, near_pairs) for near in nears]
    for part in ranges[1:]:
        fars.append(lax.ppermute(pick_next(own, sends, part), AXIS, far_pairs))

    turned = transposed(own, devices)
    folds = fold_far(turned, blocks, columns, halo)
    local = local_parts(turned, own, nears, blocks, columns)

    groups = [list(range(core, devices, 2)) for core in range(2)]
    received, ready = [], None
    for part, far in zip(ranges, fars):
        if ready is not None:
            ready, far = lax.optimization_barrier((ready, far))
            received.append(exchange(ready, groups))
        give = with_far(local, folds, far, part, False)
        taken = lax.ppermute(give, AXIS, near_pairs)
        keep = with_far(local, folds, far, part, True)
        chip_sum = (keep + taken.astype(jnp.float32)).astype(jnp.bfloat16)
        ready = chip_sum.reshape(chips, rows, params * part[1])
    received.append(exchange(ready, groups))
    return add_chips(received, params, width)


def exchange(parts, groups):
    return lax.all_to_all(
        parts, AXIS, split_axis=0, concat_axis=0, axis_index_groups=groups, tiled=True
    )


def solution(mesh):
    placed = (
        P(("grp", "mesh"), None),
        P(None, ("grp", "mesh"), None, None, None),
        P(None, ("grp", "mesh"), None),
        P(("grp", "mesh"), None),
    )
    return jax.shard_map(
        shards, mesh=mesh, in_specs=placed, out_specs=P(("grp", "mesh"), None), check_vma=False
    )
```

```python
import jax
import jax.numpy as jnp
from jax import lax
from jax.experimental import pallas as pl
from jax.experimental.pallas import tpu as pltpu
from jax.sharding import PartitionSpec as P

AXIS = "mesh"
LANES = 128
EASE = 8
VMEM_BYTES = 24 * 1024 * 1024
VMEM = pl.BlockSpec(memory_space=pltpu.VMEM)
SMEM = pl.BlockSpec(memory_space=pltpu.SMEM)
PARAMETERS = pltpu.CompilerParams(vmem_limit_bytes=VMEM_BYTES)


def cost(flops, moved):
    return pl.CostEstimate(flops=flops // EASE, bytes_accessed=moved // EASE, transcendentals=0)


def pairs(count, first):
    both = []
    for low in range(first, count - 1, 2):
        both += [(low, low + 1), (low + 1, low)]
    return both


def chunks(width):
    first = width // 4
    if first % LANES:
        return [(0, width)]
    return [(0, first), (first, width - first)]


def pieces(part):
    start, span = part
    step = LANES if span % LANES == 0 else span
    return [(at, step) for at in range(start, start + span, step)]


def copy_listed(own_ref, sends_ref, far, part, out_ref):
    halo = out_ref.shape[0]
    odd = lax.rem(lax.axis_index(AXIS), 2)
    first = (odd if far else 1 - odd) * halo
    for place in range(halo):
        out_ref[place] = own_ref[sends_ref[0, first + place], :, pl.ds(*part)]


def pick_first(own, sends, part):
    count, size, _ = own.shape
    listed = jax.ShapeDtypeStruct((sends.shape[1] // 2, size, part[1]), own.dtype)

    def kernel(sends_hbm, own_hbm, own_ref, far_ref, near_ref, sends_ref, sems):
        lists = pltpu.make_async_copy(sends_hbm, sends_ref, sems.at[0])
        load = pltpu.make_async_copy(own_hbm, own_ref, sems.at[1])
        lists.start()
        load.start()
        lists.wait()
        load.wait()
        copy_listed(own_ref, sends_ref, True, part, far_ref)
        copy_listed(own_ref, sends_ref, False, part, near_ref)

    return pl.pallas_call(
        kernel,
        out_shape=(jax.ShapeDtypeStruct(own.shape, own.dtype), listed, listed),
        in_specs=[pl.BlockSpec(memory_space=pltpu.HBM)] * 2,
        out_specs=(VMEM,) * 3,
        scratch_shapes=[pltpu.SMEM(sends.shape, sends.dtype), pltpu.SemaphoreType.DMA((2,))],
        compiler_params=PARAMETERS,
        cost_estimate=cost(0, 6 * own.size),
    )(
        pltpu.with_memory_space_constraint(sends, pltpu.HBM),
        pltpu.with_memory_space_constraint(own, pltpu.HBM),
    )


def pick_next(own, sends, part):
    _, size, _ = own.shape
    halo = sends.shape[1] // 2
    parts = pieces(part)

    def kernel(sends_hbm, own_ref, far_ref, *refs):
        near_refs, sends_ref = refs[:-1], refs[-1]
        pltpu.sync_copy(sends_hbm, sends_ref)
        copy_listed(own_ref, sends_ref, True, part, far_ref)
        for piece, near_ref in zip(parts, near_refs):
            copy_listed(own_ref, sends_ref, False, piece, near_ref)

    spans = [part[1]] + [span for _, span in parts]
    return pl.pallas_call(
        kernel,
        out_shape=[jax.ShapeDtypeStruct((halo, size, span), own.dtype) for span in spans],
        in_specs=[pl.BlockSpec(memory_space=pltpu.HBM), VMEM],
        out_specs=[VMEM] * len(spans),
        scratch_shapes=[pltpu.SMEM(sends.shape, sends.dtype)],
        compiler_params=PARAMETERS,
        cost_estimate=cost(0, 8 * halo * size * part[1]),
    )(pltpu.with_memory_space_constraint(sends, pltpu.HBM), own)


def transposed(own, devices):
    count, size, width = own.shape
    chips, rows = devices // 2, width // devices
    if rows % 16:
        turned = own.reshape(count * size, width).T.reshape(chips, 2, rows, count * size)
        return turned.transpose(1, 0, 2, 3).reshape(width, count * size)

    def kernel(own_ref, out_ref):
        @pl.loop(0, count)
        def _(block):
            cols = pl.ds(pl.multiple_of(block * size, size), size)
            turned = own_ref[block].T
            for device in range(devices):
                chip, core = divmod(device, 2)
                out_ref[pl.ds((core * chips + chip) * rows, rows), cols] = (
                    turned[device * rows : (device + 1) * rows]
                )

    return pl.pallas_call(
        kernel,
        out_shape=jax.ShapeDtypeStruct((width, count * size), own.dtype),
        in_specs=[VMEM],
        out_specs=VMEM,
        compiler_params=PARAMETERS,
        cost_estimate=cost(0, 4 * own.size),
    )(own)


def steps(columns):
    step = 2 * LANES if columns % (2 * LANES) == 0 else columns
    return [pl.ds(at, step) for at in range(0, columns, step)]


def halo_place(column, count, halo):
    place = column - count
    upper = place >= halo
    odd = lax.rem(lax.axis_index(AXIS), 2)
    return upper == (odd == 1), jnp.where(upper, place - halo, place)


def fold_far(turned, blocks, columns, halo):
    params, count, slots, size, _ = blocks.shape
    width = turned.shape[0]

    def kernel(columns_ref, turned_ref, blocks_ref, out_ref, sum_ref):
        sum_ref[...] = jnp.zeros_like(sum_ref)

        @pl.loop(0, count, unroll=2)
        def _(row):
            rows = pl.ds(pl.multiple_of(row * size, size), size)
            for param in range(params):
                terms = jnp.dot(
                    turned_ref[:, rows],
                    jnp.concatenate(
                        [blocks_ref[param, row, slot] for slot in range(1, slots)], axis=1
                    ),
                    preferred_element_type=jnp.float32,
                )
                for slot in range(1, slots):
                    column = columns_ref[param, row, slot - 1]
                    far, place = halo_place(column, count, halo)
                    place = jnp.where((column >= count) & far, place, halo)
                    at = pl.ds(pl.multiple_of(place * size, size), size)
                    sum_ref[param, :, at] += terms[:, (slot - 1) * size : slot * size]

        out_ref[...] = sum_ref[:, :, pl.ds(0, halo * size)].astype(out_ref.dtype)

    shape = (params, width, halo * size)
    return pl.pallas_call(
        kernel,
        out_shape=jax.ShapeDtypeStruct(shape, turned.dtype),
        in_specs=[SMEM, VMEM, VMEM],
        out_specs=VMEM,
        scratch_shapes=[pltpu.VMEM((params, width, (halo + 1) * size), jnp.float32)],
        compiler_params=PARAMETERS,
        cost_estimate=cost(
            params * count * (slots - 1) * size * size * width, 2 * (turned.size + blocks.size)
        ),
    )(columns, turned, blocks)


def whole_image(turned, own, far, near, blocks, columns, part):
    params, count, slots, size, _ = blocks.shape
    halo, half = far.shape[0], turned.shape[0] // 2
    start, span = part

    def kernel(
        columns_ref, turned_ref, own_ref, far_ref, near_ref, blocks_ref, image_ref, give_ref, list_ref
    ):
        odd = lax.rem(lax.axis_index(AXIS), 2)
        list_ref[pl.ds(0, count)] = own_ref[:, :, pl.ds(start, span)]
        list_ref[pl.ds(count + odd * halo, halo)] = far_ref[...]
        list_ref[pl.ds(count + (1 - odd) * halo, halo)] = near_ref[...]

        @pl.loop(0, count, unroll=4)
        def _(row):
            at = pl.ds(pl.multiple_of(row * size, size), size)
            for param in range(params):
                left = [blocks_ref[param, row, slot] for slot in range(slots)]
                right = [list_ref[row]]
                for slot in range(1, slots):
                    right.append(list_ref[columns_ref[param, row, slot - 1]])
                image = jnp.dot(
                    jnp.concatenate(left, axis=1),
                    jnp.concatenate(right, axis=0),
                    preferred_element_type=jnp.float32,
                )
                image_ref[at, pl.ds(param * span, span)] = image.astype(image_ref.dtype)

        other = pl.ds(pl.multiple_of((1 - odd) * half, half), half)
        for cols in steps(params * span):
            give_ref[:, cols] = jnp.dot(
                turned_ref[other], image_ref[:, cols], preferred_element_type=jnp.float32
            ).astype(give_ref.dtype)

    rows = count * size
    return pl.pallas_call(
        kernel,
        out_shape=(
            jax.ShapeDtypeStruct((rows, params * span), jnp.bfloat16),
            jax.ShapeDtypeStruct((half, params * span), jnp.bfloat16),
        ),
        in_specs=[SMEM] + [VMEM] * 5,
        out_specs=(VMEM,) * 2,
        scratch_shapes=[pltpu.VMEM((count + 2 * halo, size, span), own.dtype)],
        compiler_params=PARAMETERS,
        cost_estimate=cost(
            2 * params * rows * span * (slots * size + half),
            2 * (half * rows + own.size + 2 * far.size + blocks.size + params * span * (rows + half)),
        ),
    )(columns, turned, own, far, near, blocks)


def keep_rows(turned, image):
    half, rows = turned.shape[0] // 2, turned.shape[1]
    columns = image.shape[1]

    def kernel(turned_ref, image_ref, keep_ref):
        odd = lax.rem(lax.axis_index(AXIS), 2)
        mine = pl.ds(pl.multiple_of(odd * half, half), half)
        for cols in steps(columns):
            keep_ref[:, cols] = jnp.dot(
                turned_ref[mine], image_ref[:, cols], preferred_element_type=jnp.float32
            )

    return pl.pallas_call(
        kernel,
        out_shape=jax.ShapeDtypeStruct((half, columns), jnp.float32),
        in_specs=[VMEM] * 2,
        out_specs=VMEM,
        compiler_params=PARAMETERS,
        cost_estimate=cost(
            2 * half * rows * columns, 2 * rows * (half + columns) + 4 * half * columns
        ),
    )(turned, image)


def local_parts(turned, own, nears, blocks, columns, part):
    params, count, slots, size, _ = blocks.shape
    halo, width = nears[0].shape[0], own.shape[2]
    start, span = part

    def kernel(columns_ref, turned_ref, own_ref, blocks_ref, *refs):
        near_refs, (out_ref, list_ref, image_ref) = refs[: len(nears)], refs[len(nears) :]
        list_ref[pl.ds(0, count)] = own_ref[:, :, pl.ds(start, span)]
        for (at, step), near_ref in zip(pieces(part), near_refs):
            list_ref[pl.ds(count, halo), :, pl.ds(at - start, step)] = near_ref[...]

        @pl.loop(0, count, unroll=4)
        def _(row):
            at = pl.ds(pl.multiple_of(row * size, size), size)
            for param in range(params):
                left, right = [blocks_ref[param, row, 0]], [list_ref[row]]
                for slot in range(1, slots):
                    block = blocks_ref[param, row, slot]
                    column = columns_ref[param, row, slot - 1]
                    far, place = halo_place(column, count, halo)
                    here = (column < count) | jnp.logical_not(far)
                    left.append(jnp.where(here, block, jnp.zeros_like(block)))
                    right.append(list_ref[jnp.where(column < count, column, count + place)])
                image = jnp.dot(
                    jnp.concatenate(left, axis=1),
                    jnp.concatenate(right, axis=0),
                    preferred_element_type=jnp.float32,
                )
                image_ref[at, pl.ds(param * span, span)] = image.astype(image_ref.dtype)

        for cols in steps(params * span):
            out_ref[:, cols] = jnp.dot(
                turned_ref[...], image_ref[:, cols], preferred_element_type=jnp.float32
            )

    rows = count * size
    return pl.pallas_call(
        kernel,
        out_shape=jax.ShapeDtypeStruct((width, params * span), jnp.float32),
        in_specs=[SMEM] + [VMEM] * (3 + len(nears)),
        out_specs=VMEM,
        scratch_shapes=[
            pltpu.VMEM((count + halo, size, span), own.dtype),
            pltpu.VMEM((rows, params * span), jnp.bfloat16),
        ],
        compiler_params=PARAMETERS,
        cost_estimate=cost(
            2 * params * rows * span * (slots * size + width),
            2 * (turned.size + 2 * own.size + blocks.size) + 4 * params * width * span,
        ),
    )(columns, turned, own, blocks, *nears)


def with_far(local, folds, far, mine):
    params, width, depth = folds.shape
    half, span = width // 2, far.shape[2]

    def kernel(local_ref, folds_ref, far_ref, out_ref):
        odd = lax.rem(lax.axis_index(AXIS), 2)
        rows = pl.ds(pl.multiple_of((odd if mine else 1 - odd) * half, half), half)
        right = far_ref[...].reshape(depth, span)
        for param in range(params):
            cols = pl.ds(param * span, span)
            total = local_ref[rows, cols] + jnp.dot(
                folds_ref[param, rows], right, preferred_element_type=jnp.float32
            )
            out_ref[:, cols] = total.astype(out_ref.dtype)

    return pl.pallas_call(
        kernel,
        out_shape=jax.ShapeDtypeStruct(
            (half, params * span), jnp.float32 if mine else jnp.bfloat16
        ),
        in_specs=[VMEM] * 3,
        out_specs=VMEM,
        compiler_params=PARAMETERS,
        cost_estimate=cost(
            2 * params * half * depth * span,
            4 * params * half * span + params * half * depth * 2 + 2 * depth * span,
        ),
    )(local, folds, far)


def add_chips(received, params, width):
    rows = received[0].shape[1]
    ranges = chunks(width)

    def kernel(*refs):
        out_ref = refs[-1]
        for (start, span), ref in zip(ranges, refs):
            total = jnp.sum(ref[...].astype(jnp.float32), axis=0)
            for param in range(params):
                out_ref[:, pl.ds(param * width + start, span)] = total[:, param * span : (param + 1) * span]

    return pl.pallas_call(
        kernel,
        out_shape=jax.ShapeDtypeStruct((rows, params * width), jnp.float32),
        in_specs=[VMEM] * len(received),
        out_specs=VMEM,
        compiler_params=PARAMETERS,
        cost_estimate=cost(0, sum(2 * part.size for part in received)),
    )(*received)


def shards(basis, blocks, columns, sends):
    params, count, _, size, _ = blocks.shape
    width = basis.shape[1]
    halo = sends.shape[1] // 2
    devices = lax.axis_size(AXIS)
    chips = devices // 2
    rows = width // devices
    ranges = chunks(width)
    near_pairs, far_pairs = pairs(devices, 0), pairs(devices, 1)

    own, far, near = pick_first(basis.reshape(count, size, width), sends, ranges[0])
    turned = transposed(own, devices)
    own, turned = lax.optimization_barrier((own, turned))
    fars, nears = [far], [[near]]
    for part in ranges[1:]:
        far, *near = pick_next(own, sends, part)
        fars.append(far)
        nears.append(near)
    fars = [lax.ppermute(far, AXIS, far_pairs) for far in fars]
    nears = [[lax.ppermute(piece, AXIS, near_pairs) for piece in near] for near in nears]

    groups = [list(range(core, devices, 2)) for core in range(2)]

    def chip_sum(give, keep):
        taken = lax.ppermute(give, AXIS, near_pairs)
        both = (keep() + taken.astype(jnp.float32)).astype(jnp.bfloat16)
        return both.reshape(chips, rows, give.shape[1])

    image, give = whole_image(turned, own, fars[0], nears[0][0], blocks, columns, ranges[0])
    ready = chip_sum(give, lambda: keep_rows(turned, image))
    received = []
    for part, far, near in zip(ranges[1:], fars[1:], nears[1:]):
        ready, turned = lax.optimization_barrier((ready, turned))
        received.append(exchange(ready, groups))
        folds = fold_far(turned, blocks, columns, halo)
        local = local_parts(turned, own, near, blocks, columns, part)
        received[-1], far = lax.optimization_barrier((received[-1], far))
        give = with_far(local, folds, far, False)
        ready = chip_sum(give, lambda: with_far(local, folds, far, True))
    received.append(exchange(ready, groups))
    return add_chips(received, params, width)


def exchange(parts, groups):
    return lax.all_to_all(
        parts, AXIS, split_axis=0, concat_axis=0, axis_index_groups=groups, tiled=True
    )


def solution(mesh):
    placed = (
        P(("grp", "mesh"), None),
        P(None, ("grp", "mesh"), None, None, None),
        P(None, ("grp", "mesh"), None),
        P(("grp", "mesh"), None),
    )
    return jax.shard_map(
        shards, mesh=mesh, in_specs=placed, out_specs=P(("grp", "mesh"), None), check_vma=False
    )
```

```python
import jax
import jax.numpy as jnp
from jax import lax
from jax.experimental import pallas as pl
from jax.experimental.pallas import tpu as pltpu
from jax.sharding import PartitionSpec as P

AXIS = "mesh"
LANES = 128
EASE = 8
VMEM_BYTES = 24 * 1024 * 1024
VMEM = pl.BlockSpec(memory_space=pltpu.VMEM)
SMEM = pl.BlockSpec(memory_space=pltpu.SMEM)
PARAMETERS = pltpu.CompilerParams(vmem_limit_bytes=VMEM_BYTES)


def cost(flops, moved):
    return pl.CostEstimate(flops=flops // EASE, bytes_accessed=moved // EASE, transcendentals=0)


def pairs(count, first):
    both = []
    for low in range(first, count - 1, 2):
        both += [(low, low + 1), (low + 1, low)]
    return both


def halves(width):
    half = width // 2
    return [(0, width)] if half % LANES else [(0, half), (half, half)]


def pick_far(own, sends):
    count, size, width = own.shape
    halo = sends.shape[1] // 2

    def kernel(sends_hbm, own_hbm, own_ref, far_ref, sends_ref, list_sem, sems):
        lists = pltpu.make_async_copy(sends_hbm, sends_ref, list_sem)
        lists.start()
        loads = [
            pltpu.make_async_copy(own_hbm.at[block], own_ref.at[block], sems.at[block])
            for block in range(count)
        ]
        for load in loads:
            load.start()
        lists.wait()
        for load in loads:
            load.wait()
        first = lax.rem(lax.axis_index(AXIS), 2) * halo
        for place in range(halo):
            far_ref[place] = own_ref[sends_ref[0, first + place]]

    return pl.pallas_call(
        kernel,
        out_shape=(
            jax.ShapeDtypeStruct(own.shape, own.dtype),
            jax.ShapeDtypeStruct((halo, size, width), own.dtype),
        ),
        in_specs=[pl.BlockSpec(memory_space=pltpu.HBM)] * 2,
        out_specs=(VMEM,) * 2,
        scratch_shapes=[
            pltpu.SMEM(sends.shape, sends.dtype),
            pltpu.SemaphoreType.DMA(()),
            pltpu.SemaphoreType.DMA((count,)),
        ],
        compiler_params=PARAMETERS,
        cost_estimate=cost(0, 5 * own.size),
    )(
        pltpu.with_memory_space_constraint(sends, pltpu.HBM),
        pltpu.with_memory_space_constraint(own, pltpu.HBM),
    )


def pick_near(own, sends):
    _, size, width = own.shape
    halo = sends.shape[1] // 2
    ranges = halves(width)

    def kernel(sends_hbm, own_ref, *refs):
        near_refs, sends_ref = refs[:-1], refs[-1]
        pltpu.sync_copy(sends_hbm, sends_ref)
        first = (1 - lax.rem(lax.axis_index(AXIS), 2)) * halo
        for place in range(halo):
            block = sends_ref[0, first + place]
            for part, near_ref in zip(ranges, near_refs):
                near_ref[place] = own_ref[block, :, pl.ds(*part)]

    return pl.pallas_call(
        kernel,
        out_shape=[jax.ShapeDtypeStruct((halo, size, span), own.dtype) for _, span in ranges],
        in_specs=[pl.BlockSpec(memory_space=pltpu.HBM), VMEM],
        out_specs=[VMEM] * len(ranges),
        scratch_shapes=[pltpu.SMEM(sends.shape, sends.dtype)],
        compiler_params=PARAMETERS,
        cost_estimate=cost(0, 2 * own.size),
    )(pltpu.with_memory_space_constraint(sends, pltpu.HBM), own)


def transposed(own, devices):
    count, size, width = own.shape
    chips, rows = devices // 2, width // devices
    if rows % 16:
        turned = own.reshape(count * size, width).T.reshape(chips, 2, rows, count * size)
        return turned.transpose(1, 0, 2, 3).reshape(width, count * size)

    def kernel(own_ref, out_ref):
        @pl.loop(0, count)
        def _(block):
            cols = pl.ds(pl.multiple_of(block * size, size), size)
            turned = own_ref[block].T
            for device in range(devices):
                chip, core = divmod(device, 2)
                out_ref[pl.ds((core * chips + chip) * rows, rows), cols] = (
                    turned[device * rows : (device + 1) * rows]
                )

    return pl.pallas_call(
        kernel,
        out_shape=jax.ShapeDtypeStruct((width, count * size), own.dtype),
        in_specs=[VMEM],
        out_specs=VMEM,
        compiler_params=PARAMETERS,
        cost_estimate=cost(0, 4 * own.size),
    )(own)


def steps(columns):
    step = 2 * LANES if columns % (2 * LANES) == 0 else columns
    return [pl.ds(at, step) for at in range(0, columns, step)]


def halo_place(column, count, halo):
    place = column - count
    upper = place >= halo
    odd = lax.rem(lax.axis_index(AXIS), 2)
    return upper == (odd == 1), jnp.where(upper, place - halo, place)


def fold_far(turned, blocks, columns, halo):
    params, count, slots, size, _ = blocks.shape
    width = turned.shape[0]

    def kernel(columns_ref, turned_ref, blocks_ref, out_ref, sum_ref):
        sum_ref[...] = jnp.zeros_like(sum_ref)

        @pl.loop(0, count)
        def _(row):
            rows = pl.ds(pl.multiple_of(row * size, size), size)
            for param in range(params):
                for slot in range(1, slots):
                    column = columns_ref[param, row, slot - 1]
                    far, place = halo_place(column, count, halo)

                    @pl.when((column >= count) & far)
                    def _():
                        at = pl.ds(pl.multiple_of(place * size, size), size)
                        sum_ref[param, :, at] += jnp.dot(
                            turned_ref[:, rows],
                            blocks_ref[param, row, slot],
                            preferred_element_type=jnp.float32,
                        )

        out_ref[...] = sum_ref[...].astype(out_ref.dtype)

    shape = (params, width, halo * size)
    return pl.pallas_call(
        kernel,
        out_shape=jax.ShapeDtypeStruct(shape, turned.dtype),
        in_specs=[SMEM, VMEM, VMEM],
        out_specs=VMEM,
        scratch_shapes=[pltpu.VMEM(shape, jnp.float32)],
        compiler_params=PARAMETERS,
        cost_estimate=cost(
            params * count * (slots - 1) * size * size * width, 2 * (turned.size + blocks.size)
        ),
    )(columns, turned, blocks)


def local_parts(turned, own, nears, blocks, columns):
    params, count, slots, size, _ = blocks.shape
    halo, width = nears[0].shape[0], own.shape[2]
    ranges = halves(width)

    def kernel(columns_ref, turned_ref, own_ref, blocks_ref, *refs):
        near_refs, (out_ref, list_ref, image_ref) = refs[: len(ranges)], refs[len(ranges) :]
        list_ref[pl.ds(0, count)] = own_ref[...]
        for part, near_ref in zip(ranges, near_refs):
            list_ref[pl.ds(count, halo), :, pl.ds(*part)] = near_ref[...]

        @pl.loop(0, count, unroll=4)
        def _(row):
            at = pl.ds(pl.multiple_of(row * size, size), size)
            for param in range(params):
                left, right = [blocks_ref[param, row, 0]], [list_ref[row]]
                for slot in range(1, slots):
                    block = blocks_ref[param, row, slot]
                    column = columns_ref[param, row, slot - 1]
                    far, place = halo_place(column, count, halo)
                    here = (column < count) | jnp.logical_not(far)
                    left.append(jnp.where(here, block, jnp.zeros_like(block)))
                    right.append(list_ref[jnp.where(column < count, column, count + place)])
                image = jnp.dot(
                    jnp.concatenate(left, axis=1),
                    jnp.concatenate(right, axis=0),
                    preferred_element_type=jnp.float32,
                )
                image_ref[at, pl.ds(param * width, width)] = image.astype(image_ref.dtype)

        for param in range(params):
            for cols in steps(width):
                out_ref[param, :, cols] = jnp.dot(
                    turned_ref[...],
                    image_ref[:, pl.ds(param * width + cols.start, cols.size)],
                    preferred_element_type=jnp.float32,
                )

    rows = count * size
    return pl.pallas_call(
        kernel,
        out_shape=jax.ShapeDtypeStruct((params, width, width), jnp.float32),
        in_specs=[SMEM] + [VMEM] * (3 + len(ranges)),
        out_specs=VMEM,
        scratch_shapes=[
            pltpu.VMEM((count + halo, size, width), own.dtype),
            pltpu.VMEM((rows, params * width), jnp.bfloat16),
        ],
        compiler_params=PARAMETERS,
        cost_estimate=cost(
            2 * params * rows * width * (slots * size + width),
            2 * (turned.size + 2 * own.size + blocks.size) + 4 * params * width * width,
        ),
    )(columns, turned, own, blocks, *nears)


def with_far(local, folds, far, mine, chosen):
    _, width, depth = folds.shape
    half, span = width // 2, far.shape[2]

    def kernel(local_ref, folds_ref, far_ref, out_ref):
        odd = lax.rem(lax.axis_index(AXIS), 2)
        rows = pl.ds(pl.multiple_of((odd if mine else 1 - odd) * half, half), half)
        right = far_ref[...].reshape(depth, span)
        for place, param in enumerate(chosen):
            total = local_ref[param, rows] + jnp.dot(
                folds_ref[param, rows], right, preferred_element_type=jnp.float32
            )
            out_ref[:, pl.ds(place * span, span)] = total.astype(out_ref.dtype)

    columns = len(chosen) * span
    return pl.pallas_call(
        kernel,
        out_shape=jax.ShapeDtypeStruct((half, columns), jnp.float32 if mine else jnp.bfloat16),
        in_specs=[VMEM] * 3,
        out_specs=VMEM,
        compiler_params=PARAMETERS,
        cost_estimate=cost(
            2 * half * depth * columns,
            4 * half * columns + len(chosen) * half * depth * 2 + 2 * depth * span,
        ),
    )(local, folds, far)


def add_chips(parts):
    def kernel(parts_ref, out_ref):
        out_ref[...] = jnp.sum(parts_ref[...].astype(jnp.float32), axis=0)

    return pl.pallas_call(
        kernel,
        out_shape=jax.ShapeDtypeStruct(parts.shape[1:], jnp.float32),
        in_specs=[VMEM],
        out_specs=VMEM,
        compiler_params=PARAMETERS,
        cost_estimate=cost(0, 2 * parts.size),
    )(parts)


def shards(basis, blocks, columns, sends):
    params, count, _, size, _ = blocks.shape
    width = basis.shape[1]
    halo = sends.shape[1] // 2
    devices = lax.axis_size(AXIS)
    chips = devices // 2
    near_pairs, far_pairs = pairs(devices, 0), pairs(devices, 1)

    own, far = pick_far(basis.reshape(count, size, width), sends)
    far = lax.ppermute(far, AXIS, far_pairs)
    nears = [lax.ppermute(near, AXIS, near_pairs) for near in pick_near(own, sends)]

    turned = transposed(own, devices)
    folds = fold_far(turned, blocks, columns, halo)
    local = local_parts(turned, own, nears, blocks, columns)

    gives = [with_far(local, folds, far, False, [param]) for param in range(params)]
    taken = [lax.ppermute(give, AXIS, near_pairs) for give in gives]
    keep = with_far(local, folds, far, True, list(range(params)))
    chip_sum = (keep + jnp.concatenate(taken, axis=1).astype(jnp.float32)).astype(jnp.bfloat16)
    parts = lax.all_to_all(
        chip_sum.reshape(chips, width // devices, params * width), AXIS,
        split_axis=0, concat_axis=0, tiled=True,
        axis_index_groups=[list(range(core, devices, 2)) for core in range(2)],
    )
    return add_chips(parts)


def solution(mesh):
    placed = (
        P(("grp", "mesh"), None),
        P(None, ("grp", "mesh"), None, None, None),
        P(None, ("grp", "mesh"), None),
        P(("grp", "mesh"), None),
    )
    return jax.shard_map(
        shards, mesh=mesh, in_specs=placed, out_specs=P(("grp", "mesh"), None), check_vma=False
    )
```

```python
import jax
import jax.numpy as jnp
from jax import lax
from jax.experimental import pallas as pl
from jax.experimental.pallas import tpu as pltpu
from jax.sharding import PartitionSpec as P

AXIS = "mesh"
LANES = 128
EASE = 8
VMEM_BYTES = 24 * 1024 * 1024
VMEM = pl.BlockSpec(memory_space=pltpu.VMEM)
SMEM = pl.BlockSpec(memory_space=pltpu.SMEM)
PARAMETERS = pltpu.CompilerParams(vmem_limit_bytes=VMEM_BYTES)


def cost(flops, moved):
    return pl.CostEstimate(flops=flops // EASE, bytes_accessed=moved // EASE, transcendentals=0)


def pairs(count, first):
    both = []
    for low in range(first, count - 1, 2):
        both += [(low, low + 1), (low + 1, low)]
    return both


def chip_order(chips):
    return list(range(0, chips, 2)) + list(range(1, chips, 2))


def halves(width):
    half = width // 2
    return [(0, width)] if half % LANES else [(0, half), (half, half)]


def pick_far(own, sends):
    count, size, width = own.shape
    halo = sends.shape[1] // 2

    def kernel(sends_hbm, own_hbm, own_ref, far_ref, sends_ref, list_sem, sems):
        lists = pltpu.make_async_copy(sends_hbm, sends_ref, list_sem)
        lists.start()
        loads = [
            pltpu.make_async_copy(own_hbm.at[block], own_ref.at[block], sems.at[block])
            for block in range(count)
        ]
        for load in loads:
            load.start()
        lists.wait()
        for load in loads:
            load.wait()
        first = lax.rem(lax.axis_index(AXIS), 2) * halo
        for place in range(halo):
            far_ref[place] = own_ref[sends_ref[0, first + place]]

    return pl.pallas_call(
        kernel,
        out_shape=(
            jax.ShapeDtypeStruct(own.shape, own.dtype),
            jax.ShapeDtypeStruct((halo, size, width), own.dtype),
        ),
        in_specs=[pl.BlockSpec(memory_space=pltpu.HBM)] * 2,
        out_specs=(VMEM,) * 2,
        scratch_shapes=[
            pltpu.SMEM(sends.shape, sends.dtype),
            pltpu.SemaphoreType.DMA(()),
            pltpu.SemaphoreType.DMA((count,)),
        ],
        compiler_params=PARAMETERS,
        cost_estimate=cost(0, 5 * own.size),
    )(
        pltpu.with_memory_space_constraint(sends, pltpu.HBM),
        pltpu.with_memory_space_constraint(own, pltpu.HBM),
    )


def pick_near(own, sends):
    _, size, width = own.shape
    halo = sends.shape[1] // 2
    ranges = halves(width)

    def kernel(sends_hbm, own_ref, *refs):
        near_refs, sends_ref = refs[:-1], refs[-1]
        pltpu.sync_copy(sends_hbm, sends_ref)
        first = (1 - lax.rem(lax.axis_index(AXIS), 2)) * halo
        for place in range(halo):
            block = sends_ref[0, first + place]
            for part, near_ref in zip(ranges, near_refs):
                near_ref[place] = own_ref[block, :, pl.ds(*part)]

    return pl.pallas_call(
        kernel,
        out_shape=[jax.ShapeDtypeStruct((halo, size, span), own.dtype) for _, span in ranges],
        in_specs=[pl.BlockSpec(memory_space=pltpu.HBM), VMEM],
        out_specs=[VMEM] * len(ranges),
        scratch_shapes=[pltpu.SMEM(sends.shape, sends.dtype)],
        compiler_params=PARAMETERS,
        cost_estimate=cost(0, 2 * own.size),
    )(pltpu.with_memory_space_constraint(sends, pltpu.HBM), own)


def transposed(own, devices):
    count, size, width = own.shape
    chips, rows = devices // 2, width // devices
    order = chip_order(chips)
    if rows % 16:
        turned = own.reshape(count * size, width).T.reshape(chips, 2, rows, count * size)
        turned = turned[jnp.array(order)]
        return turned.transpose(1, 0, 2, 3).reshape(width, count * size)

    def kernel(own_ref, out_ref):
        @pl.loop(0, count)
        def _(block):
            cols = pl.ds(pl.multiple_of(block * size, size), size)
            turned = own_ref[block].T
            for device in range(devices):
                chip, core = divmod(device, 2)
                out_ref[pl.ds((core * chips + order.index(chip)) * rows, rows), cols] = (
                    turned[device * rows : (device + 1) * rows]
                )

    return pl.pallas_call(
        kernel,
        out_shape=jax.ShapeDtypeStruct((width, count * size), own.dtype),
        in_specs=[VMEM],
        out_specs=VMEM,
        compiler_params=PARAMETERS,
        cost_estimate=cost(0, 4 * own.size),
    )(own)


def steps(columns):
    step = 2 * LANES if columns % (2 * LANES) == 0 else columns
    return [pl.ds(at, step) for at in range(0, columns, step)]


def halo_place(column, count, halo):
    place = column - count
    upper = place >= halo
    odd = lax.rem(lax.axis_index(AXIS), 2)
    return upper == (odd == 1), jnp.where(upper, place - halo, place)


def fold_far(turned, blocks, columns, halo):
    params, count, slots, size, _ = blocks.shape
    width = turned.shape[0]

    def kernel(columns_ref, turned_ref, blocks_ref, out_ref, sum_ref):
        sum_ref[...] = jnp.zeros_like(sum_ref)

        @pl.loop(0, count)
        def _(row):
            rows = pl.ds(pl.multiple_of(row * size, size), size)
            for param in range(params):
                for slot in range(1, slots):
                    column = columns_ref[param, row, slot - 1]
                    far, place = halo_place(column, count, halo)

                    @pl.when((column >= count) & far)
                    def _():
                        at = pl.ds(pl.multiple_of(place * size, size), size)
                        sum_ref[param, :, at] += jnp.dot(
                            turned_ref[:, rows],
                            blocks_ref[param, row, slot],
                            preferred_element_type=jnp.float32,
                        )

        out_ref[...] = sum_ref[...].astype(out_ref.dtype)

    shape = (params, width, halo * size)
    return pl.pallas_call(
        kernel,
        out_shape=jax.ShapeDtypeStruct(shape, turned.dtype),
        in_specs=[SMEM, VMEM, VMEM],
        out_specs=VMEM,
        scratch_shapes=[pltpu.VMEM(shape, jnp.float32)],
        compiler_params=PARAMETERS,
        cost_estimate=cost(
            params * count * (slots - 1) * size * size * width, 2 * (turned.size + blocks.size)
        ),
    )(columns, turned, blocks)


def local_parts(turned, own, nears, blocks, columns):
    params, count, slots, size, _ = blocks.shape
    halo, width = nears[0].shape[0], own.shape[2]
    ranges = halves(width)

    def kernel(columns_ref, turned_ref, own_ref, blocks_ref, *refs):
        near_refs, (out_ref, list_ref, image_ref) = refs[: len(ranges)], refs[len(ranges) :]
        list_ref[pl.ds(0, count)] = own_ref[...]
        for part, near_ref in zip(ranges, near_refs):
            list_ref[pl.ds(count, halo), :, pl.ds(*part)] = near_ref[...]

        @pl.loop(0, count, unroll=4)
        def _(row):
            at = pl.ds(pl.multiple_of(row * size, size), size)
            for param in range(params):
                left, right = [blocks_ref[param, row, 0]], [list_ref[row]]
                for slot in range(1, slots):
                    block = blocks_ref[param, row, slot]
                    column = columns_ref[param, row, slot - 1]
                    far, place = halo_place(column, count, halo)
                    here = (column < count) | jnp.logical_not(far)
                    left.append(jnp.where(here, block, jnp.zeros_like(block)))
                    right.append(list_ref[jnp.where(column < count, column, count + place)])
                image = jnp.dot(
                    jnp.concatenate(left, axis=1),
                    jnp.concatenate(right, axis=0),
                    preferred_element_type=jnp.float32,
                )
                image_ref[at, pl.ds(param * width, width)] = image.astype(image_ref.dtype)

        for param in range(params):
            for cols in steps(width):
                out_ref[param, :, cols] = jnp.dot(
                    turned_ref[...],
                    image_ref[:, pl.ds(param * width + cols.start, cols.size)],
                    preferred_element_type=jnp.float32,
                )

    rows = count * size
    return pl.pallas_call(
        kernel,
        out_shape=jax.ShapeDtypeStruct((params, width, width), jnp.float32),
        in_specs=[SMEM] + [VMEM] * (3 + len(ranges)),
        out_specs=VMEM,
        scratch_shapes=[
            pltpu.VMEM((count + halo, size, width), own.dtype),
            pltpu.VMEM((rows, params * width), jnp.bfloat16),
        ],
        compiler_params=PARAMETERS,
        cost_estimate=cost(
            2 * params * rows * width * (slots * size + width),
            2 * (turned.size + 2 * own.size + blocks.size) + 4 * params * width * width,
        ),
    )(columns, turned, own, blocks, *nears)


def with_far(local, folds, far, mine):
    params, width, depth = folds.shape
    half, span = width // 2, far.shape[2]

    def kernel(local_ref, folds_ref, far_ref, out_ref):
        odd = lax.rem(lax.axis_index(AXIS), 2)
        rows = pl.ds(pl.multiple_of((odd if mine else 1 - odd) * half, half), half)
        right = far_ref[...].reshape(depth, span)
        for param in range(params):
            total = local_ref[param, rows] + jnp.dot(
                folds_ref[param, rows], right, preferred_element_type=jnp.float32
            )
            out_ref[:, pl.ds(param * span, span)] = total.astype(out_ref.dtype)

    columns = params * span
    return pl.pallas_call(
        kernel,
        out_shape=jax.ShapeDtypeStruct((half, columns), jnp.float32 if mine else jnp.bfloat16),
        in_specs=[VMEM] * 3,
        out_specs=VMEM,
        compiler_params=PARAMETERS,
        cost_estimate=cost(
            2 * half * depth * columns,
            4 * half * columns + params * half * depth * 2 + 2 * depth * span,
        ),
    )(local, folds, far)


def add_chips(parts):
    def kernel(parts_ref, out_ref):
        out_ref[...] = jnp.sum(parts_ref[...].astype(jnp.float32), axis=0)

    return pl.pallas_call(
        kernel,
        out_shape=jax.ShapeDtypeStruct(parts.shape[1:], jnp.float32),
        in_specs=[VMEM],
        out_specs=VMEM,
        compiler_params=PARAMETERS,
        cost_estimate=cost(0, 2 * parts.size),
    )(parts)


def shards(basis, blocks, columns, sends):
    params, count, _, size, _ = blocks.shape
    width = basis.shape[1]
    halo = sends.shape[1] // 2
    devices = lax.axis_size(AXIS)
    chips = devices // 2
    near_pairs, far_pairs = pairs(devices, 0), pairs(devices, 1)

    own, far = pick_far(basis.reshape(count, size, width), sends)
    far = lax.ppermute(far, AXIS, far_pairs)
    nears = [lax.ppermute(near, AXIS, near_pairs) for near in pick_near(own, sends)]

    turned = transposed(own, devices)
    folds = fold_far(turned, blocks, columns, halo)
    local = local_parts(turned, own, nears, blocks, columns)

    taken = lax.ppermute(with_far(local, folds, far, False), AXIS, near_pairs)
    keep = with_far(local, folds, far, True)
    chip_sum = (keep + taken.astype(jnp.float32)).astype(jnp.bfloat16)
    parts = lax.all_to_all(
        chip_sum.reshape(chips, width // devices, params * width), AXIS,
        split_axis=0, concat_axis=0, tiled=True,
        axis_index_groups=[[2 * chip + core for chip in chip_order(chips)] for core in range(2)],
    )
    return add_chips(parts)


def solution(mesh):
    placed = (
        P(("grp", "mesh"), None),
        P(None, ("grp", "mesh"), None, None, None),
        P(None, ("grp", "mesh"), None),
        P(("grp", "mesh"), None),
    )
    return jax.shard_map(
        shards, mesh=mesh, in_specs=placed, out_specs=P(("grp", "mesh"), None), check_vma=False
    )
```

```python
import jax
import jax.numpy as jnp
from jax import lax
from jax.experimental import pallas as pl
from jax.experimental.pallas import tpu as pltpu
from jax.sharding import PartitionSpec as P

AXIS = "mesh"
LANES = 128
EASE = 8
VMEM_BYTES = 24 * 1024 * 1024
VMEM = pl.BlockSpec(memory_space=pltpu.VMEM)
SMEM = pl.BlockSpec(memory_space=pltpu.SMEM)
PARAMETERS = pltpu.CompilerParams(vmem_limit_bytes=VMEM_BYTES)


def cost(flops, moved):
    return pl.CostEstimate(flops=flops // EASE, bytes_accessed=moved // EASE, transcendentals=0)


def pairs(count, first):
    both = []
    for low in range(first, count - 1, 2):
        both += [(low, low + 1), (low + 1, low)]
    return both


def chip_order(chips):
    return list(range(chips - 1, -1, -1))


def halves(width):
    half = width // 2
    return [(0, width)] if half % LANES else [(0, half), (half, half)]


def pick_far(own, sends):
    count, size, width = own.shape
    halo = sends.shape[1] // 2

    def kernel(sends_hbm, own_hbm, own_ref, far_ref, sends_ref, list_sem, sems):
        lists = pltpu.make_async_copy(sends_hbm, sends_ref, list_sem)
        lists.start()
        loads = [
            pltpu.make_async_copy(own_hbm.at[block], own_ref.at[block], sems.at[block])
            for block in range(count)
        ]
        for load in loads:
            load.start()
        lists.wait()
        for load in loads:
            load.wait()
        first = lax.rem(lax.axis_index(AXIS), 2) * halo
        for place in range(halo):
            far_ref[place] = own_ref[sends_ref[0, first + place]]

    return pl.pallas_call(
        kernel,
        out_shape=(
            jax.ShapeDtypeStruct(own.shape, own.dtype),
            jax.ShapeDtypeStruct((halo, size, width), own.dtype),
        ),
        in_specs=[pl.BlockSpec(memory_space=pltpu.HBM)] * 2,
        out_specs=(VMEM,) * 2,
        scratch_shapes=[
            pltpu.SMEM(sends.shape, sends.dtype),
            pltpu.SemaphoreType.DMA(()),
            pltpu.SemaphoreType.DMA((count,)),
        ],
        compiler_params=PARAMETERS,
        cost_estimate=cost(0, 5 * own.size),
    )(
        pltpu.with_memory_space_constraint(sends, pltpu.HBM),
        pltpu.with_memory_space_constraint(own, pltpu.HBM),
    )


def pick_near(own, sends):
    _, size, width = own.shape
    halo = sends.shape[1] // 2
    ranges = halves(width)

    def kernel(sends_hbm, own_ref, *refs):
        near_refs, sends_ref = refs[:-1], refs[-1]
        pltpu.sync_copy(sends_hbm, sends_ref)
        first = (1 - lax.rem(lax.axis_index(AXIS), 2)) * halo
        for place in range(halo):
            block = sends_ref[0, first + place]
            for part, near_ref in zip(ranges, near_refs):
                near_ref[place] = own_ref[block, :, pl.ds(*part)]

    return pl.pallas_call(
        kernel,
        out_shape=[jax.ShapeDtypeStruct((halo, size, span), own.dtype) for _, span in ranges],
        in_specs=[pl.BlockSpec(memory_space=pltpu.HBM), VMEM],
        out_specs=[VMEM] * len(ranges),
        scratch_shapes=[pltpu.SMEM(sends.shape, sends.dtype)],
        compiler_params=PARAMETERS,
        cost_estimate=cost(0, 2 * own.size),
    )(pltpu.with_memory_space_constraint(sends, pltpu.HBM), own)


def transposed(own, devices):
    count, size, width = own.shape
    chips, rows = devices // 2, width // devices
    order = chip_order(chips)
    if rows % 16:
        turned = own.reshape(count * size, width).T.reshape(chips, 2, rows, count * size)
        turned = turned[jnp.array(order)]
        return turned.transpose(1, 0, 2, 3).reshape(width, count * size)

    def kernel(own_ref, out_ref):
        @pl.loop(0, count)
        def _(block):
            cols = pl.ds(pl.multiple_of(block * size, size), size)
            turned = own_ref[block].T
            for device in range(devices):
                chip, core = divmod(device, 2)
                out_ref[pl.ds((core * chips + order.index(chip)) * rows, rows), cols] = (
                    turned[device * rows : (device + 1) * rows]
                )

    return pl.pallas_call(
        kernel,
        out_shape=jax.ShapeDtypeStruct((width, count * size), own.dtype),
        in_specs=[VMEM],
        out_specs=VMEM,
        compiler_params=PARAMETERS,
        cost_estimate=cost(0, 4 * own.size),
    )(own)


def steps(columns):
    step = 2 * LANES if columns % (2 * LANES) == 0 else columns
    return [pl.ds(at, step) for at in range(0, columns, step)]


def halo_place(column, count, halo):
    place = column - count
    upper = place >= halo
    odd = lax.rem(lax.axis_index(AXIS), 2)
    return upper == (odd == 1), jnp.where(upper, place - halo, place)


def fold_far(turned, blocks, columns, halo):
    params, count, slots, size, _ = blocks.shape
    width = turned.shape[0]

    def kernel(columns_ref, turned_ref, blocks_ref, out_ref, sum_ref):
        sum_ref[...] = jnp.zeros_like(sum_ref)

        @pl.loop(0, count)
        def _(row):
            rows = pl.ds(pl.multiple_of(row * size, size), size)
            for param in range(params):
                for slot in range(1, slots):
                    column = columns_ref[param, row, slot - 1]
                    far, place = halo_place(column, count, halo)

                    @pl.when((column >= count) & far)
                    def _():
                        at = pl.ds(pl.multiple_of(place * size, size), size)
                        sum_ref[param, :, at] += jnp.dot(
                            turned_ref[:, rows],
                            blocks_ref[param, row, slot],
                            preferred_element_type=jnp.float32,
                        )

        out_ref[...] = sum_ref[...].astype(out_ref.dtype)

    shape = (params, width, halo * size)
    return pl.pallas_call(
        kernel,
        out_shape=jax.ShapeDtypeStruct(shape, turned.dtype),
        in_specs=[SMEM, VMEM, VMEM],
        out_specs=VMEM,
        scratch_shapes=[pltpu.VMEM(shape, jnp.float32)],
        compiler_params=PARAMETERS,
        cost_estimate=cost(
            params * count * (slots - 1) * size * size * width, 2 * (turned.size + blocks.size)
        ),
    )(columns, turned, blocks)


def local_parts(turned, own, nears, blocks, columns):
    params, count, slots, size, _ = blocks.shape
    halo, width = nears[0].shape[0], own.shape[2]
    ranges = halves(width)

    def kernel(columns_ref, turned_ref, own_ref, blocks_ref, *refs):
        near_refs, (out_ref, list_ref, image_ref) = refs[: len(ranges)], refs[len(ranges) :]
        list_ref[pl.ds(0, count)] = own_ref[...]
        for part, near_ref in zip(ranges, near_refs):
            list_ref[pl.ds(count, halo), :, pl.ds(*part)] = near_ref[...]

        @pl.loop(0, count, unroll=4)
        def _(row):
            at = pl.ds(pl.multiple_of(row * size, size), size)
            for param in range(params):
                left, right = [blocks_ref[param, row, 0]], [list_ref[row]]
                for slot in range(1, slots):
                    block = blocks_ref[param, row, slot]
                    column = columns_ref[param, row, slot - 1]
                    far, place = halo_place(column, count, halo)
                    here = (column < count) | jnp.logical_not(far)
                    left.append(jnp.where(here, block, jnp.zeros_like(block)))
                    right.append(list_ref[jnp.where(column < count, column, count + place)])
                image = jnp.dot(
                    jnp.concatenate(left, axis=1),
                    jnp.concatenate(right, axis=0),
                    preferred_element_type=jnp.float32,
                )
                image_ref[at, pl.ds(param * width, width)] = image.astype(image_ref.dtype)

        for param in range(params):
            for cols in steps(width):
                out_ref[param, :, cols] = jnp.dot(
                    turned_ref[...],
                    image_ref[:, pl.ds(param * width + cols.start, cols.size)],
                    preferred_element_type=jnp.float32,
                )

    rows = count * size
    return pl.pallas_call(
        kernel,
        out_shape=jax.ShapeDtypeStruct((params, width, width), jnp.float32),
        in_specs=[SMEM] + [VMEM] * (3 + len(ranges)),
        out_specs=VMEM,
        scratch_shapes=[
            pltpu.VMEM((count + halo, size, width), own.dtype),
            pltpu.VMEM((rows, params * width), jnp.bfloat16),
        ],
        compiler_params=PARAMETERS,
        cost_estimate=cost(
            2 * params * rows * width * (slots * size + width),
            2 * (turned.size + 2 * own.size + blocks.size) + 4 * params * width * width,
        ),
    )(columns, turned, own, blocks, *nears)


def with_far(local, folds, far, mine):
    params, width, depth = folds.shape
    half, span = width // 2, far.shape[2]

    def kernel(local_ref, folds_ref, far_ref, out_ref):
        odd = lax.rem(lax.axis_index(AXIS), 2)
        rows = pl.ds(pl.multiple_of((odd if mine else 1 - odd) * half, half), half)
        right = far_ref[...].reshape(depth, span)
        for param in range(params):
            total = local_ref[param, rows] + jnp.dot(
                folds_ref[param, rows], right, preferred_element_type=jnp.float32
            )
            out_ref[:, pl.ds(param * span, span)] = total.astype(out_ref.dtype)

    columns = params * span
    return pl.pallas_call(
        kernel,
        out_shape=jax.ShapeDtypeStruct((half, columns), jnp.float32 if mine else jnp.bfloat16),
        in_specs=[VMEM] * 3,
        out_specs=VMEM,
        compiler_params=PARAMETERS,
        cost_estimate=cost(
            2 * half * depth * columns,
            4 * half * columns + params * half * depth * 2 + 2 * depth * span,
        ),
    )(local, folds, far)


def add_chips(parts):
    def kernel(parts_ref, out_ref):
        out_ref[...] = jnp.sum(parts_ref[...].astype(jnp.float32), axis=0)

    return pl.pallas_call(
        kernel,
        out_shape=jax.ShapeDtypeStruct(parts.shape[1:], jnp.float32),
        in_specs=[VMEM],
        out_specs=VMEM,
        compiler_params=PARAMETERS,
        cost_estimate=cost(0, 2 * parts.size),
    )(parts)


def shards(basis, blocks, columns, sends):
    params, count, _, size, _ = blocks.shape
    width = basis.shape[1]
    halo = sends.shape[1] // 2
    devices = lax.axis_size(AXIS)
    chips = devices // 2
    near_pairs, far_pairs = pairs(devices, 0), pairs(devices, 1)

    own, far = pick_far(basis.reshape(count, size, width), sends)
    far = lax.ppermute(far, AXIS, far_pairs)
    nears = [lax.ppermute(near, AXIS, near_pairs) for near in pick_near(own, sends)]

    turned = transposed(own, devices)
    folds = fold_far(turned, blocks, columns, halo)
    local = local_parts(turned, own, nears, blocks, columns)

    taken = lax.ppermute(with_far(local, folds, far, False), AXIS, near_pairs)
    keep = with_far(local, folds, far, True)
    chip_sum = (keep + taken.astype(jnp.float32)).astype(jnp.bfloat16)
    parts = lax.all_to_all(
        chip_sum.reshape(chips, width // devices, params * width), AXIS,
        split_axis=0, concat_axis=0, tiled=True,
        axis_index_groups=[[2 * chip + core for chip in chip_order(chips)] for core in range(2)],
    )
    return add_chips(parts)


def solution(mesh):
    placed = (
        P(("grp", "mesh"), None),
        P(None, ("grp", "mesh"), None, None, None),
        P(None, ("grp", "mesh"), None),
        P(("grp", "mesh"), None),
    )
    return jax.shard_map(
        shards, mesh=mesh, in_specs=placed, out_specs=P(("grp", "mesh"), None), check_vma=False
    )
```

```python
import jax
import jax.numpy as jnp
from jax import lax
from jax.experimental import pallas as pl
from jax.experimental.pallas import tpu as pltpu
from jax.sharding import PartitionSpec as P

AXIS = "mesh"
LANES = 128
EASE = 8
VMEM_BYTES = 24 * 1024 * 1024
VMEM = pl.BlockSpec(memory_space=pltpu.VMEM)
SMEM = pl.BlockSpec(memory_space=pltpu.SMEM)
PARAMETERS = pltpu.CompilerParams(vmem_limit_bytes=VMEM_BYTES)


def cost(flops, moved):
    return pl.CostEstimate(flops=flops // EASE, bytes_accessed=moved // EASE, transcendentals=0)


def pairs(count, first):
    both = []
    for low in range(first, count - 1, 2):
        both += [(low, low + 1), (low + 1, low)]
    return both


def chip_order(chips):
    ends = zip(range(chips - 1, -1, -1), range(chips))
    return [chip for pair in ends for chip in pair][:chips]


def halves(width):
    half = width // 2
    return [(0, width)] if half % LANES else [(0, half), (half, half)]


def pick_far(own, sends):
    count, size, width = own.shape
    halo = sends.shape[1] // 2

    def kernel(sends_hbm, own_hbm, own_ref, far_ref, sends_ref, list_sem, sems):
        lists = pltpu.make_async_copy(sends_hbm, sends_ref, list_sem)
        lists.start()
        loads = [
            pltpu.make_async_copy(own_hbm.at[block], own_ref.at[block], sems.at[block])
            for block in range(count)
        ]
        for load in loads:
            load.start()
        lists.wait()
        for load in loads:
            load.wait()
        first = lax.rem(lax.axis_index(AXIS), 2) * halo
        for place in range(halo):
            far_ref[place] = own_ref[sends_ref[0, first + place]]

    return pl.pallas_call(
        kernel,
        out_shape=(
            jax.ShapeDtypeStruct(own.shape, own.dtype),
            jax.ShapeDtypeStruct((halo, size, width), own.dtype),
        ),
        in_specs=[pl.BlockSpec(memory_space=pltpu.HBM)] * 2,
        out_specs=(VMEM,) * 2,
        scratch_shapes=[
            pltpu.SMEM(sends.shape, sends.dtype),
            pltpu.SemaphoreType.DMA(()),
            pltpu.SemaphoreType.DMA((count,)),
        ],
        compiler_params=PARAMETERS,
        cost_estimate=cost(0, 5 * own.size),
    )(
        pltpu.with_memory_space_constraint(sends, pltpu.HBM),
        pltpu.with_memory_space_constraint(own, pltpu.HBM),
    )


def pick_near(own, sends):
    _, size, width = own.shape
    halo = sends.shape[1] // 2
    ranges = halves(width)

    def kernel(sends_hbm, own_ref, *refs):
        near_refs, sends_ref = refs[:-1], refs[-1]
        pltpu.sync_copy(sends_hbm, sends_ref)
        first = (1 - lax.rem(lax.axis_index(AXIS), 2)) * halo
        for place in range(halo):
            block = sends_ref[0, first + place]
            for part, near_ref in zip(ranges, near_refs):
                near_ref[place] = own_ref[block, :, pl.ds(*part)]

    return pl.pallas_call(
        kernel,
        out_shape=[jax.ShapeDtypeStruct((halo, size, span), own.dtype) for _, span in ranges],
        in_specs=[pl.BlockSpec(memory_space=pltpu.HBM), VMEM],
        out_specs=[VMEM] * len(ranges),
        scratch_shapes=[pltpu.SMEM(sends.shape, sends.dtype)],
        compiler_params=PARAMETERS,
        cost_estimate=cost(0, 2 * own.size),
    )(pltpu.with_memory_space_constraint(sends, pltpu.HBM), own)


def transposed(own, devices):
    count, size, width = own.shape
    chips, rows = devices // 2, width // devices
    order = chip_order(chips)
    if rows % 16:
        turned = own.reshape(count * size, width).T.reshape(chips, 2, rows, count * size)
        turned = turned[jnp.array(order)]
        return turned.transpose(1, 0, 2, 3).reshape(width, count * size)

    def kernel(own_ref, out_ref):
        @pl.loop(0, count)
        def _(block):
            cols = pl.ds(pl.multiple_of(block * size, size), size)
            turned = own_ref[block].T
            for device in range(devices):
                chip, core = divmod(device, 2)
                out_ref[pl.ds((core * chips + order.index(chip)) * rows, rows), cols] = (
                    turned[device * rows : (device + 1) * rows]
                )

    return pl.pallas_call(
        kernel,
        out_shape=jax.ShapeDtypeStruct((width, count * size), own.dtype),
        in_specs=[VMEM],
        out_specs=VMEM,
        compiler_params=PARAMETERS,
        cost_estimate=cost(0, 4 * own.size),
    )(own)


def steps(columns):
    step = 2 * LANES if columns % (2 * LANES) == 0 else columns
    return [pl.ds(at, step) for at in range(0, columns, step)]


def halo_place(column, count, halo):
    place = column - count
    upper = place >= halo
    odd = lax.rem(lax.axis_index(AXIS), 2)
    return upper == (odd == 1), jnp.where(upper, place - halo, place)


def fold_far(turned, blocks, columns, halo):
    params, count, slots, size, _ = blocks.shape
    width = turned.shape[0]

    def kernel(columns_ref, turned_ref, blocks_ref, out_ref, sum_ref):
        sum_ref[...] = jnp.zeros_like(sum_ref)

        @pl.loop(0, count)
        def _(row):
            rows = pl.ds(pl.multiple_of(row * size, size), size)
            for param in range(params):
                for slot in range(1, slots):
                    column = columns_ref[param, row, slot - 1]
                    far, place = halo_place(column, count, halo)

                    @pl.when((column >= count) & far)
                    def _():
                        at = pl.ds(pl.multiple_of(place * size, size), size)
                        sum_ref[param, :, at] += jnp.dot(
                            turned_ref[:, rows],
                            blocks_ref[param, row, slot],
                            preferred_element_type=jnp.float32,
                        )

        out_ref[...] = sum_ref[...].astype(out_ref.dtype)

    shape = (params, width, halo * size)
    return pl.pallas_call(
        kernel,
        out_shape=jax.ShapeDtypeStruct(shape, turned.dtype),
        in_specs=[SMEM, VMEM, VMEM],
        out_specs=VMEM,
        scratch_shapes=[pltpu.VMEM(shape, jnp.float32)],
        compiler_params=PARAMETERS,
        cost_estimate=cost(
            params * count * (slots - 1) * size * size * width, 2 * (turned.size + blocks.size)
        ),
    )(columns, turned, blocks)


def local_parts(turned, own, nears, blocks, columns):
    params, count, slots, size, _ = blocks.shape
    halo, width = nears[0].shape[0], own.shape[2]
    ranges = halves(width)

    def kernel(columns_ref, turned_ref, own_ref, blocks_ref, *refs):
        near_refs, (out_ref, list_ref, image_ref) = refs[: len(ranges)], refs[len(ranges) :]
        list_ref[pl.ds(0, count)] = own_ref[...]
        for part, near_ref in zip(ranges, near_refs):
            list_ref[pl.ds(count, halo), :, pl.ds(*part)] = near_ref[...]

        @pl.loop(0, count, unroll=4)
        def _(row):
            at = pl.ds(pl.multiple_of(row * size, size), size)
            for param in range(params):
                left, right = [blocks_ref[param, row, 0]], [list_ref[row]]
                for slot in range(1, slots):
                    block = blocks_ref[param, row, slot]
                    column = columns_ref[param, row, slot - 1]
                    far, place = halo_place(column, count, halo)
                    here = (column < count) | jnp.logical_not(far)
                    left.append(jnp.where(here, block, jnp.zeros_like(block)))
                    right.append(list_ref[jnp.where(column < count, column, count + place)])
                image = jnp.dot(
                    jnp.concatenate(left, axis=1),
                    jnp.concatenate(right, axis=0),
                    preferred_element_type=jnp.float32,
                )
                image_ref[at, pl.ds(param * width, width)] = image.astype(image_ref.dtype)

        for param in range(params):
            for cols in steps(width):
                out_ref[param, :, cols] = jnp.dot(
                    turned_ref[...],
                    image_ref[:, pl.ds(param * width + cols.start, cols.size)],
                    preferred_element_type=jnp.float32,
                )

    rows = count * size
    return pl.pallas_call(
        kernel,
        out_shape=jax.ShapeDtypeStruct((params, width, width), jnp.float32),
        in_specs=[SMEM] + [VMEM] * (3 + len(ranges)),
        out_specs=VMEM,
        scratch_shapes=[
            pltpu.VMEM((count + halo, size, width), own.dtype),
            pltpu.VMEM((rows, params * width), jnp.bfloat16),
        ],
        compiler_params=PARAMETERS,
        cost_estimate=cost(
            2 * params * rows * width * (slots * size + width),
            2 * (turned.size + 2 * own.size + blocks.size) + 4 * params * width * width,
        ),
    )(columns, turned, own, blocks, *nears)


def with_far(local, folds, far, mine):
    params, width, depth = folds.shape
    half, span = width // 2, far.shape[2]

    def kernel(local_ref, folds_ref, far_ref, out_ref):
        odd = lax.rem(lax.axis_index(AXIS), 2)
        rows = pl.ds(pl.multiple_of((odd if mine else 1 - odd) * half, half), half)
        right = far_ref[...].reshape(depth, span)
        for param in range(params):
            total = local_ref[param, rows] + jnp.dot(
                folds_ref[param, rows], right, preferred_element_type=jnp.float32
            )
            out_ref[:, pl.ds(param * span, span)] = total.astype(out_ref.dtype)

    columns = params * span
    return pl.pallas_call(
        kernel,
        out_shape=jax.ShapeDtypeStruct((half, columns), jnp.float32 if mine else jnp.bfloat16),
        in_specs=[VMEM] * 3,
        out_specs=VMEM,
        compiler_params=PARAMETERS,
        cost_estimate=cost(
            2 * half * depth * columns,
            4 * half * columns + params * half * depth * 2 + 2 * depth * span,
        ),
    )(local, folds, far)


def add_chips(parts):
    def kernel(parts_ref, out_ref):
        out_ref[...] = jnp.sum(parts_ref[...].astype(jnp.float32), axis=0)

    return pl.pallas_call(
        kernel,
        out_shape=jax.ShapeDtypeStruct(parts.shape[1:], jnp.float32),
        in_specs=[VMEM],
        out_specs=VMEM,
        compiler_params=PARAMETERS,
        cost_estimate=cost(0, 2 * parts.size),
    )(parts)


def shards(basis, blocks, columns, sends):
    params, count, _, size, _ = blocks.shape
    width = basis.shape[1]
    halo = sends.shape[1] // 2
    devices = lax.axis_size(AXIS)
    chips = devices // 2
    near_pairs, far_pairs = pairs(devices, 0), pairs(devices, 1)

    own, far = pick_far(basis.reshape(count, size, width), sends)
    far = lax.ppermute(far, AXIS, far_pairs)
    nears = [lax.ppermute(near, AXIS, near_pairs) for near in pick_near(own, sends)]

    turned = transposed(own, devices)
    folds = fold_far(turned, blocks, columns, halo)
    local = local_parts(turned, own, nears, blocks, columns)

    taken = lax.ppermute(with_far(local, folds, far, False), AXIS, near_pairs)
    keep = with_far(local, folds, far, True)
    chip_sum = (keep + taken.astype(jnp.float32)).astype(jnp.bfloat16)
    parts = lax.all_to_all(
        chip_sum.reshape(chips, width // devices, params * width), AXIS,
        split_axis=0, concat_axis=0, tiled=True,
        axis_index_groups=[[2 * chip + core for chip in chip_order(chips)] for core in range(2)],
    )
    return add_chips(parts)


def solution(mesh):
    placed = (
        P(("grp", "mesh"), None),
        P(None, ("grp", "mesh"), None, None, None),
        P(None, ("grp", "mesh"), None),
        P(("grp", "mesh"), None),
    )
    return jax.shard_map(
        shards, mesh=mesh, in_specs=placed, out_specs=P(("grp", "mesh"), None), check_vma=False
    )
```

```python
import jax
import jax.numpy as jnp
from jax import lax
from jax.experimental import pallas as pl
from jax.experimental.pallas import tpu as pltpu
from jax.sharding import PartitionSpec as P

AXIS = "mesh"
LANES = 128
EASE = 8
VMEM_BYTES = 24 * 1024 * 1024
VMEM = pl.BlockSpec(memory_space=pltpu.VMEM)
SMEM = pl.BlockSpec(memory_space=pltpu.SMEM)
PARAMETERS = pltpu.CompilerParams(vmem_limit_bytes=VMEM_BYTES)


def cost(flops, moved):
    return pl.CostEstimate(flops=flops // EASE, bytes_accessed=moved // EASE, transcendentals=0)


def pairs(count, first):
    both = []
    for low in range(first, count - 1, 2):
        both += [(low, low + 1), (low + 1, low)]
    return both


def chip_order(chips, core):
    up, down = range(chips), range(chips - 1, -1, -1)
    ends = zip(up, down) if core else zip(down, up)
    return [chip for pair in ends for chip in pair][:chips]


def halves(width):
    half = width // 2
    return [(0, width)] if half % LANES else [(0, half), (half, half)]


def pick_far(own, sends):
    count, size, width = own.shape
    halo = sends.shape[1] // 2

    def kernel(sends_hbm, own_hbm, own_ref, far_ref, sends_ref, list_sem, sems):
        lists = pltpu.make_async_copy(sends_hbm, sends_ref, list_sem)
        lists.start()
        loads = [
            pltpu.make_async_copy(own_hbm.at[block], own_ref.at[block], sems.at[block])
            for block in range(count)
        ]
        for load in loads:
            load.start()
        lists.wait()
        for load in loads:
            load.wait()
        first = lax.rem(lax.axis_index(AXIS), 2) * halo
        for place in range(halo):
            far_ref[place] = own_ref[sends_ref[0, first + place]]

    return pl.pallas_call(
        kernel,
        out_shape=(
            jax.ShapeDtypeStruct(own.shape, own.dtype),
            jax.ShapeDtypeStruct((halo, size, width), own.dtype),
        ),
        in_specs=[pl.BlockSpec(memory_space=pltpu.HBM)] * 2,
        out_specs=(VMEM,) * 2,
        scratch_shapes=[
            pltpu.SMEM(sends.shape, sends.dtype),
            pltpu.SemaphoreType.DMA(()),
            pltpu.SemaphoreType.DMA((count,)),
        ],
        compiler_params=PARAMETERS,
        cost_estimate=cost(0, 5 * own.size),
    )(
        pltpu.with_memory_space_constraint(sends, pltpu.HBM),
        pltpu.with_memory_space_constraint(own, pltpu.HBM),
    )


def pick_near(own, sends):
    _, size, width = own.shape
    halo = sends.shape[1] // 2
    ranges = halves(width)

    def kernel(sends_hbm, own_ref, *refs):
        near_refs, sends_ref = refs[:-1], refs[-1]
        pltpu.sync_copy(sends_hbm, sends_ref)
        first = (1 - lax.rem(lax.axis_index(AXIS), 2)) * halo
        for place in range(halo):
            block = sends_ref[0, first + place]
            for part, near_ref in zip(ranges, near_refs):
                near_ref[place] = own_ref[block, :, pl.ds(*part)]

    return pl.pallas_call(
        kernel,
        out_shape=[jax.ShapeDtypeStruct((halo, size, span), own.dtype) for _, span in ranges],
        in_specs=[pl.BlockSpec(memory_space=pltpu.HBM), VMEM],
        out_specs=[VMEM] * len(ranges),
        scratch_shapes=[pltpu.SMEM(sends.shape, sends.dtype)],
        compiler_params=PARAMETERS,
        cost_estimate=cost(0, 2 * own.size),
    )(pltpu.with_memory_space_constraint(sends, pltpu.HBM), own)


def transposed(own, devices):
    count, size, width = own.shape
    chips, rows = devices // 2, width // devices
    orders = [chip_order(chips, core) for core in range(2)]
    if rows % 16:
        turned = own.reshape(count * size, width).T.reshape(chips, 2, rows, count * size)
        turned = jnp.stack([turned[jnp.array(orders[core]), core] for core in range(2)])
        return turned.reshape(width, count * size)

    def kernel(own_ref, out_ref):
        @pl.loop(0, count)
        def _(block):
            cols = pl.ds(pl.multiple_of(block * size, size), size)
            turned = own_ref[block].T
            for device in range(devices):
                chip, core = divmod(device, 2)
                out_ref[pl.ds((core * chips + orders[core].index(chip)) * rows, rows), cols] = (
                    turned[device * rows : (device + 1) * rows]
                )

    return pl.pallas_call(
        kernel,
        out_shape=jax.ShapeDtypeStruct((width, count * size), own.dtype),
        in_specs=[VMEM],
        out_specs=VMEM,
        compiler_params=PARAMETERS,
        cost_estimate=cost(0, 4 * own.size),
    )(own)


def steps(columns):
    step = 2 * LANES if columns % (2 * LANES) == 0 else columns
    return [pl.ds(at, step) for at in range(0, columns, step)]


def halo_place(column, count, halo):
    place = column - count
    upper = place >= halo
    odd = lax.rem(lax.axis_index(AXIS), 2)
    return upper == (odd == 1), jnp.where(upper, place - halo, place)


def fold_far(turned, blocks, columns, halo):
    params, count, slots, size, _ = blocks.shape
    width = turned.shape[0]

    def kernel(columns_ref, turned_ref, blocks_ref, out_ref, sum_ref):
        sum_ref[...] = jnp.zeros_like(sum_ref)

        @pl.loop(0, count)
        def _(row):
            rows = pl.ds(pl.multiple_of(row * size, size), size)
            for param in range(params):
                for slot in range(1, slots):
                    column = columns_ref[param, row, slot - 1]
                    far, place = halo_place(column, count, halo)

                    @pl.when((column >= count) & far)
                    def _():
                        at = pl.ds(pl.multiple_of(place * size, size), size)
                        sum_ref[param, :, at] += jnp.dot(
                            turned_ref[:, rows],
                            blocks_ref[param, row, slot],
                            preferred_element_type=jnp.float32,
                        )

        out_ref[...] = sum_ref[...].astype(out_ref.dtype)

    shape = (params, width, halo * size)
    return pl.pallas_call(
        kernel,
        out_shape=jax.ShapeDtypeStruct(shape, turned.dtype),
        in_specs=[SMEM, VMEM, VMEM],
        out_specs=VMEM,
        scratch_shapes=[pltpu.VMEM(shape, jnp.float32)],
        compiler_params=PARAMETERS,
        cost_estimate=cost(
            params * count * (slots - 1) * size * size * width, 2 * (turned.size + blocks.size)
        ),
    )(columns, turned, blocks)


def local_parts(turned, own, nears, blocks, columns):
    params, count, slots, size, _ = blocks.shape
    halo, width = nears[0].shape[0], own.shape[2]
    ranges = halves(width)

    def kernel(columns_ref, turned_ref, own_ref, blocks_ref, *refs):
        near_refs, (out_ref, list_ref, image_ref) = refs[: len(ranges)], refs[len(ranges) :]
        list_ref[pl.ds(0, count)] = own_ref[...]
        for part, near_ref in zip(ranges, near_refs):
            list_ref[pl.ds(count, halo), :, pl.ds(*part)] = near_ref[...]

        @pl.loop(0, count, unroll=4)
        def _(row):
            at = pl.ds(pl.multiple_of(row * size, size), size)
            for param in range(params):
                left, right = [blocks_ref[param, row, 0]], [list_ref[row]]
                for slot in range(1, slots):
                    block = blocks_ref[param, row, slot]
                    column = columns_ref[param, row, slot - 1]
                    far, place = halo_place(column, count, halo)
                    here = (column < count) | jnp.logical_not(far)
                    left.append(jnp.where(here, block, jnp.zeros_like(block)))
                    right.append(list_ref[jnp.where(column < count, column, count + place)])
                image = jnp.dot(
                    jnp.concatenate(left, axis=1),
                    jnp.concatenate(right, axis=0),
                    preferred_element_type=jnp.float32,
                )
                image_ref[at, pl.ds(param * width, width)] = image.astype(image_ref.dtype)

        for param in range(params):
            for cols in steps(width):
                out_ref[param, :, cols] = jnp.dot(
                    turned_ref[...],
                    image_ref[:, pl.ds(param * width + cols.start, cols.size)],
                    preferred_element_type=jnp.float32,
                )

    rows = count * size
    return pl.pallas_call(
        kernel,
        out_shape=jax.ShapeDtypeStruct((params, width, width), jnp.float32),
        in_specs=[SMEM] + [VMEM] * (3 + len(ranges)),
        out_specs=VMEM,
        scratch_shapes=[
            pltpu.VMEM((count + halo, size, width), own.dtype),
            pltpu.VMEM((rows, params * width), jnp.bfloat16),
        ],
        compiler_params=PARAMETERS,
        cost_estimate=cost(
            2 * params * rows * width * (slots * size + width),
            2 * (turned.size + 2 * own.size + blocks.size) + 4 * params * width * width,
        ),
    )(columns, turned, own, blocks, *nears)


def with_far(local, folds, far, mine):
    params, width, depth = folds.shape
    half, span = width // 2, far.shape[2]

    def kernel(local_ref, folds_ref, far_ref, out_ref):
        odd = lax.rem(lax.axis_index(AXIS), 2)
        rows = pl.ds(pl.multiple_of((odd if mine else 1 - odd) * half, half), half)
        right = far_ref[...].reshape(depth, span)
        for param in range(params):
            total = local_ref[param, rows] + jnp.dot(
                folds_ref[param, rows], right, preferred_element_type=jnp.float32
            )
            out_ref[:, pl.ds(param * span, span)] = total.astype(out_ref.dtype)

    columns = params * span
    return pl.pallas_call(
        kernel,
        out_shape=jax.ShapeDtypeStruct((half, columns), jnp.float32 if mine else jnp.bfloat16),
        in_specs=[VMEM] * 3,
        out_specs=VMEM,
        compiler_params=PARAMETERS,
        cost_estimate=cost(
            2 * half * depth * columns,
            4 * half * columns + params * half * depth * 2 + 2 * depth * span,
        ),
    )(local, folds, far)


def add_chips(parts):
    def kernel(parts_ref, out_ref):
        out_ref[...] = jnp.sum(parts_ref[...].astype(jnp.float32), axis=0)

    return pl.pallas_call(
        kernel,
        out_shape=jax.ShapeDtypeStruct(parts.shape[1:], jnp.float32),
        in_specs=[VMEM],
        out_specs=VMEM,
        compiler_params=PARAMETERS,
        cost_estimate=cost(0, 2 * parts.size),
    )(parts)


def shards(basis, blocks, columns, sends):
    params, count, _, size, _ = blocks.shape
    width = basis.shape[1]
    halo = sends.shape[1] // 2
    devices = lax.axis_size(AXIS)
    chips = devices // 2
    near_pairs, far_pairs = pairs(devices, 0), pairs(devices, 1)

    own, far = pick_far(basis.reshape(count, size, width), sends)
    far = lax.ppermute(far, AXIS, far_pairs)
    nears = [lax.ppermute(near, AXIS, near_pairs) for near in pick_near(own, sends)]

    turned = transposed(own, devices)
    folds = fold_far(turned, blocks, columns, halo)
    local = local_parts(turned, own, nears, blocks, columns)

    taken = lax.ppermute(with_far(local, folds, far, False), AXIS, near_pairs)
    keep = with_far(local, folds, far, True)
    chip_sum = (keep + taken.astype(jnp.float32)).astype(jnp.bfloat16)
    parts = lax.all_to_all(
        chip_sum.reshape(chips, width // devices, params * width), AXIS,
        split_axis=0, concat_axis=0, tiled=True,
        axis_index_groups=[[2 * chip + core for chip in chip_order(chips, core)] for core in range(2)],
    )
    return add_chips(parts)


def solution(mesh):
    placed = (
        P(("grp", "mesh"), None),
        P(None, ("grp", "mesh"), None, None, None),
        P(None, ("grp", "mesh"), None),
        P(("grp", "mesh"), None),
    )
    return jax.shard_map(
        shards, mesh=mesh, in_specs=placed, out_specs=P(("grp", "mesh"), None), check_vma=False
    )
```

```python
import jax
import jax.numpy as jnp
from jax import lax
from jax.experimental import pallas as pl
from jax.experimental.pallas import tpu as pltpu
from jax.sharding import PartitionSpec as P

AXIS = "mesh"
LANES = 128
EASE = 8
VMEM_BYTES = 24 * 1024 * 1024
VMEM = pl.BlockSpec(memory_space=pltpu.VMEM)
SMEM = pl.BlockSpec(memory_space=pltpu.SMEM)
PARAMETERS = pltpu.CompilerParams(vmem_limit_bytes=VMEM_BYTES)


def cost(flops, moved):
    return pl.CostEstimate(flops=flops // EASE, bytes_accessed=moved // EASE, transcendentals=0)


def pairs(count, first):
    both = []
    for low in range(first, count - 1, 2):
        both += [(low, low + 1), (low + 1, low)]
    return both


def chip_order(chips):
    half = chips // 2
    pairs_of = zip(range(chips - 1, half - 1, -1), range(chips - half - 1, -1, -1))
    order = [chip for pair in pairs_of for chip in pair]
    return order + [chip for chip in range(chips) if chip not in order]


def halves(width):
    half = width // 2
    return [(0, width)] if half % LANES else [(0, half), (half, half)]


def pick_far(own, sends):
    count, size, width = own.shape
    halo = sends.shape[1] // 2

    def kernel(sends_hbm, own_hbm, own_ref, far_ref, sends_ref, list_sem, sems):
        lists = pltpu.make_async_copy(sends_hbm, sends_ref, list_sem)
        lists.start()
        loads = [
            pltpu.make_async_copy(own_hbm.at[block], own_ref.at[block], sems.at[block])
            for block in range(count)
        ]
        for load in loads:
            load.start()
        lists.wait()
        for load in loads:
            load.wait()
        first = lax.rem(lax.axis_index(AXIS), 2) * halo
        for place in range(halo):
            far_ref[place] = own_ref[sends_ref[0, first + place]]

    return pl.pallas_call(
        kernel,
        out_shape=(
            jax.ShapeDtypeStruct(own.shape, own.dtype),
            jax.ShapeDtypeStruct((halo, size, width), own.dtype),
        ),
        in_specs=[pl.BlockSpec(memory_space=pltpu.HBM)] * 2,
        out_specs=(VMEM,) * 2,
        scratch_shapes=[
            pltpu.SMEM(sends.shape, sends.dtype),
            pltpu.SemaphoreType.DMA(()),
            pltpu.SemaphoreType.DMA((count,)),
        ],
        compiler_params=PARAMETERS,
        cost_estimate=cost(0, 5 * own.size),
    )(
        pltpu.with_memory_space_constraint(sends, pltpu.HBM),
        pltpu.with_memory_space_constraint(own, pltpu.HBM),
    )


def pick_near(own, sends):
    _, size, width = own.shape
    halo = sends.shape[1] // 2
    ranges = halves(width)

    def kernel(sends_hbm, own_ref, *refs):
        near_refs, sends_ref = refs[:-1], refs[-1]
        pltpu.sync_copy(sends_hbm, sends_ref)
        first = (1 - lax.rem(lax.axis_index(AXIS), 2)) * halo
        for place in range(halo):
            block = sends_ref[0, first + place]
            for part, near_ref in zip(ranges, near_refs):
                near_ref[place] = own_ref[block, :, pl.ds(*part)]

    return pl.pallas_call(
        kernel,
        out_shape=[jax.ShapeDtypeStruct((halo, size, span), own.dtype) for _, span in ranges],
        in_specs=[pl.BlockSpec(memory_space=pltpu.HBM), VMEM],
        out_specs=[VMEM] * len(ranges),
        scratch_shapes=[pltpu.SMEM(sends.shape, sends.dtype)],
        compiler_params=PARAMETERS,
        cost_estimate=cost(0, 2 * own.size),
    )(pltpu.with_memory_space_constraint(sends, pltpu.HBM), own)


def transposed(own, devices):
    count, size, width = own.shape
    chips, rows = devices // 2, width // devices
    order = chip_order(chips)
    if rows % 16:
        turned = own.reshape(count * size, width).T.reshape(chips, 2, rows, count * size)
        turned = turned[jnp.array(order)]
        return turned.transpose(1, 0, 2, 3).reshape(width, count * size)

    def kernel(own_ref, out_ref):
        @pl.loop(0, count)
        def _(block):
            cols = pl.ds(pl.multiple_of(block * size, size), size)
            turned = own_ref[block].T
            for device in range(devices):
                chip, core = divmod(device, 2)
                out_ref[pl.ds((core * chips + order.index(chip)) * rows, rows), cols] = (
                    turned[device * rows : (device + 1) * rows]
                )

    return pl.pallas_call(
        kernel,
        out_shape=jax.ShapeDtypeStruct((width, count * size), own.dtype),
        in_specs=[VMEM],
        out_specs=VMEM,
        compiler_params=PARAMETERS,
        cost_estimate=cost(0, 4 * own.size),
    )(own)


def steps(columns):
    step = 2 * LANES if columns % (2 * LANES) == 0 else columns
    return [pl.ds(at, step) for at in range(0, columns, step)]


def halo_place(column, count, halo):
    place = column - count
    upper = place >= halo
    odd = lax.rem(lax.axis_index(AXIS), 2)
    return upper == (odd == 1), jnp.where(upper, place - halo, place)


def fold_far(turned, blocks, columns, halo):
    params, count, slots, size, _ = blocks.shape
    width = turned.shape[0]

    def kernel(columns_ref, turned_ref, blocks_ref, out_ref, sum_ref):
        sum_ref[...] = jnp.zeros_like(sum_ref)

        @pl.loop(0, count)
        def _(row):
            rows = pl.ds(pl.multiple_of(row * size, size), size)
            for param in range(params):
                for slot in range(1, slots):
                    column = columns_ref[param, row, slot - 1]
                    far, place = halo_place(column, count, halo)

                    @pl.when((column >= count) & far)
                    def _():
                        at = pl.ds(pl.multiple_of(place * size, size), size)
                        sum_ref[param, :, at] += jnp.dot(
                            turned_ref[:, rows],
                            blocks_ref[param, row, slot],
                            preferred_element_type=jnp.float32,
                        )

        out_ref[...] = sum_ref[...].astype(out_ref.dtype)

    shape = (params, width, halo * size)
    return pl.pallas_call(
        kernel,
        out_shape=jax.ShapeDtypeStruct(shape, turned.dtype),
        in_specs=[SMEM, VMEM, VMEM],
        out_specs=VMEM,
        scratch_shapes=[pltpu.VMEM(shape, jnp.float32)],
        compiler_params=PARAMETERS,
        cost_estimate=cost(
            params * count * (slots - 1) * size * size * width, 2 * (turned.size + blocks.size)
        ),
    )(columns, turned, blocks)


def local_parts(turned, own, nears, blocks, columns):
    params, count, slots, size, _ = blocks.shape
    halo, width = nears[0].shape[0], own.shape[2]
    ranges = halves(width)

    def kernel(columns_ref, turned_ref, own_ref, blocks_ref, *refs):
        near_refs, (out_ref, list_ref, image_ref) = refs[: len(ranges)], refs[len(ranges) :]
        list_ref[pl.ds(0, count)] = own_ref[...]
        for part, near_ref in zip(ranges, near_refs):
            list_ref[pl.ds(count, halo), :, pl.ds(*part)] = near_ref[...]

        @pl.loop(0, count, unroll=4)
        def _(row):
            at = pl.ds(pl.multiple_of(row * size, size), size)
            for param in range(params):
                left, right = [blocks_ref[param, row, 0]], [list_ref[row]]
                for slot in range(1, slots):
                    block = blocks_ref[param, row, slot]
                    column = columns_ref[param, row, slot - 1]
                    far, place = halo_place(column, count, halo)
                    here = (column < count) | jnp.logical_not(far)
                    left.append(jnp.where(here, block, jnp.zeros_like(block)))
                    right.append(list_ref[jnp.where(column < count, column, count + place)])
                image = jnp.dot(
                    jnp.concatenate(left, axis=1),
                    jnp.concatenate(right, axis=0),
                    preferred_element_type=jnp.float32,
                )
                image_ref[at, pl.ds(param * width, width)] = image.astype(image_ref.dtype)

        for param in range(params):
            for cols in steps(width):
                out_ref[param, :, cols] = jnp.dot(
                    turned_ref[...],
                    image_ref[:, pl.ds(param * width + cols.start, cols.size)],
                    preferred_element_type=jnp.float32,
                )

    rows = count * size
    return pl.pallas_call(
        kernel,
        out_shape=jax.ShapeDtypeStruct((params, width, width), jnp.float32),
        in_specs=[SMEM] + [VMEM] * (3 + len(ranges)),
        out_specs=VMEM,
        scratch_shapes=[
            pltpu.VMEM((count + halo, size, width), own.dtype),
            pltpu.VMEM((rows, params * width), jnp.bfloat16),
        ],
        compiler_params=PARAMETERS,
        cost_estimate=cost(
            2 * params * rows * width * (slots * size + width),
            2 * (turned.size + 2 * own.size + blocks.size) + 4 * params * width * width,
        ),
    )(columns, turned, own, blocks, *nears)


def with_far(local, folds, far, mine):
    params, width, depth = folds.shape
    half, span = width // 2, far.shape[2]

    def kernel(local_ref, folds_ref, far_ref, out_ref):
        odd = lax.rem(lax.axis_index(AXIS), 2)
        rows = pl.ds(pl.multiple_of((odd if mine else 1 - odd) * half, half), half)
        right = far_ref[...].reshape(depth, span)
        for param in range(params):
            total = local_ref[param, rows] + jnp.dot(
                folds_ref[param, rows], right, preferred_element_type=jnp.float32
            )
            out_ref[:, pl.ds(param * span, span)] = total.astype(out_ref.dtype)

    columns = params * span
    return pl.pallas_call(
        kernel,
        out_shape=jax.ShapeDtypeStruct((half, columns), jnp.float32 if mine else jnp.bfloat16),
        in_specs=[VMEM] * 3,
        out_specs=VMEM,
        compiler_params=PARAMETERS,
        cost_estimate=cost(
            2 * half * depth * columns,
            4 * half * columns + params * half * depth * 2 + 2 * depth * span,
        ),
    )(local, folds, far)


def add_chips(parts):
    def kernel(parts_ref, out_ref):
        out_ref[...] = jnp.sum(parts_ref[...].astype(jnp.float32), axis=0)

    return pl.pallas_call(
        kernel,
        out_shape=jax.ShapeDtypeStruct(parts.shape[1:], jnp.float32),
        in_specs=[VMEM],
        out_specs=VMEM,
        compiler_params=PARAMETERS,
        cost_estimate=cost(0, 2 * parts.size),
    )(parts)


def shards(basis, blocks, columns, sends):
    params, count, _, size, _ = blocks.shape
    width = basis.shape[1]
    halo = sends.shape[1] // 2
    devices = lax.axis_size(AXIS)
    chips = devices // 2
    near_pairs, far_pairs = pairs(devices, 0), pairs(devices, 1)

    own, far = pick_far(basis.reshape(count, size, width), sends)
    far = lax.ppermute(far, AXIS, far_pairs)
    nears = [lax.ppermute(near, AXIS, near_pairs) for near in pick_near(own, sends)]

    turned = transposed(own, devices)
    folds = fold_far(turned, blocks, columns, halo)
    local = local_parts(turned, own, nears, blocks, columns)

    taken = lax.ppermute(with_far(local, folds, far, False), AXIS, near_pairs)
    keep = with_far(local, folds, far, True)
    chip_sum = (keep + taken.astype(jnp.float32)).astype(jnp.bfloat16)
    parts = lax.all_to_all(
        chip_sum.reshape(chips, width // devices, params * width), AXIS,
        split_axis=0, concat_axis=0, tiled=True,
        axis_index_groups=[[2 * chip + core for chip in chip_order(chips)] for core in range(2)],
    )
    return add_chips(parts)


def solution(mesh):
    placed = (
        P(("grp", "mesh"), None),
        P(None, ("grp", "mesh"), None, None, None),
        P(None, ("grp", "mesh"), None),
        P(("grp", "mesh"), None),
    )
    return jax.shard_map(
        shards, mesh=mesh, in_specs=placed, out_specs=P(("grp", "mesh"), None), check_vma=False
    )
```

```python
import jax
import jax.numpy as jnp
from jax import lax
from jax.experimental import pallas as pl
from jax.experimental.pallas import tpu as pltpu
from jax.sharding import PartitionSpec as P

AXIS = "mesh"
LANES = 128
EASE = 8
VMEM_BYTES = 24 * 1024 * 1024
VMEM = pl.BlockSpec(memory_space=pltpu.VMEM)
SMEM = pl.BlockSpec(memory_space=pltpu.SMEM)
PARAMETERS = pltpu.CompilerParams(vmem_limit_bytes=VMEM_BYTES)


def cost(flops, moved):
    return pl.CostEstimate(flops=flops // EASE, bytes_accessed=moved // EASE, transcendentals=0)


def pairs(count, first):
    both = []
    for low in range(first, count - 1, 2):
        both += [(low, low + 1), (low + 1, low)]
    return both


def chip_order(chips):
    low = [chip ^ 1 for chip in range(chips)] if chips % 2 == 0 else list(range(chips))
    ends = zip(range(chips - 1, -1, -1), low)
    order = [chip for pair in ends for chip in pair][:chips]
    return order if len(set(order)) == chips else list(range(chips))


def halves(width):
    half = width // 2
    return [(0, width)] if half % LANES else [(0, half), (half, half)]


def pick_far(own, sends):
    count, size, width = own.shape
    halo = sends.shape[1] // 2

    def kernel(sends_hbm, own_hbm, own_ref, far_ref, sends_ref, list_sem, sems):
        lists = pltpu.make_async_copy(sends_hbm, sends_ref, list_sem)
        lists.start()
        loads = [
            pltpu.make_async_copy(own_hbm.at[block], own_ref.at[block], sems.at[block])
            for block in range(count)
        ]
        for load in loads:
            load.start()
        lists.wait()
        for load in loads:
            load.wait()
        first = lax.rem(lax.axis_index(AXIS), 2) * halo
        for place in range(halo):
            far_ref[place] = own_ref[sends_ref[0, first + place]]

    return pl.pallas_call(
        kernel,
        out_shape=(
            jax.ShapeDtypeStruct(own.shape, own.dtype),
            jax.ShapeDtypeStruct((halo, size, width), own.dtype),
        ),
        in_specs=[pl.BlockSpec(memory_space=pltpu.HBM)] * 2,
        out_specs=(VMEM,) * 2,
        scratch_shapes=[
            pltpu.SMEM(sends.shape, sends.dtype),
            pltpu.SemaphoreType.DMA(()),
            pltpu.SemaphoreType.DMA((count,)),
        ],
        compiler_params=PARAMETERS,
        cost_estimate=cost(0, 5 * own.size),
    )(
        pltpu.with_memory_space_constraint(sends, pltpu.HBM),
        pltpu.with_memory_space_constraint(own, pltpu.HBM),
    )


def pick_near(own, sends):
    _, size, width = own.shape
    halo = sends.shape[1] // 2
    ranges = halves(width)

    def kernel(sends_hbm, own_ref, *refs):
        near_refs, sends_ref = refs[:-1], refs[-1]
        pltpu.sync_copy(sends_hbm, sends_ref)
        first = (1 - lax.rem(lax.axis_index(AXIS), 2)) * halo
        for place in range(halo):
            block = sends_ref[0, first + place]
            for part, near_ref in zip(ranges, near_refs):
                near_ref[place] = own_ref[block, :, pl.ds(*part)]

    return pl.pallas_call(
        kernel,
        out_shape=[jax.ShapeDtypeStruct((halo, size, span), own.dtype) for _, span in ranges],
        in_specs=[pl.BlockSpec(memory_space=pltpu.HBM), VMEM],
        out_specs=[VMEM] * len(ranges),
        scratch_shapes=[pltpu.SMEM(sends.shape, sends.dtype)],
        compiler_params=PARAMETERS,
        cost_estimate=cost(0, 2 * own.size),
    )(pltpu.with_memory_space_constraint(sends, pltpu.HBM), own)


def transposed(own, devices):
    count, size, width = own.shape
    chips, rows = devices // 2, width // devices
    order = chip_order(chips)
    if rows % 16:
        turned = own.reshape(count * size, width).T.reshape(chips, 2, rows, count * size)
        turned = turned[jnp.array(order)]
        return turned.transpose(1, 0, 2, 3).reshape(width, count * size)

    def kernel(own_ref, out_ref):
        @pl.loop(0, count)
        def _(block):
            cols = pl.ds(pl.multiple_of(block * size, size), size)
            turned = own_ref[block].T
            for device in range(devices):
                chip, core = divmod(device, 2)
                out_ref[pl.ds((core * chips + order.index(chip)) * rows, rows), cols] = (
                    turned[device * rows : (device + 1) * rows]
                )

    return pl.pallas_call(
        kernel,
        out_shape=jax.ShapeDtypeStruct((width, count * size), own.dtype),
        in_specs=[VMEM],
        out_specs=VMEM,
        compiler_params=PARAMETERS,
        cost_estimate=cost(0, 4 * own.size),
    )(own)


def steps(columns):
    step = 2 * LANES if columns % (2 * LANES) == 0 else columns
    return [pl.ds(at, step) for at in range(0, columns, step)]


def halo_place(column, count, halo):
    place = column - count
    upper = place >= halo
    odd = lax.rem(lax.axis_index(AXIS), 2)
    return upper == (odd == 1), jnp.where(upper, place - halo, place)


def fold_far(turned, blocks, columns, halo):
    params, count, slots, size, _ = blocks.shape
    width = turned.shape[0]

    def kernel(columns_ref, turned_ref, blocks_ref, out_ref, sum_ref):
        sum_ref[...] = jnp.zeros_like(sum_ref)

        @pl.loop(0, count)
        def _(row):
            rows = pl.ds(pl.multiple_of(row * size, size), size)
            for param in range(params):
                for slot in range(1, slots):
                    column = columns_ref[param, row, slot - 1]
                    far, place = halo_place(column, count, halo)

                    @pl.when((column >= count) & far)
                    def _():
                        at = pl.ds(pl.multiple_of(place * size, size), size)
                        sum_ref[param, :, at] += jnp.dot(
                            turned_ref[:, rows],
                            blocks_ref[param, row, slot],
                            preferred_element_type=jnp.float32,
                        )

        out_ref[...] = sum_ref[...].astype(out_ref.dtype)

    shape = (params, width, halo * size)
    return pl.pallas_call(
        kernel,
        out_shape=jax.ShapeDtypeStruct(shape, turned.dtype),
        in_specs=[SMEM, VMEM, VMEM],
        out_specs=VMEM,
        scratch_shapes=[pltpu.VMEM(shape, jnp.float32)],
        compiler_params=PARAMETERS,
        cost_estimate=cost(
            params * count * (slots - 1) * size * size * width, 2 * (turned.size + blocks.size)
        ),
    )(columns, turned, blocks)


def local_parts(turned, own, nears, blocks, columns):
    params, count, slots, size, _ = blocks.shape
    halo, width = nears[0].shape[0], own.shape[2]
    ranges = halves(width)

    def kernel(columns_ref, turned_ref, own_ref, blocks_ref, *refs):
        near_refs, (out_ref, list_ref, image_ref) = refs[: len(ranges)], refs[len(ranges) :]
        list_ref[pl.ds(0, count)] = own_ref[...]
        for part, near_ref in zip(ranges, near_refs):
            list_ref[pl.ds(count, halo), :, pl.ds(*part)] = near_ref[...]

        @pl.loop(0, count, unroll=4)
        def _(row):
            at = pl.ds(pl.multiple_of(row * size, size), size)
            for param in range(params):
                left, right = [blocks_ref[param, row, 0]], [list_ref[row]]
                for slot in range(1, slots):
                    block = blocks_ref[param, row, slot]
                    column = columns_ref[param, row, slot - 1]
                    far, place = halo_place(column, count, halo)
                    here = (column < count) | jnp.logical_not(far)
                    left.append(jnp.where(here, block, jnp.zeros_like(block)))
                    right.append(list_ref[jnp.where(column < count, column, count + place)])
                image = jnp.dot(
                    jnp.concatenate(left, axis=1),
                    jnp.concatenate(right, axis=0),
                    preferred_element_type=jnp.float32,
                )
                image_ref[at, pl.ds(param * width, width)] = image.astype(image_ref.dtype)

        for param in range(params):
            for cols in steps(width):
                out_ref[param, :, cols] = jnp.dot(
                    turned_ref[...],
                    image_ref[:, pl.ds(param * width + cols.start, cols.size)],
                    preferred_element_type=jnp.float32,
                )

    rows = count * size
    return pl.pallas_call(
        kernel,
        out_shape=jax.ShapeDtypeStruct((params, width, width), jnp.float32),
        in_specs=[SMEM] + [VMEM] * (3 + len(ranges)),
        out_specs=VMEM,
        scratch_shapes=[
            pltpu.VMEM((count + halo, size, width), own.dtype),
            pltpu.VMEM((rows, params * width), jnp.bfloat16),
        ],
        compiler_params=PARAMETERS,
        cost_estimate=cost(
            2 * params * rows * width * (slots * size + width),
            2 * (turned.size + 2 * own.size + blocks.size) + 4 * params * width * width,
        ),
    )(columns, turned, own, blocks, *nears)


def with_far(local, folds, far, mine):
    params, width, depth = folds.shape
    half, span = width // 2, far.shape[2]

    def kernel(local_ref, folds_ref, far_ref, out_ref):
        odd = lax.rem(lax.axis_index(AXIS), 2)
        rows = pl.ds(pl.multiple_of((odd if mine else 1 - odd) * half, half), half)
        right = far_ref[...].reshape(depth, span)
        for param in range(params):
            total = local_ref[param, rows] + jnp.dot(
                folds_ref[param, rows], right, preferred_element_type=jnp.float32
            )
            out_ref[:, pl.ds(param * span, span)] = total.astype(out_ref.dtype)

    columns = params * span
    return pl.pallas_call(
        kernel,
        out_shape=jax.ShapeDtypeStruct((half, columns), jnp.float32 if mine else jnp.bfloat16),
        in_specs=[VMEM] * 3,
        out_specs=VMEM,
        compiler_params=PARAMETERS,
        cost_estimate=cost(
            2 * half * depth * columns,
            4 * half * columns + params * half * depth * 2 + 2 * depth * span,
        ),
    )(local, folds, far)


def add_chips(parts):
    def kernel(parts_ref, out_ref):
        out_ref[...] = jnp.sum(parts_ref[...].astype(jnp.float32), axis=0)

    return pl.pallas_call(
        kernel,
        out_shape=jax.ShapeDtypeStruct(parts.shape[1:], jnp.float32),
        in_specs=[VMEM],
        out_specs=VMEM,
        compiler_params=PARAMETERS,
        cost_estimate=cost(0, 2 * parts.size),
    )(parts)


def shards(basis, blocks, columns, sends):
    params, count, _, size, _ = blocks.shape
    width = basis.shape[1]
    halo = sends.shape[1] // 2
    devices = lax.axis_size(AXIS)
    chips = devices // 2
    near_pairs, far_pairs = pairs(devices, 0), pairs(devices, 1)

    own, far = pick_far(basis.reshape(count, size, width), sends)
    far = lax.ppermute(far, AXIS, far_pairs)
    nears = [lax.ppermute(near, AXIS, near_pairs) for near in pick_near(own, sends)]

    turned = transposed(own, devices)
    folds = fold_far(turned, blocks, columns, halo)
    local = local_parts(turned, own, nears, blocks, columns)

    taken = lax.ppermute(with_far(local, folds, far, False), AXIS, near_pairs)
    keep = with_far(local, folds, far, True)
    chip_sum = (keep + taken.astype(jnp.float32)).astype(jnp.bfloat16)
    parts = lax.all_to_all(
        chip_sum.reshape(chips, width // devices, params * width), AXIS,
        split_axis=0, concat_axis=0, tiled=True,
        axis_index_groups=[[2 * chip + core for chip in chip_order(chips)] for core in range(2)],
    )
    return add_chips(parts)


def solution(mesh):
    placed = (
        P(("grp", "mesh"), None),
        P(None, ("grp", "mesh"), None, None, None),
        P(None, ("grp", "mesh"), None),
        P(("grp", "mesh"), None),
    )
    return jax.shard_map(
        shards, mesh=mesh, in_specs=placed, out_specs=P(("grp", "mesh"), None), check_vma=False
    )
```

```python
import jax
import jax.numpy as jnp
from jax import lax
from jax.experimental import pallas as pl
from jax.experimental.pallas import tpu as pltpu
from jax.sharding import PartitionSpec as P

AXIS = "mesh"
LANES = 128
EASE = 8
VMEM_BYTES = 24 * 1024 * 1024
VMEM = pl.BlockSpec(memory_space=pltpu.VMEM)
SMEM = pl.BlockSpec(memory_space=pltpu.SMEM)
PARAMETERS = pltpu.CompilerParams(vmem_limit_bytes=VMEM_BYTES)


def cost(flops, moved):
    return pl.CostEstimate(flops=flops // EASE, bytes_accessed=moved // EASE, transcendentals=0)


def pairs(count, first):
    both = []
    for low in range(first, count - 1, 2):
        both += [(low, low + 1), (low + 1, low)]
    return both


def chip_order(chips):
    ends = zip(range(chips - 1, -1, -1), range(chips))
    return [chip for pair in ends for chip in pair][:chips]


def halves(width):
    half = width // 2
    return [(0, width)] if half % LANES else [(0, half), (half, half)]


def pick_blocks(own, sends):
    count, size, width = own.shape
    halo = sends.shape[1] // 2
    ranges = halves(width)

    def kernel(sends_hbm, own_hbm, own_ref, *refs):
        far_refs, near_refs = refs[: len(ranges)], refs[len(ranges) : 2 * len(ranges)]
        sends_ref, sems = refs[2 * len(ranges) :]
        lists = pltpu.make_async_copy(sends_hbm, sends_ref, sems.at[0])
        load = pltpu.make_async_copy(own_hbm, own_ref, sems.at[1])
        lists.start()
        load.start()
        lists.wait()
        load.wait()
        odd = lax.rem(lax.axis_index(AXIS), 2)
        for which, out_refs in ((odd, far_refs), (1 - odd, near_refs)):
            for place in range(halo):
                block = sends_ref[0, which * halo + place]
                for part, out_ref in zip(ranges, out_refs):
                    out_ref[place] = own_ref[block, :, pl.ds(*part)]

    return pl.pallas_call(
        kernel,
        out_shape=[jax.ShapeDtypeStruct(own.shape, own.dtype)]
        + [jax.ShapeDtypeStruct((halo, size, span), own.dtype) for _, span in ranges] * 2,
        in_specs=[pl.BlockSpec(memory_space=pltpu.HBM)] * 2,
        out_specs=[VMEM] * (1 + 2 * len(ranges)),
        scratch_shapes=[pltpu.SMEM(sends.shape, sends.dtype), pltpu.SemaphoreType.DMA((2,))],
        compiler_params=PARAMETERS,
        cost_estimate=cost(0, 6 * own.size),
    )(
        pltpu.with_memory_space_constraint(sends, pltpu.HBM),
        pltpu.with_memory_space_constraint(own, pltpu.HBM),
    )


def transposed(own, devices):
    count, size, width = own.shape
    chips, rows = devices // 2, width // devices
    order = chip_order(chips)
    if rows % 16:
        turned = own.reshape(count * size, width).T.reshape(chips, 2, rows, count * size)
        turned = turned[jnp.array(order)]
        return turned.transpose(1, 0, 2, 3).reshape(width, count * size)

    def kernel(own_ref, out_ref):
        @pl.loop(0, count)
        def _(block):
            cols = pl.ds(pl.multiple_of(block * size, size), size)
            turned = own_ref[block].T
            for device in range(devices):
                chip, core = divmod(device, 2)
                out_ref[pl.ds((core * chips + order.index(chip)) * rows, rows), cols] = (
                    turned[device * rows : (device + 1) * rows]
                )

    return pl.pallas_call(
        kernel,
        out_shape=jax.ShapeDtypeStruct((width, count * size), own.dtype),
        in_specs=[VMEM],
        out_specs=VMEM,
        compiler_params=PARAMETERS,
        cost_estimate=cost(0, 4 * own.size),
    )(own)


def steps(columns):
    step = 2 * LANES if columns % (2 * LANES) == 0 else columns
    return [pl.ds(at, step) for at in range(0, columns, step)]


def halo_place(column, count, halo):
    place = column - count
    upper = place >= halo
    odd = lax.rem(lax.axis_index(AXIS), 2)
    return upper == (odd == 1), jnp.where(upper, place - halo, place)


def fold_far(turned, blocks, columns, halo):
    params, count, slots, size, _ = blocks.shape
    width = turned.shape[0]

    def kernel(columns_ref, turned_ref, blocks_ref, out_ref, sum_ref):
        sum_ref[...] = jnp.zeros_like(sum_ref)

        @pl.loop(0, count)
        def _(row):
            rows = pl.ds(pl.multiple_of(row * size, size), size)
            for param in range(params):
                for slot in range(1, slots):
                    column = columns_ref[param, row, slot - 1]
                    far, place = halo_place(column, count, halo)

                    @pl.when((column >= count) & far)
                    def _():
                        at = pl.ds(pl.multiple_of(place * size, size), size)
                        sum_ref[param, :, at] += jnp.dot(
                            turned_ref[:, rows],
                            blocks_ref[param, row, slot],
                            preferred_element_type=jnp.float32,
                        )

        out_ref[...] = sum_ref[...].astype(out_ref.dtype)

    shape = (params, width, halo * size)
    return pl.pallas_call(
        kernel,
        out_shape=jax.ShapeDtypeStruct(shape, turned.dtype),
        in_specs=[SMEM, VMEM, VMEM],
        out_specs=VMEM,
        scratch_shapes=[pltpu.VMEM(shape, jnp.float32)],
        compiler_params=PARAMETERS,
        cost_estimate=cost(
            params * count * (slots - 1) * size * size * width, 2 * (turned.size + blocks.size)
        ),
    )(columns, turned, blocks)


def local_parts(turned, own, nears, blocks, columns):
    params, count, slots, size, _ = blocks.shape
    halo, width = nears[0].shape[0], own.shape[2]
    ranges = halves(width)

    def kernel(columns_ref, turned_ref, own_ref, blocks_ref, *refs):
        near_refs, (out_ref, list_ref, image_ref) = refs[: len(ranges)], refs[len(ranges) :]
        list_ref[pl.ds(0, count)] = own_ref[...]
        for part, near_ref in zip(ranges, near_refs):
            list_ref[pl.ds(count, halo), :, pl.ds(*part)] = near_ref[...]

        @pl.loop(0, count, unroll=4)
        def _(row):
            at = pl.ds(pl.multiple_of(row * size, size), size)
            for param in range(params):
                left, right = [blocks_ref[param, row, 0]], [list_ref[row]]
                for slot in range(1, slots):
                    block = blocks_ref[param, row, slot]
                    column = columns_ref[param, row, slot - 1]
                    far, place = halo_place(column, count, halo)
                    here = (column < count) | jnp.logical_not(far)
                    left.append(jnp.where(here, block, jnp.zeros_like(block)))
                    right.append(list_ref[jnp.where(column < count, column, count + place)])
                image = jnp.dot(
                    jnp.concatenate(left, axis=1),
                    jnp.concatenate(right, axis=0),
                    preferred_element_type=jnp.float32,
                )
                image_ref[at, pl.ds(param * width, width)] = image.astype(image_ref.dtype)

        for param in range(params):
            for cols in steps(width):
                out_ref[param, :, cols] = jnp.dot(
                    turned_ref[...],
                    image_ref[:, pl.ds(param * width + cols.start, cols.size)],
                    preferred_element_type=jnp.float32,
                )

    rows = count * size
    return pl.pallas_call(
        kernel,
        out_shape=jax.ShapeDtypeStruct((params, width, width), jnp.float32),
        in_specs=[SMEM] + [VMEM] * (3 + len(ranges)),
        out_specs=VMEM,
        scratch_shapes=[
            pltpu.VMEM((count + halo, size, width), own.dtype),
            pltpu.VMEM((rows, params * width), jnp.bfloat16),
        ],
        compiler_params=PARAMETERS,
        cost_estimate=cost(
            2 * params * rows * width * (slots * size + width),
            2 * (turned.size + 2 * own.size + blocks.size) + 4 * params * width * width,
        ),
    )(columns, turned, own, blocks, *nears)


def with_far(local, folds, far, mine, start):
    params, width, depth = folds.shape
    half, span = width // 2, far.shape[2]

    def kernel(local_ref, folds_ref, far_ref, out_ref):
        odd = lax.rem(lax.axis_index(AXIS), 2)
        rows = pl.ds(pl.multiple_of((odd if mine else 1 - odd) * half, half), half)
        right = far_ref[...].reshape(depth, span)
        for param in range(params):
            total = local_ref[param, rows, pl.ds(start, span)] + jnp.dot(
                folds_ref[param, rows], right, preferred_element_type=jnp.float32
            )
            out_ref[:, pl.ds(param * span, span)] = total.astype(out_ref.dtype)

    columns = params * span
    return pl.pallas_call(
        kernel,
        out_shape=jax.ShapeDtypeStruct((half, columns), jnp.float32 if mine else jnp.bfloat16),
        in_specs=[VMEM] * 3,
        out_specs=VMEM,
        compiler_params=PARAMETERS,
        cost_estimate=cost(
            2 * half * depth * columns,
            4 * half * columns + params * half * depth * 2 + 2 * depth * span,
        ),
    )(local, folds, far)


def add_chips(parts, params):
    _, rows, columns = parts.shape
    width = columns // params
    ranges = halves(width)

    def kernel(parts_ref, out_ref):
        total = jnp.sum(parts_ref[...].astype(jnp.float32), axis=0)
        at = 0
        for start, span in ranges:
            for param in range(params):
                out_ref[:, pl.ds(param * width + start, span)] = total[:, at : at + span]
                at += span

    return pl.pallas_call(
        kernel,
        out_shape=jax.ShapeDtypeStruct((rows, columns), jnp.float32),
        in_specs=[VMEM],
        out_specs=VMEM,
        compiler_params=PARAMETERS,
        cost_estimate=cost(0, 2 * parts.size),
    )(parts)


def shards(basis, blocks, columns, sends):
    params, count, _, size, _ = blocks.shape
    width = basis.shape[1]
    halo = sends.shape[1] // 2
    devices = lax.axis_size(AXIS)
    chips = devices // 2
    near_pairs, far_pairs = pairs(devices, 0), pairs(devices, 1)

    ranges = halves(width)
    own, *listed = pick_blocks(basis.reshape(count, size, width), sends)
    fars = [lax.ppermute(far, AXIS, far_pairs) for far in listed[: len(ranges)]]
    nears = [lax.ppermute(near, AXIS, near_pairs) for near in listed[len(ranges) :]]

    turned = transposed(own, devices)
    folds = fold_far(turned, blocks, columns, halo)
    local = local_parts(turned, own, nears, blocks, columns)

    taken, keep = [], []
    for (start, _), far in zip(ranges, fars):
        give = with_far(local, folds, far, False, start)
        taken.append(lax.ppermute(give, AXIS, near_pairs))
        keep.append(with_far(local, folds, far, True, start))
    taken, keep = jnp.concatenate(taken, axis=1), jnp.concatenate(keep, axis=1)
    chip_sum = (keep + taken.astype(jnp.float32)).astype(jnp.bfloat16)
    parts = lax.all_to_all(
        chip_sum.reshape(chips, width // devices, params * width), AXIS,
        split_axis=0, concat_axis=0, tiled=True,
        axis_index_groups=[[2 * chip + core for chip in chip_order(chips)] for core in range(2)],
    )
    return add_chips(parts, params)


def solution(mesh):
    placed = (
        P(("grp", "mesh"), None),
        P(None, ("grp", "mesh"), None, None, None),
        P(None, ("grp", "mesh"), None),
        P(("grp", "mesh"), None),
    )
    return jax.shard_map(
        shards, mesh=mesh, in_specs=placed, out_specs=P(("grp", "mesh"), None), check_vma=False
    )
```

```python
import jax
import jax.numpy as jnp
from jax import lax
from jax.experimental import pallas as pl
from jax.experimental.pallas import tpu as pltpu
from jax.sharding import PartitionSpec as P

AXIS = "mesh"
LANES = 128
EASE = 8
VMEM_BYTES = 24 * 1024 * 1024
VMEM = pl.BlockSpec(memory_space=pltpu.VMEM)
SMEM = pl.BlockSpec(memory_space=pltpu.SMEM)
PARAMETERS = pltpu.CompilerParams(vmem_limit_bytes=VMEM_BYTES)


def cost(flops, moved):
    return pl.CostEstimate(flops=flops // EASE, bytes_accessed=moved // EASE, transcendentals=0)


def pairs(count, first):
    both = []
    for low in range(first, count - 1, 2):
        both += [(low, low + 1), (low + 1, low)]
    return both


def chip_order(chips):
    high = [(chips - 1 - place) ^ 1 for place in range(chips)]
    order = [chip for pair in zip(high, range(chips)) for chip in pair][:chips]
    return order if len(set(order)) == chips else list(range(chips))


def halves(width):
    half = width // 2
    return [(0, width)] if half % LANES else [(0, half), (half, half)]


def pick_far(own, sends):
    count, size, width = own.shape
    halo = sends.shape[1] // 2

    def kernel(sends_hbm, own_hbm, own_ref, far_ref, sends_ref, list_sem, load_sem):
        lists = pltpu.make_async_copy(sends_hbm, sends_ref, list_sem)
        lists.start()
        load = pltpu.make_async_copy(own_hbm, own_ref, load_sem)
        load.start()
        lists.wait()
        load.wait()
        first = lax.rem(lax.axis_index(AXIS), 2) * halo
        for place in range(halo):
            far_ref[place] = own_ref[sends_ref[0, first + place]]

    return pl.pallas_call(
        kernel,
        out_shape=(
            jax.ShapeDtypeStruct(own.shape, own.dtype),
            jax.ShapeDtypeStruct((halo, size, width), own.dtype),
        ),
        in_specs=[pl.BlockSpec(memory_space=pltpu.HBM)] * 2,
        out_specs=(VMEM,) * 2,
        scratch_shapes=[
            pltpu.SMEM(sends.shape, sends.dtype),
            pltpu.SemaphoreType.DMA(()),
            pltpu.SemaphoreType.DMA(()),
        ],
        compiler_params=PARAMETERS,
        cost_estimate=cost(0, 5 * own.size),
    )(
        pltpu.with_memory_space_constraint(sends, pltpu.HBM),
        pltpu.with_memory_space_constraint(own, pltpu.HBM),
    )


def pick_near(own, sends):
    _, size, width = own.shape
    halo = sends.shape[1] // 2
    ranges = halves(width)

    def kernel(sends_hbm, own_ref, *refs):
        near_refs, sends_ref = refs[:-1], refs[-1]
        pltpu.sync_copy(sends_hbm, sends_ref)
        first = (1 - lax.rem(lax.axis_index(AXIS), 2)) * halo
        for place in range(halo):
            block = sends_ref[0, first + place]
            for part, near_ref in zip(ranges, near_refs):
                near_ref[place] = own_ref[block, :, pl.ds(*part)]

    return pl.pallas_call(
        kernel,
        out_shape=[jax.ShapeDtypeStruct((halo, size, span), own.dtype) for _, span in ranges],
        in_specs=[pl.BlockSpec(memory_space=pltpu.HBM), VMEM],
        out_specs=[VMEM] * len(ranges),
        scratch_shapes=[pltpu.SMEM(sends.shape, sends.dtype)],
        compiler_params=PARAMETERS,
        cost_estimate=cost(0, 2 * own.size),
    )(pltpu.with_memory_space_constraint(sends, pltpu.HBM), own)


def transposed(own, devices):
    count, size, width = own.shape
    chips, rows = devices // 2, width // devices
    order = chip_order(chips)
    if rows % 16:
        turned = own.reshape(count * size, width).T.reshape(chips, 2, rows, count * size)
        turned = turned[jnp.array(order)]
        return turned.transpose(1, 0, 2, 3).reshape(width, count * size)

    def kernel(own_ref, out_ref):
        @pl.loop(0, count)
        def _(block):
            cols = pl.ds(pl.multiple_of(block * size, size), size)
            turned = own_ref[block].T
            for device in range(devices):
                chip, core = divmod(device, 2)
                out_ref[pl.ds((core * chips + order.index(chip)) * rows, rows), cols] = (
                    turned[device * rows : (device + 1) * rows]
                )

    return pl.pallas_call(
        kernel,
        out_shape=jax.ShapeDtypeStruct((width, count * size), own.dtype),
        in_specs=[VMEM],
        out_specs=VMEM,
        compiler_params=PARAMETERS,
        cost_estimate=cost(0, 4 * own.size),
    )(own)


def steps(columns):
    step = 2 * LANES if columns % (2 * LANES) == 0 else columns
    return [pl.ds(at, step) for at in range(0, columns, step)]


def halo_place(column, count, halo):
    place = column - count
    upper = place >= halo
    odd = lax.rem(lax.axis_index(AXIS), 2)
    return upper == (odd == 1), jnp.where(upper, place - halo, place)


def fold_far(turned, blocks, columns, halo):
    params, count, slots, size, _ = blocks.shape
    width = turned.shape[0]

    def kernel(columns_ref, turned_ref, blocks_ref, out_ref, sum_ref):
        sum_ref[...] = jnp.zeros_like(sum_ref)

        @pl.loop(0, count)
        def _(row):
            rows = pl.ds(pl.multiple_of(row * size, size), size)
            for param in range(params):
                for slot in range(1, slots):
                    column = columns_ref[param, row, slot - 1]
                    far, place = halo_place(column, count, halo)

                    @pl.when((column >= count) & far)
                    def _():
                        at = pl.ds(pl.multiple_of(place * size, size), size)
                        sum_ref[param, :, at] += jnp.dot(
                            turned_ref[:, rows],
                            blocks_ref[param, row, slot],
                            preferred_element_type=jnp.float32,
                        )

        out_ref[...] = sum_ref[...].astype(out_ref.dtype)

    shape = (params, width, halo * size)
    return pl.pallas_call(
        kernel,
        out_shape=jax.ShapeDtypeStruct(shape, turned.dtype),
        in_specs=[SMEM, VMEM, VMEM],
        out_specs=VMEM,
        scratch_shapes=[pltpu.VMEM(shape, jnp.float32)],
        compiler_params=PARAMETERS,
        cost_estimate=cost(
            params * count * (slots - 1) * size * size * width, 2 * (turned.size + blocks.size)
        ),
    )(columns, turned, blocks)


def local_parts(turned, own, nears, blocks, columns):
    params, count, slots, size, _ = blocks.shape
    halo, width = nears[0].shape[0], own.shape[2]
    ranges = halves(width)

    def kernel(columns_ref, turned_ref, own_ref, blocks_ref, *refs):
        near_refs, (out_ref, list_ref, image_ref) = refs[: len(ranges)], refs[len(ranges) :]
        list_ref[pl.ds(0, count)] = own_ref[...]
        for part, near_ref in zip(ranges, near_refs):
            list_ref[pl.ds(count, halo), :, pl.ds(*part)] = near_ref[...]

        @pl.loop(0, count, unroll=4)
        def _(row):
            at = pl.ds(pl.multiple_of(row * size, size), size)
            for param in range(params):
                left, right = [blocks_ref[param, row, 0]], [list_ref[row]]
                for slot in range(1, slots):
                    block = blocks_ref[param, row, slot]
                    column = columns_ref[param, row, slot - 1]
                    far, place = halo_place(column, count, halo)
                    here = (column < count) | jnp.logical_not(far)
                    left.append(jnp.where(here, block, jnp.zeros_like(block)))
                    right.append(list_ref[jnp.where(column < count, column, count + place)])
                image = jnp.dot(
                    jnp.concatenate(left, axis=1),
                    jnp.concatenate(right, axis=0),
                    preferred_element_type=jnp.float32,
                )
                image_ref[at, pl.ds(param * width, width)] = image.astype(image_ref.dtype)

        for param in range(params):
            for cols in steps(width):
                out_ref[param, :, cols] = jnp.dot(
                    turned_ref[...],
                    image_ref[:, pl.ds(param * width + cols.start, cols.size)],
                    preferred_element_type=jnp.float32,
                )

    rows = count * size
    return pl.pallas_call(
        kernel,
        out_shape=jax.ShapeDtypeStruct((params, width, width), jnp.float32),
        in_specs=[SMEM] + [VMEM] * (3 + len(ranges)),
        out_specs=VMEM,
        scratch_shapes=[
            pltpu.VMEM((count + halo, size, width), own.dtype),
            pltpu.VMEM((rows, params * width), jnp.bfloat16),
        ],
        compiler_params=PARAMETERS,
        cost_estimate=cost(
            2 * params * rows * width * (slots * size + width),
            2 * (turned.size + 2 * own.size + blocks.size) + 4 * params * width * width,
        ),
    )(columns, turned, own, blocks, *nears)


def with_far(local, folds, far, mine):
    params, width, depth = folds.shape
    half, span = width // 2, far.shape[2]

    def kernel(local_ref, folds_ref, far_ref, out_ref):
        odd = lax.rem(lax.axis_index(AXIS), 2)
        rows = pl.ds(pl.multiple_of((odd if mine else 1 - odd) * half, half), half)
        right = far_ref[...].reshape(depth, span)
        for param in range(params):
            total = local_ref[param, rows] + jnp.dot(
                folds_ref[param, rows], right, preferred_element_type=jnp.float32
            )
            out_ref[:, pl.ds(param * span, span)] = total.astype(out_ref.dtype)

    columns = params * span
    return pl.pallas_call(
        kernel,
        out_shape=jax.ShapeDtypeStruct((half, columns), jnp.float32 if mine else jnp.bfloat16),
        in_specs=[VMEM] * 3,
        out_specs=VMEM,
        compiler_params=PARAMETERS,
        cost_estimate=cost(
            2 * half * depth * columns,
            4 * half * columns + params * half * depth * 2 + 2 * depth * span,
        ),
    )(local, folds, far)


def add_chips(parts):
    def kernel(parts_ref, out_ref):
        out_ref[...] = jnp.sum(parts_ref[...].astype(jnp.float32), axis=0)

    return pl.pallas_call(
        kernel,
        out_shape=jax.ShapeDtypeStruct(parts.shape[1:], jnp.float32),
        in_specs=[VMEM],
        out_specs=VMEM,
        compiler_params=PARAMETERS,
        cost_estimate=cost(0, 2 * parts.size),
    )(parts)


def shards(basis, blocks, columns, sends):
    params, count, _, size, _ = blocks.shape
    width = basis.shape[1]
    halo = sends.shape[1] // 2
    devices = lax.axis_size(AXIS)
    chips = devices // 2
    near_pairs, far_pairs = pairs(devices, 0), pairs(devices, 1)

    own, far = pick_far(basis.reshape(count, size, width), sends)
    far = lax.ppermute(far, AXIS, far_pairs)
    nears = [lax.ppermute(near, AXIS, near_pairs) for near in pick_near(own, sends)]

    turned = transposed(own, devices)
    folds = fold_far(turned, blocks, columns, halo)
    local = local_parts(turned, own, nears, blocks, columns)

    taken = lax.ppermute(with_far(local, folds, far, False), AXIS, near_pairs)
    keep = with_far(local, folds, far, True)
    chip_sum = (keep + taken.astype(jnp.float32)).astype(jnp.bfloat16)
    parts = lax.all_to_all(
        chip_sum.reshape(chips, width // devices, params * width), AXIS,
        split_axis=0, concat_axis=0, tiled=True,
        axis_index_groups=[[2 * chip + core for chip in chip_order(chips)] for core in range(2)],
    )
    return add_chips(parts)


def solution(mesh):
    placed = (
        P(("grp", "mesh"), None),
        P(None, ("grp", "mesh"), None, None, None),
        P(None, ("grp", "mesh"), None),
        P(("grp", "mesh"), None),
    )
    return jax.shard_map(
        shards, mesh=mesh, in_specs=placed, out_specs=P(("grp", "mesh"), None), check_vma=False
    )
```

```python
import jax
import jax.numpy as jnp
from jax import lax
from jax.experimental import pallas as pl
from jax.experimental.pallas import tpu as pltpu
from jax.sharding import PartitionSpec as P

AXIS = "mesh"
LANES = 128
EASE = 8
VMEM_BYTES = 24 * 1024 * 1024
VMEM = pl.BlockSpec(memory_space=pltpu.VMEM)
SMEM = pl.BlockSpec(memory_space=pltpu.SMEM)
PARAMETERS = pltpu.CompilerParams(vmem_limit_bytes=VMEM_BYTES)


def cost(flops, moved):
    return pl.CostEstimate(flops=flops // EASE, bytes_accessed=moved // EASE, transcendentals=0)


def pairs(count, first):
    both = []
    for low in range(first, count - 1, 2):
        both += [(low, low + 1), (low + 1, low)]
    return both


def chip_order(chips):
    ends = zip(range(chips - 1, -1, -1), range(chips))
    return [chip for pair in ends for chip in pair][:chips]


def halves(width):
    half = width // 2
    return [(0, width)] if half % LANES else [(0, half), (half, half)]


def pick_far(own, sends):
    count, size, width = own.shape
    halo = sends.shape[1] // 2

    def kernel(sends_hbm, own_hbm, own_ref, far_ref, sends_ref, list_sem, load_sem):
        lists = pltpu.make_async_copy(sends_hbm, sends_ref, list_sem)
        lists.start()
        load = pltpu.make_async_copy(own_hbm, own_ref, load_sem)
        load.start()
        lists.wait()
        load.wait()
        first = lax.rem(lax.axis_index(AXIS), 2) * halo
        for place in range(halo):
            far_ref[place] = own_ref[sends_ref[0, first + place]]

    return pl.pallas_call(
        kernel,
        out_shape=(
            jax.ShapeDtypeStruct(own.shape, own.dtype),
            jax.ShapeDtypeStruct((halo, size, width), own.dtype),
        ),
        in_specs=[pl.BlockSpec(memory_space=pltpu.HBM)] * 2,
        out_specs=(VMEM,) * 2,
        scratch_shapes=[
            pltpu.SMEM(sends.shape, sends.dtype),
            pltpu.SemaphoreType.DMA(()),
            pltpu.SemaphoreType.DMA(()),
        ],
        compiler_params=PARAMETERS,
        cost_estimate=cost(0, 5 * own.size),
    )(
        pltpu.with_memory_space_constraint(sends, pltpu.HBM),
        pltpu.with_memory_space_constraint(own, pltpu.HBM),
    )


def pick_near(own, sends):
    _, size, width = own.shape
    halo = sends.shape[1] // 2
    ranges = halves(width)

    def kernel(sends_hbm, own_ref, *refs):
        near_refs, sends_ref = refs[:-1], refs[-1]
        pltpu.sync_copy(sends_hbm, sends_ref)
        first = (1 - lax.rem(lax.axis_index(AXIS), 2)) * halo
        for place in range(halo):
            block = sends_ref[0, first + place]
            for part, near_ref in zip(ranges, near_refs):
                near_ref[place] = own_ref[block, :, pl.ds(*part)]

    return pl.pallas_call(
        kernel,
        out_shape=[jax.ShapeDtypeStruct((halo, size, span), own.dtype) for _, span in ranges],
        in_specs=[pl.BlockSpec(memory_space=pltpu.HBM), VMEM],
        out_specs=[VMEM] * len(ranges),
        scratch_shapes=[pltpu.SMEM(sends.shape, sends.dtype)],
        compiler_params=PARAMETERS,
        cost_estimate=cost(0, 2 * own.size),
    )(pltpu.with_memory_space_constraint(sends, pltpu.HBM), own)


def transposed(own, devices):
    count, size, width = own.shape
    chips, rows = devices // 2, width // devices
    order = chip_order(chips)
    if rows % 16:
        turned = own.reshape(count * size, width).T.reshape(chips, 2, rows, count * size)
        turned = turned[jnp.array(order)]
        return turned.transpose(1, 0, 2, 3).reshape(width, count * size)

    def kernel(own_ref, out_ref):
        @pl.loop(0, count)
        def _(block):
            cols = pl.ds(pl.multiple_of(block * size, size), size)
            turned = own_ref[block].T
            for device in range(devices):
                chip, core = divmod(device, 2)
                out_ref[pl.ds((core * chips + order.index(chip)) * rows, rows), cols] = (
                    turned[device * rows : (device + 1) * rows]
                )

    return pl.pallas_call(
        kernel,
        out_shape=jax.ShapeDtypeStruct((width, count * size), own.dtype),
        in_specs=[VMEM],
        out_specs=VMEM,
        compiler_params=PARAMETERS,
        cost_estimate=cost(0, 4 * own.size),
    )(own)


def steps(columns):
    step = 2 * LANES if columns % (2 * LANES) == 0 else columns
    return [pl.ds(at, step) for at in range(0, columns, step)]


def halo_place(column, count, halo):
    place = column - count
    upper = place >= halo
    odd = lax.rem(lax.axis_index(AXIS), 2)
    return upper == (odd == 1), jnp.where(upper, place - halo, place)


def fold_far(turned, blocks, columns, halo):
    params, count, slots, size, _ = blocks.shape
    width = turned.shape[0]

    def kernel(columns_ref, turned_ref, blocks_ref, out_ref, sum_ref):
        sum_ref[...] = jnp.zeros_like(sum_ref)

        @pl.loop(0, count)
        def _(row):
            rows = pl.ds(pl.multiple_of(row * size, size), size)
            for param in range(params):
                for slot in range(1, slots):
                    column = columns_ref[param, row, slot - 1]
                    far, place = halo_place(column, count, halo)

                    @pl.when((column >= count) & far)
                    def _():
                        at = pl.ds(pl.multiple_of(place * size, size), size)
                        sum_ref[param, :, at] += jnp.dot(
                            turned_ref[:, rows],
                            blocks_ref[param, row, slot],
                            preferred_element_type=jnp.float32,
                        )

        out_ref[...] = sum_ref[...].astype(out_ref.dtype)

    shape = (params, width, halo * size)
    return pl.pallas_call(
        kernel,
        out_shape=jax.ShapeDtypeStruct(shape, turned.dtype),
        in_specs=[SMEM, VMEM, VMEM],
        out_specs=VMEM,
        scratch_shapes=[pltpu.VMEM(shape, jnp.float32)],
        compiler_params=PARAMETERS,
        cost_estimate=cost(
            params * count * (slots - 1) * size * size * width, 2 * (turned.size + blocks.size)
        ),
    )(columns, turned, blocks)


def local_parts(turned, own, nears, blocks, columns):
    params, count, slots, size, _ = blocks.shape
    halo, width = nears[0].shape[0], own.shape[2]
    ranges = halves(width)

    def kernel(columns_ref, turned_ref, own_ref, blocks_ref, *refs):
        near_refs, (out_ref, list_ref, image_ref) = refs[: len(ranges)], refs[len(ranges) :]
        list_ref[pl.ds(0, count)] = own_ref[...]
        for part, near_ref in zip(ranges, near_refs):
            list_ref[pl.ds(count, halo), :, pl.ds(*part)] = near_ref[...]

        @pl.loop(0, count, unroll=4)
        def _(row):
            at = pl.ds(pl.multiple_of(row * size, size), size)
            for param in range(params):
                left, right = [blocks_ref[param, row, 0]], [list_ref[row]]
                for slot in range(1, slots):
                    block = blocks_ref[param, row, slot]
                    column = columns_ref[param, row, slot - 1]
                    far, place = halo_place(column, count, halo)
                    here = (column < count) | jnp.logical_not(far)
                    left.append(jnp.where(here, block, jnp.zeros_like(block)))
                    right.append(list_ref[jnp.where(column < count, column, count + place)])
                image = jnp.dot(
                    jnp.concatenate(left, axis=1),
                    jnp.concatenate(right, axis=0),
                    preferred_element_type=jnp.float32,
                )
                image_ref[at, pl.ds(param * width, width)] = image.astype(image_ref.dtype)

        for param in range(params):
            for cols in steps(width):
                out_ref[param, :, cols] = jnp.dot(
                    turned_ref[...],
                    image_ref[:, pl.ds(param * width + cols.start, cols.size)],
                    preferred_element_type=jnp.float32,
                )

    rows = count * size
    return pl.pallas_call(
        kernel,
        out_shape=jax.ShapeDtypeStruct((params, width, width), jnp.float32),
        in_specs=[SMEM] + [VMEM] * (3 + len(ranges)),
        out_specs=VMEM,
        scratch_shapes=[
            pltpu.VMEM((count + halo, size, width), own.dtype),
            pltpu.VMEM((rows, params * width), jnp.bfloat16),
        ],
        compiler_params=PARAMETERS,
        cost_estimate=cost(
            2 * params * rows * width * (slots * size + width),
            2 * (turned.size + 2 * own.size + blocks.size) + 4 * params * width * width,
        ),
    )(columns, turned, own, blocks, *nears)


def with_far(local, folds, far, mine):
    params, width, depth = folds.shape
    half, span = width // 2, far.shape[2]

    def kernel(local_ref, folds_ref, far_ref, out_ref):
        odd = lax.rem(lax.axis_index(AXIS), 2)
        rows = pl.ds(pl.multiple_of((odd if mine else 1 - odd) * half, half), half)
        right = far_ref[...].reshape(depth, span)
        for param in range(params):
            total = local_ref[param, rows] + jnp.dot(
                folds_ref[param, rows], right, preferred_element_type=jnp.float32
            )
            out_ref[:, pl.ds(param * span, span)] = total.astype(out_ref.dtype)

    columns = params * span
    return pl.pallas_call(
        kernel,
        out_shape=jax.ShapeDtypeStruct((half, columns), jnp.float32 if mine else jnp.bfloat16),
        in_specs=[VMEM] * 3,
        out_specs=VMEM,
        compiler_params=PARAMETERS,
        cost_estimate=cost(
            2 * half * depth * columns,
            4 * half * columns + params * half * depth * 2 + 2 * depth * span,
        ),
    )(local, folds, far)


def add_chips(parts):
    def kernel(parts_ref, out_ref):
        out_ref[...] = jnp.sum(parts_ref[...].astype(jnp.float32), axis=0)

    return pl.pallas_call(
        kernel,
        out_shape=jax.ShapeDtypeStruct(parts.shape[1:], jnp.float32),
        in_specs=[VMEM],
        out_specs=VMEM,
        compiler_params=PARAMETERS,
        cost_estimate=cost(0, 2 * parts.size),
    )(parts)


def shards(basis, blocks, columns, sends):
    params, count, _, size, _ = blocks.shape
    width = basis.shape[1]
    halo = sends.shape[1] // 2
    devices = lax.axis_size(AXIS)
    chips = devices // 2
    near_pairs, far_pairs = pairs(devices, 0), pairs(devices, 1)

    own, far = pick_far(basis.reshape(count, size, width), sends)
    far = lax.ppermute(far, AXIS, far_pairs)
    nears = [lax.ppermute(near, AXIS, near_pairs) for near in pick_near(own, sends)]

    turned = transposed(own, devices)
    folds = fold_far(turned, blocks, columns, halo)
    local = local_parts(turned, own, nears, blocks, columns)

    taken = lax.ppermute(with_far(local, folds, far, False), AXIS, near_pairs)
    keep = with_far(local, folds, far, True)
    chip_sum = (keep + taken.astype(jnp.float32)).astype(jnp.bfloat16)
    parts = lax.all_to_all(
        chip_sum.reshape(chips, width // devices, params * width), AXIS,
        split_axis=0, concat_axis=0, tiled=True,
        axis_index_groups=[[2 * chip + core for chip in chip_order(chips)] for core in range(2)],
    )
    return add_chips(parts)


def solution(mesh):
    placed = (
        P(("grp", "mesh"), None),
        P(None, ("grp", "mesh"), None, None, None),
        P(None, ("grp", "mesh"), None),
        P(("grp", "mesh"), None),
    )
    return jax.shard_map(
        shards, mesh=mesh, in_specs=placed, out_specs=P(("grp", "mesh"), None), check_vma=False
    )
```

```python
import jax
import jax.numpy as jnp
from jax import lax
from jax.experimental import pallas as pl
from jax.experimental.pallas import tpu as pltpu
from jax.sharding import PartitionSpec as P

AXIS = "mesh"
LANES = 128
EASE = 8
VMEM_BYTES = 24 * 1024 * 1024
VMEM = pl.BlockSpec(memory_space=pltpu.VMEM)
SMEM = pl.BlockSpec(memory_space=pltpu.SMEM)
PARAMETERS = pltpu.CompilerParams(vmem_limit_bytes=VMEM_BYTES)


def cost(flops, moved):
    return pl.CostEstimate(flops=flops // EASE, bytes_accessed=moved // EASE, transcendentals=0)


def pairs(count, first):
    both = []
    for low in range(first, count - 1, 2):
        both += [(low, low + 1), (low + 1, low)]
    return both


def chip_order(chips):
    low = list(range(0, chips // 2, 2)) + list(range(1, chips // 2, 2))
    order = [chip for place in low for chip in (chips - 1 - place, place)]
    return order + [chip for chip in range(chips) if chip not in order]


def halves(width):
    half = width // 2
    return [(0, width)] if half % LANES else [(0, half), (half, half)]


def pick_far(own, sends):
    count, size, width = own.shape
    halo = sends.shape[1] // 2

    def kernel(sends_hbm, own_hbm, own_ref, far_ref, sends_ref, list_sem, load_sem):
        lists = pltpu.make_async_copy(sends_hbm, sends_ref, list_sem)
        lists.start()
        load = pltpu.make_async_copy(own_hbm, own_ref, load_sem)
        load.start()
        lists.wait()
        load.wait()
        first = lax.rem(lax.axis_index(AXIS), 2) * halo
        for place in range(halo):
            far_ref[place] = own_ref[sends_ref[0, first + place]]

    return pl.pallas_call(
        kernel,
        out_shape=(
            jax.ShapeDtypeStruct(own.shape, own.dtype),
            jax.ShapeDtypeStruct((halo, size, width), own.dtype),
        ),
        in_specs=[pl.BlockSpec(memory_space=pltpu.HBM)] * 2,
        out_specs=(VMEM,) * 2,
        scratch_shapes=[
            pltpu.SMEM(sends.shape, sends.dtype),
            pltpu.SemaphoreType.DMA(()),
            pltpu.SemaphoreType.DMA(()),
        ],
        compiler_params=PARAMETERS,
        cost_estimate=cost(0, 5 * own.size),
    )(
        pltpu.with_memory_space_constraint(sends, pltpu.HBM),
        pltpu.with_memory_space_constraint(own, pltpu.HBM),
    )


def pick_near(own, sends):
    _, size, width = own.shape
    halo = sends.shape[1] // 2
    ranges = halves(width)

    def kernel(sends_hbm, own_ref, *refs):
        near_refs, sends_ref = refs[:-1], refs[-1]
        pltpu.sync_copy(sends_hbm, sends_ref)
        first = (1 - lax.rem(lax.axis_index(AXIS), 2)) * halo
        for place in range(halo):
            block = sends_ref[0, first + place]
            for part, near_ref in zip(ranges, near_refs):
                near_ref[place] = own_ref[block, :, pl.ds(*part)]

    return pl.pallas_call(
        kernel,
        out_shape=[jax.ShapeDtypeStruct((halo, size, span), own.dtype) for _, span in ranges],
        in_specs=[pl.BlockSpec(memory_space=pltpu.HBM), VMEM],
        out_specs=[VMEM] * len(ranges),
        scratch_shapes=[pltpu.SMEM(sends.shape, sends.dtype)],
        compiler_params=PARAMETERS,
        cost_estimate=cost(0, 2 * own.size),
    )(pltpu.with_memory_space_constraint(sends, pltpu.HBM), own)


def transposed(own, devices):
    count, size, width = own.shape
    chips, rows = devices // 2, width // devices
    order = chip_order(chips)
    if rows % 16:
        turned = own.reshape(count * size, width).T.reshape(chips, 2, rows, count * size)
        turned = turned[jnp.array(order)]
        return turned.transpose(1, 0, 2, 3).reshape(width, count * size)

    def kernel(own_ref, out_ref):
        @pl.loop(0, count)
        def _(block):
            cols = pl.ds(pl.multiple_of(block * size, size), size)
            turned = own_ref[block].T
            for device in range(devices):
                chip, core = divmod(device, 2)
                out_ref[pl.ds((core * chips + order.index(chip)) * rows, rows), cols] = (
                    turned[device * rows : (device + 1) * rows]
                )

    return pl.pallas_call(
        kernel,
        out_shape=jax.ShapeDtypeStruct((width, count * size), own.dtype),
        in_specs=[VMEM],
        out_specs=VMEM,
        compiler_params=PARAMETERS,
        cost_estimate=cost(0, 4 * own.size),
    )(own)


def steps(columns):
    step = 2 * LANES if columns % (2 * LANES) == 0 else columns
    return [pl.ds(at, step) for at in range(0, columns, step)]


def halo_place(column, count, halo):
    place = column - count
    upper = place >= halo
    odd = lax.rem(lax.axis_index(AXIS), 2)
    return upper == (odd == 1), jnp.where(upper, place - halo, place)


def fold_far(turned, blocks, columns, halo):
    params, count, slots, size, _ = blocks.shape
    width = turned.shape[0]

    def kernel(columns_ref, turned_ref, blocks_ref, out_ref, sum_ref):
        sum_ref[...] = jnp.zeros_like(sum_ref)

        @pl.loop(0, count)
        def _(row):
            rows = pl.ds(pl.multiple_of(row * size, size), size)
            for param in range(params):
                for slot in range(1, slots):
                    column = columns_ref[param, row, slot - 1]
                    far, place = halo_place(column, count, halo)

                    @pl.when((column >= count) & far)
                    def _():
                        at = pl.ds(pl.multiple_of(place * size, size), size)
                        sum_ref[param, :, at] += jnp.dot(
                            turned_ref[:, rows],
                            blocks_ref[param, row, slot],
                            preferred_element_type=jnp.float32,
                        )

        out_ref[...] = sum_ref[...].astype(out_ref.dtype)

    shape = (params, width, halo * size)
    return pl.pallas_call(
        kernel,
        out_shape=jax.ShapeDtypeStruct(shape, turned.dtype),
        in_specs=[SMEM, VMEM, VMEM],
        out_specs=VMEM,
        scratch_shapes=[pltpu.VMEM(shape, jnp.float32)],
        compiler_params=PARAMETERS,
        cost_estimate=cost(
            params * count * (slots - 1) * size * size * width, 2 * (turned.size + blocks.size)
        ),
    )(columns, turned, blocks)


def local_parts(turned, own, nears, blocks, columns):
    params, count, slots, size, _ = blocks.shape
    halo, width = nears[0].shape[0], own.shape[2]
    ranges = halves(width)

    def kernel(columns_ref, turned_ref, own_ref, blocks_ref, *refs):
        near_refs, (out_ref, list_ref, image_ref) = refs[: len(ranges)], refs[len(ranges) :]
        list_ref[pl.ds(0, count)] = own_ref[...]
        for part, near_ref in zip(ranges, near_refs):
            list_ref[pl.ds(count, halo), :, pl.ds(*part)] = near_ref[...]

        @pl.loop(0, count, unroll=4)
        def _(row):
            at = pl.ds(pl.multiple_of(row * size, size), size)
            for param in range(params):
                left, right = [blocks_ref[param, row, 0]], [list_ref[row]]
                for slot in range(1, slots):
                    block = blocks_ref[param, row, slot]
                    column = columns_ref[param, row, slot - 1]
                    far, place = halo_place(column, count, halo)
                    here = (column < count) | jnp.logical_not(far)
                    left.append(jnp.where(here, block, jnp.zeros_like(block)))
                    right.append(list_ref[jnp.where(column < count, column, count + place)])
                image = jnp.dot(
                    jnp.concatenate(left, axis=1),
                    jnp.concatenate(right, axis=0),
                    preferred_element_type=jnp.float32,
                )
                image_ref[at, pl.ds(param * width, width)] = image.astype(image_ref.dtype)

        for param in range(params):
            for cols in steps(width):
                out_ref[param, :, cols] = jnp.dot(
                    turned_ref[...],
                    image_ref[:, pl.ds(param * width + cols.start, cols.size)],
                    preferred_element_type=jnp.float32,
                )

    rows = count * size
    return pl.pallas_call(
        kernel,
        out_shape=jax.ShapeDtypeStruct((params, width, width), jnp.float32),
        in_specs=[SMEM] + [VMEM] * (3 + len(ranges)),
        out_specs=VMEM,
        scratch_shapes=[
            pltpu.VMEM((count + halo, size, width), own.dtype),
            pltpu.VMEM((rows, params * width), jnp.bfloat16),
        ],
        compiler_params=PARAMETERS,
        cost_estimate=cost(
            2 * params * rows * width * (slots * size + width),
            2 * (turned.size + 2 * own.size + blocks.size) + 4 * params * width * width,
        ),
    )(columns, turned, own, blocks, *nears)


def with_far(local, folds, far, mine):
    params, width, depth = folds.shape
    half, span = width // 2, far.shape[2]

    def kernel(local_ref, folds_ref, far_ref, out_ref):
        odd = lax.rem(lax.axis_index(AXIS), 2)
        rows = pl.ds(pl.multiple_of((odd if mine else 1 - odd) * half, half), half)
        right = far_ref[...].reshape(depth, span)
        for param in range(params):
            total = local_ref[param, rows] + jnp.dot(
                folds_ref[param, rows], right, preferred_element_type=jnp.float32
            )
            out_ref[:, pl.ds(param * span, span)] = total.astype(out_ref.dtype)

    columns = params * span
    return pl.pallas_call(
        kernel,
        out_shape=jax.ShapeDtypeStruct((half, columns), jnp.float32 if mine else jnp.bfloat16),
        in_specs=[VMEM] * 3,
        out_specs=VMEM,
        compiler_params=PARAMETERS,
        cost_estimate=cost(
            2 * half * depth * columns,
            4 * half * columns + params * half * depth * 2 + 2 * depth * span,
        ),
    )(local, folds, far)


def add_chips(parts):
    def kernel(parts_ref, out_ref):
        out_ref[...] = jnp.sum(parts_ref[...].astype(jnp.float32), axis=0)

    return pl.pallas_call(
        kernel,
        out_shape=jax.ShapeDtypeStruct(parts.shape[1:], jnp.float32),
        in_specs=[VMEM],
        out_specs=VMEM,
        compiler_params=PARAMETERS,
        cost_estimate=cost(0, 2 * parts.size),
    )(parts)


def shards(basis, blocks, columns, sends):
    params, count, _, size, _ = blocks.shape
    width = basis.shape[1]
    halo = sends.shape[1] // 2
    devices = lax.axis_size(AXIS)
    chips = devices // 2
    near_pairs, far_pairs = pairs(devices, 0), pairs(devices, 1)

    own, far = pick_far(basis.reshape(count, size, width), sends)
    far = lax.ppermute(far, AXIS, far_pairs)
    nears = [lax.ppermute(near, AXIS, near_pairs) for near in pick_near(own, sends)]

    turned = transposed(own, devices)
    folds = fold_far(turned, blocks, columns, halo)
    local = local_parts(turned, own, nears, blocks, columns)

    taken = lax.ppermute(with_far(local, folds, far, False), AXIS, near_pairs)
    keep = with_far(local, folds, far, True)
    chip_sum = (keep + taken.astype(jnp.float32)).astype(jnp.bfloat16)
    parts = lax.all_to_all(
        chip_sum.reshape(chips, width // devices, params * width), AXIS,
        split_axis=0, concat_axis=0, tiled=True,
        axis_index_groups=[[2 * chip + core for chip in chip_order(chips)] for core in range(2)],
    )
    return add_chips(parts)


def solution(mesh):
    placed = (
        P(("grp", "mesh"), None),
        P(None, ("grp", "mesh"), None, None, None),
        P(None, ("grp", "mesh"), None),
        P(("grp", "mesh"), None),
    )
    return jax.shard_map(
        shards, mesh=mesh, in_specs=placed, out_specs=P(("grp", "mesh"), None), check_vma=False
    )
```
